256 devices in a mesh: ax: 128 (over z, x_lo, y, core), xs: 2 (over x_hi).
Axes of the slice: x: 4 (x_hi: 2, x_lo: 2; x = x_hi * 2 + x_lo), y: 4, z: 8, core: 2. Of those that a mesh axis runs over, the one named last changes fastest.
Arguments:
- displacement: float32 [3, 512, 16, 1536], P(None, 'ax', 'xs'), may hold values from -6 to 6
- previous: float32 [3, 512, 16, 1536], P(None, 'ax', 'xs'), may hold values from -6 to 6
- stiffness: float32 [512, 16, 1536], P('ax', 'xs'), may hold values from 0.5 to 2
- tissue_mask: int32 [512], P('ax'), may hold values 0 or 1
- compartment: int32 [16, 1536], P('xs'), may hold values from 0 to 3
- drive: float32 [3, 4], replicated, may hold values from -1 to 1
Outputs:
- fine_field: float32 [3, 512, 16, 1536], P(None, 'ax', 'xs')
- coarse_field: float32 [3, 256, 8, 768], P(None, 'ax', 'xs')
The draws below stay inside these ranges and needn't reach their ends.
All inputs are finite; a program needn't handle non-finite values. No bound on the sum of `tissue_mask` on one device may be relied on, other than what follows from the above.
Results may differ from the reference program's by a relative error of at most 0.00011.
Values sent between devices are 32-bit elements; how exact they have to be, the bound alone decides.
No kernel may reach another device: no remote copies, remote signals or barrier semaphores. Data moves between devices by JAX's collectives and lax.ppermute only.
A program may use at most 192 MiB of HBM per device.

```python
import math
import jax
import jax.numpy as jnp
from jax import lax

NX = 1536
STEPS = 4
GROUPS = 4
NZ = 512
NY = 16


def touch_ends(drawn, own_key, smallest, high):
    extent = drawn.shape
    place = [jax.random.randint(jax.random.fold_in(own_key, axis), (), 0, extent[axis]) for axis in range(len(extent))]
    drawn = drawn.at[tuple(place)].set(smallest)
    longest = extent.index(max(extent))
    place[longest] = (place[longest] + 1) % extent[longest]
    return drawn.at[tuple(place)].set(high)


def block_scale(rng, dims, shards, smallest, high):
    def one(position, parts):
        heights = jax.random.uniform(jax.random.fold_in(jax.random.fold_in(rng, 6), position), (parts,), jnp.float32, smallest / len(shards), high / len(shards))
        return jnp.repeat(jnp.exp(heights), dims[position] // parts).reshape((-1,) + (1,) * (len(dims) - position - 1))

    factor_of = one(*shards[0])
    for cut in shards[1:]:
        factor_of = factor_of * one(*cut)
    return factor_of


def noise(stream_key, extent, scale, limit, shards=(), held_as=jnp.bfloat16):
    drawn = jax.random.normal(stream_key, extent, jnp.float32) * scale
    if len(shards) > 0:
        drawn = block_scale(stream_key, extent, shards, -0.22, 0.18) * drawn
    return jnp.clip(drawn, min=-limit, max=limit).astype(held_as)


def setup_inputs(seed: int = 0) -> dict:
    seeds = jax.random.split(jax.random.key(seed), 7)
    displacement = noise(seeds[0], (3, NZ, NY, NX), 1.0, 6.0, ((1, 128), (2, 2)), jnp.float32)
    previous = noise(seeds[1], (3, NZ, NY, NX), 1.0, 6.0, ((1, 128), (2, 2)), jnp.float32)
    stiffness = jnp.clip(jnp.exp(math.log(2.0) - 1.3862944 * jax.random.uniform(seeds[2], (NZ, NY, NX), jnp.float32) ** block_scale(seeds[2], (NZ, NY, NX), ((0, 128), (1, 2)), -0.2, 0.2)), 0.5, 2.0)
    tissue_mask = touch_ends((jax.random.randint(seeds[3], (NZ,), 0, 4) < 3).astype(jnp.int32), jax.random.fold_in(seeds[3], 1), 0, 1)
    compartment = touch_ends(jax.random.randint(seeds[4], (NY, NX), 0, GROUPS), jax.random.fold_in(seeds[4], 1), 0, GROUPS - 1).astype(jnp.int32)
    drive = jnp.clip(jax.random.uniform(seeds[5], (3, GROUPS), jnp.float32, -1.0, 1.0), -1.0, 1.0)
    return dict(displacement=displacement, previous=previous, stiffness=stiffness, tissue_mask=tissue_mask, compartment=compartment, drive=drive)


TIME_SQUARE = 0.12


def neighbour_windows():
    inner = slice(1, -1)
    return [(slice(2, None), inner, inner), (slice(0, -2), inner, inner),
            (inner, slice(2, None), inner), (inner, slice(0, -2), inner),
            (inner, inner, slice(2, None)), (inner, inner, slice(0, -2))]


def operate(padded, kpadded):
    inner = slice(1, -1)
    centre = padded[:, inner, inner, inner]
    stiff_mid = kpadded[inner, inner, inner]
    total = jnp.zeros_like(centre)
    for window in neighbour_windows():
        total = total + 0.5 * (stiff_mid + kpadded[window]) * (padded[(slice(None),) + window] - centre)
    return total


def make_force(tissue_mask, compartment, drive):
    groups = (compartment[None, :, :] == jnp.arange(drive.shape[1], dtype=jnp.int32)[:, None, None]).astype(jnp.float32)
    per_cell = jnp.einsum("cg,gyx->cyx", drive, groups, precision=lax.Precision.HIGHEST)
    return per_cell[:, None, :, :] * tissue_mask.astype(jnp.float32)[None, :, None, None]


def restrict(field):
    shape = field.shape
    lead = shape[:-3]
    blocks = field.reshape(lead + (shape[-3] // 2, 2, shape[-2] // 2, 2, shape[-1] // 2, 2))
    return jnp.mean(blocks, axis=(-5, -3, -1))


def evolve(current, earlier, stiff, force, factor):
    kpadded = jnp.pad(stiff, 1)
    for repeat in range(STEPS):
        padded = jnp.pad(current, ((0, 0), (1, 1), (1, 1), (1, 1)))
        fresh = 2.0 * current - earlier + TIME_SQUARE * (factor * operate(padded, kpadded) + force)
        earlier = current
        current = fresh
    return current


def reference(displacement, previous, stiffness, tissue_mask, compartment, drive):
    force = make_force(tissue_mask, compartment, drive)
    fine_field = evolve(displacement, previous, stiffness, force, 1.0)
    coarse_field = evolve(restrict(displacement), restrict(previous), restrict(stiffness), restrict(force), 0.25)
    return fine_field, coarse_field
```

```python
import functools

import jax
import jax.numpy as jnp
from jax import lax
from jax.experimental import pallas as pl
from jax.experimental.pallas import tpu as pltpu
from jax.sharding import PartitionSpec as P

TIME_SQUARE = 0.12
FINE_FACE = 0.5 * TIME_SQUARE
COARSE_FACE = 0.25 * 0.5 * TIME_SQUARE
PLANES = 4
ROWS = 8
FIELDS = 3
F32 = jnp.float32


def roll(x, shift, axis):
    return pltpu.roll(x, shift % x.shape[axis], axis)


def place():
    i = lax.axis_index("ax")
    s = lax.axis_index("xs")
    return (lax.rem(i, 2) == 1), (s == 0), (i > 0), (i < lax.axis_size("ax") - 1)


def iota(shape, dim):
    return lax.broadcasted_iota(jnp.int32, shape, dim)


def stiff_coefs(k, face, low_y, high_y, outer_row):
    width = k.shape[1]
    lane = iota(k.shape, 1)
    last = lane == width - 1
    start = lane == 0
    kp = jnp.where(last, 0.0, roll(k, -1, 1))
    km = jnp.where(start, 0.0, roll(k, 1, 1))
    full_p = face * (k + kp)
    full_m = face * (k + km)
    cyp = jnp.where(high_y, face * (k + roll(k, -1, 0)), 0.0)
    cym = jnp.where(low_y, face * (k + roll(k, 1, 0)), 0.0)
    edge = jnp.where(outer_row, face * k, 0.0)
    centre = 2.0 - (full_p + full_m + cyp + cym + edge)
    return jnp.where(last, 0.0, full_p), jnp.where(start, 0.0, full_m), cyp, cym, centre


def fine_coefs(k_ref, first, coef):
    shape = k_ref.shape[1:]
    row = iota(shape, 0)
    for z in range(PLANES - 1):
        coef[5, z] = FINE_FACE * (k_ref[z] + k_ref[z + 1])
    for z in range(PLANES):
        cxp, cxm, cyp, cym, centre = stiff_coefs(
            k_ref[z], FINE_FACE, row > 0, row < ROWS - 1, row == jnp.where(first, 0, ROWS - 1)
        )
        if z > 0:
            centre = centre - coef[5, z - 1]
        if z < PLANES - 1:
            centre = centre - coef[5, z]
        coef[0, z] = cxp
        coef[1, z] = cxm
        coef[2, z] = cyp
        coef[3, z] = cym
        coef[4, z] = centre


def fine_free(u_ref, before, c, z, coef, drive_term):
    u = u_ref[c, z]
    acc = coef[4, z] * u - before
    acc = acc + coef[0, z] * roll(u, -1, 1) + coef[1, z] * roll(u, 1, 1)
    acc = acc + coef[2, z] * roll(u, -1, 0) + coef[3, z] * roll(u, 1, 0)
    if z > 0:
        acc = acc + coef[5, z - 1] * u_ref[c, z - 1]
    if z < PLANES - 1:
        acc = acc + coef[5, z] * u_ref[c, z + 1]
    return acc + drive_term


def coarse_coefs(k, first):
    row = iota(k.shape, 0)
    inner = lax.rem(row, 4)
    cxp, cxm, cyp, cym, centre = stiff_coefs(
        k, COARSE_FACE, inner > 0, inner < 3, inner == jnp.where(first, 0, 3)
    )
    cz = COARSE_FACE * (k + roll(k, 4, 0))
    return cxp, cxm, cyp, cym, centre - cz, cz


def coarse_free(u, before, coefs, force):
    cxp, cxm, cyp, cym, centre, cz = coefs
    return (
        centre * u
        - before
        + cxp * roll(u, -1, 1)
        + cxm * roll(u, 1, 1)
        + cyp * roll(u, -1, 0)
        + cym * roll(u, 1, 0)
        + cz * roll(u, 4, 0)
        + force
    )


def group_drive(compartment, drive_ref, c):
    value = jnp.full(compartment.shape, drive_ref[c, 0], F32)
    for g in range(1, drive_ref.shape[1]):
        value = jnp.where(compartment == g, drive_ref[c, g], value)
    return value


def fine_row(r, width):
    if r < 24:
        return [(r % 8, (r // 8) * width, width)]
    half = width // 2
    return [(2 * (r - 24) + h, 3 * width, half) for h in range(2)]


def coarse_row(q, width, base):
    half = width // 2
    return [(q % 8, base + (q // 8) * half, half)]


def corner_fine(f, width):
    half = width // 2
    return [(2 * f + h, 0, half) for h in range(2)]


def corner_coarse(f, width):
    quarter = width // 4
    return [(2 * f + h, width // 2, quarter) for h in range(2)]


def put(buf, pieces, line):
    at = 0
    for row, lane, lanes in pieces:
        buf[row : row + 1, lane : lane + lanes] = line[:, at : at + lanes]
        at += lanes


def take(buf, pieces):
    parts = [buf[row : row + 1, lane : lane + lanes] for row, lane, lanes in pieces]
    return parts[0] if len(parts) == 1 else jnp.concatenate(parts, axis=1)


def spread(line, rows=ROWS):
    return jnp.broadcast_to(line, (rows, line.shape[1]))


def edge_line(tile, top_half, base=0, rows=ROWS):
    return jnp.where(top_half, tile[base + rows - 1 : base + rows], tile[base : base + 1])


def pack(odd, top_half, fine, coarse, stiff, coarse_stiff, a_buf, b_buf, y_buf, da_buf, db_buf, width):
    half = width // 2
    quarter = width // 4
    with_k = stiff is not None
    fields = 7 if with_k else 6
    zero = jnp.zeros((2, half), F32)
    upper = iota((ROWS, half), 0) < 4

    def tile(f, z):
        return fine(f, z) if f < 6 else stiff(z)

    base = 3 * width + (half if with_k else 0)
    for f in range(fields):
        for z in range(PLANES):
            t = tile(f, z)
            line = edge_line(t, top_half)
            put(y_buf, fine_row(f * PLANES + z, width), line)
            if z == 0:
                low, low_line = t, line
        a_buf[:, f * width : (f + 1) * width] = jnp.where(odd, low, t)
        b_buf[:, f * width : (f + 1) * width] = jnp.where(odd, t, low)
        g = f if f < 3 else (3 if f == 6 else None)
        if g is not None:
            put(da_buf, corner_fine(g, width), jnp.where(odd, low_line, line))
            put(db_buf, corner_fine(g, width), jnp.where(odd, line, low_line))

    for f in range(fields):
        t = coarse(f) if f < 6 else coarse_stiff
        lines = [edge_line(t, top_half, 4 * zc, 4) for zc in range(2)]
        for zc in range(2):
            put(y_buf, coarse_row(2 * f + zc, width, base), lines[zc])
        g = f if f < 3 else (3 if f == 6 else None)
        if g is not None:
            put(da_buf, corner_coarse(g, width), jnp.where(odd, lines[0], lines[1]))
            put(db_buf, corner_coarse(g, width), jnp.where(odd, lines[1], lines[0]))
    if with_k:
        y_buf[6:8, base + half : base + 2 * half] = zero
    else:
        y_buf[4:8, base + half : base + 2 * half] = jnp.zeros((4, half), F32)
        da_buf[6:8, :] = jnp.zeros((2, da_buf.shape[1]), F32)
        db_buf[6:8, :] = jnp.zeros((2, db_buf.shape[1]), F32)

    at = fields * width
    for c in range(FIELDS):
        first, second = coarse(c), coarse(c + 3)
        low = jnp.where(upper, first, roll(second, 4, 0))
        high = jnp.where(upper, roll(first, 4, 0), second)
        a_buf[:, at : at + half] = jnp.where(odd, low, high)
        b_buf[:, at : at + half] = jnp.where(odd, high, low)
        at += half
    if with_k:
        some = iota((ROWS, quarter), 0) < 4
        low, high = coarse_stiff, roll(coarse_stiff, 4, 0)
        low = jnp.where(some, low[:, :quarter], roll(low[:, quarter:], 4, 0))
        high = jnp.where(some, high[:, :quarter], roll(high[:, quarter:], 4, 0))
        a_buf[:, at : at + quarter] = jnp.where(odd, low, high)
        b_buf[:, at : at + quarter] = jnp.where(odd, high, low)


def begin_kernel(
    mask, drive, comp, stiff, now, before,
    w_out, cu_out, cw_out, ck_out, cf_out, a_buf, b_buf, y_buf, da_buf, db_buf,
    coef, group, wide,
):
    odd, top_half, _, _ = place()
    width = stiff.shape[2]
    half = width // 2
    row = iota((ROWS, width), 0)
    even_row = lax.rem(row, 2) == 0

    for c in range(FIELDS):
        group[c] = group_drive(comp[...], drive, c)

    def pooled(first, second):
        first = first + roll(first, -1, 0)
        second = second + roll(second, -1, 0)
        return jnp.where(even_row, first, roll(second, 1, 0))

    tiles = []
    for c in range(FIELDS):
        tiles.append(pooled(now[c, 0] + now[c, 1], now[c, 2] + now[c, 3]))
    for c in range(FIELDS):
        tiles.append(pooled(before[c, 0] + before[c, 1], before[c, 2] + before[c, 3]))
    tiles.append(pooled(stiff[0] + stiff[1], stiff[2] + stiff[3]))
    for c in range(FIELDS):
        tiles.append(pooled(group[c], group[c]))
    stacked = jnp.concatenate(tiles, axis=0)
    pool = jnp.where(iota((256, 128), 0) // 2 == iota((256, 128), 1), 0.125, 0.0)
    for q in range(width // 256):
        wide[q] = lax.dot_general(
            stacked[:, q * 256 : (q + 1) * 256], pool, (((1,), (0,)), ((), ())),
            precision=lax.Precision.HIGHEST, preferred_element_type=F32,
        )

    def coarse_tile(f):
        planes = [
            jnp.concatenate([wide[q, pl.ds(8 * f + zc, 4, stride=2), :] for q in range(half // 128)], axis=1)
            for zc in range(2)
        ]
        return jnp.concatenate(planes, axis=0)

    on = [mask[z].astype(F32) for z in range(PLANES)]
    upper = iota((ROWS, half), 0) < 4
    weight = jnp.where(upper, on[0] + on[1], on[2] + on[3]) * TIME_SQUARE
    ck_out[...] = coarse_tile(6)
    coefs = coarse_coefs(ck_out[...], top_half)
    for c in range(FIELDS):
        cu_out[c] = coarse_tile(c)
        cf_out[c] = coarse_tile(7 + c) * weight
        cw_out[c] = coarse_free(cu_out[c], coarse_tile(3 + c), coefs, cf_out[c])

    fine_coefs(stiff, top_half, coef)
    for c in range(FIELDS):
        for z in range(PLANES):
            w_out[c, z] = fine_free(
                now, before[c, z], c, z, coef, group[c] * (TIME_SQUARE * on[z])
            )
    pack(
        odd, top_half,
        lambda f, z: now[f, z] if f < 3 else w_out[f - 3, z],
        lambda f: cu_out[f] if f < 3 else cw_out[f - 3],
        lambda z: stiff[z], ck_out[...],
        a_buf, b_buf, y_buf, da_buf, db_buf, width,
    )


def join(
    round_one, round_two, mask, drive, comp, stiff, now, free, cu_now, cu_free, ck, cf,
    mid, mid_y, mid_low, mid_high, coef, halo, group, emit, emit_coarse, coarse_mid,
):
    odd, top_half, has_low, has_high = place()
    width = stiff.shape[2]
    half = width // 2
    quarter = width // 4
    a_one, b_one, y_one, da_one, db_one = round_one
    a_two, b_two, y_two, da_two, db_two = round_two
    row = iota((ROWS, width), 0)
    edge_row = row == jnp.where(top_half, ROWS - 1, 0)

    def low_of(a, b, at, lanes=width):
        return jnp.where(odd, a[:, at : at + lanes], b[:, at : at + lanes])

    def high_of(a, b, at, lanes=width):
        return jnp.where(odd, b[:, at : at + lanes], a[:, at : at + lanes])

    def corner(a, b, pieces):
        first, second = take(a, pieces), take(b, pieces)
        return spread(jnp.where(odd, first, second)), spread(jnp.where(odd, second, first))

    def y_tile(buf, f, z):
        return spread(take(buf, fine_row(f * PLANES + z, width)))

    for z in range(PLANES):
        halo[z] = jnp.where(edge_row, FINE_FACE * (stiff[z] + y_tile(y_one, 6, z)), 0.0)
    k_low = low_of(a_one, b_one, 6 * width)
    k_high = high_of(a_one, b_one, 6 * width)
    halo[4] = FINE_FACE * (stiff[0] + k_low)
    halo[5] = FINE_FACE * (stiff[PLANES - 1] + k_high)
    kd_low, kd_high = corner(da_one, db_one, corner_fine(3, width))
    halo[6] = jnp.where(edge_row, FINE_FACE * (k_low + kd_low), 0.0)
    halo[7] = jnp.where(edge_row, FINE_FACE * (k_high + kd_high), 0.0)
    halo[8] = FINE_FACE * (y_tile(y_one, 6, 0) + kd_low)
    halo[9] = FINE_FACE * (y_tile(y_one, 6, PLANES - 1) + kd_high)
    fine_coefs(stiff, top_half, coef)
    for c in range(FIELDS):
        group[c] = group_drive(comp[...], drive, c)
    on = [mask[z].astype(F32) * TIME_SQUARE for z in range(PLANES)]

    for c in range(FIELDS):
        d_low, d_high = corner(da_two, db_two, corner_fine(c, width))
        for z in range(PLANES):
            u = now[c, z]
            u_y = y_tile(y_two, c, z)
            flux = halo[z] * (u_y - u)
            new = free[c, z] + flux
            new_y = y_tile(y_two, 3 + c, z) - flux
            if z == 0:
                other = low_of(a_two, b_two, c * width)
                flux = halo[4] * (other - u)
                new = new + flux
                out = low_of(a_two, b_two, (3 + c) * width) - flux + halo[6] * (d_low - other)
                mid_low[c] = jnp.where(has_low, out, 0.0)
                new_y = new_y + halo[8] * (d_low - u_y)
            if z == PLANES - 1:
                other = high_of(a_two, b_two, c * width)
                flux = halo[5] * (other - u)
                new = new + flux
                out = high_of(a_two, b_two, (3 + c) * width) - flux + halo[7] * (d_high - other)
                mid_high[c] = jnp.where(has_high, out, 0.0)
                new_y = new_y + halo[9] * (d_high - u_y)
            mid[c, z] = new
            mid_y[c, z] = new_y
    for c in range(FIELDS):
        for z in range(PLANES):
            u = mid[c, z]
            new = fine_free(mid, now[c, z], c, z, coef, group[c] * on[z])
            new = new + halo[z] * (mid_y[c, z] - u)
            if z == 0:
                new = new + halo[4] * (mid_low[c] - u)
            if z == PLANES - 1:
                new = new + halo[5] * (mid_high[c] - u)
            emit(c, z, new)

    crow = iota((ROWS, half), 0)
    upper = crow < 4
    c_edge = lax.rem(crow, 4) == jnp.where(top_half, 3, 0)
    fields_one, fields_two = 7, 7 if round_two is round_one else 6
    base_one = 3 * width + half
    base_two = base_one if round_two is round_one else 3 * width

    def cy_tile(buf, f, base):
        lines = [take(buf, coarse_row(2 * f + zc, width, base)) for zc in range(2)]
        return jnp.where(upper, spread(lines[0]), spread(lines[1]))

    def c_corner(a, b, g):
        first, second = take(a, corner_coarse(g, width)), take(b, corner_coarse(g, width))
        low, high = jnp.where(odd, first, second), jnp.where(odd, second, first)
        return jnp.where(upper, spread(low), spread(high))

    def plane_pair(a, b, c):
        at = fields_two * width + c * half
        low, high = low_of(a, b, at, half), high_of(a, b, at, half)
        return (
            jnp.where(upper, low, roll(high, 4, 0)),
            jnp.where(upper, roll(low, 4, 0), high),
        )

    at = fields_one * width + 3 * half
    low, high = low_of(a_one, b_one, at, quarter), high_of(a_one, b_one, at, quarter)
    kz = jnp.where(
        upper,
        jnp.concatenate([low, roll(low, 4, 0)], axis=1),
        jnp.concatenate([roll(high, 4, 0), high], axis=1),
    )
    k = ck[...]
    kd = c_corner(da_one, db_one, 3)
    ky = cy_tile(y_one, 6, base_one)
    face_z = COARSE_FACE * (k + kz)
    face_y = jnp.where(c_edge, COARSE_FACE * (k + ky), 0.0)
    face_zd = jnp.where(c_edge, COARSE_FACE * (kz + kd), 0.0)
    face_yd = COARSE_FACE * (ky + kd)
    inside = jnp.where(upper, jnp.where(has_low, 1.0, 0.0), jnp.where(has_high, 1.0, 0.0))
    coefs = coarse_coefs(k, top_half)
    for c in range(FIELDS):
        u = cu_now[c]
        u_z, w_z = plane_pair(a_two, b_two, c)
        u_y = cy_tile(y_two, c, base_two)
        u_d = c_corner(da_two, db_two, c)
        flux_z = face_z * (u_z - u)
        flux_y = face_y * (u_y - u)
        new = cu_free[c] + flux_z + flux_y
        new_z = inside * (w_z - flux_z + face_zd * (u_d - u_z))
        new_y = cy_tile(y_two, 3 + c, base_two) - flux_y + face_yd * (u_d - u_y)
        coarse_mid[c] = new
        after = coarse_free(new, u, coefs, cf[c])
        emit_coarse(c, after + face_z * (new_z - new) + face_y * (new_y - new))
    return odd, top_half, on, coefs


def middle_kernel(
    mask, drive, comp, stiff, now, free, cu_now, cu_free, ck, cf,
    a_one, b_one, y_one, da_one, db_one,
    u_out, w_out, cu_out, cw_out, a_buf, b_buf, y_buf, da_buf, db_buf,
    mid, mid_y, mid_low, mid_high, coef, halo, group, coarse_mid,
):
    one = (a_one, b_one, y_one, da_one, db_one)

    def emit(c, z, value):
        u_out[c, z] = value

    def emit_coarse(c, value):
        cu_out[c] = value

    odd, top_half, on, coefs = join(
        one, one, mask, drive, comp, stiff, now, free, cu_now, cu_free, ck, cf,
        mid, mid_y, mid_low, mid_high, coef, halo, group, emit, emit_coarse, coarse_mid,
    )
    for c in range(FIELDS):
        cw_out[c] = coarse_free(cu_out[c], coarse_mid[c], coefs, cf[c])
        for z in range(PLANES):
            w_out[c, z] = fine_free(u_out, mid[c, z], c, z, coef, group[c] * on[z])
    pack(
        odd, top_half,
        lambda f, z: u_out[f, z] if f < 3 else w_out[f - 3, z],
        lambda f: cu_out[f] if f < 3 else cw_out[f - 3],
        None, None, a_buf, b_buf, y_buf, da_buf, db_buf, stiff.shape[2],
    )


def end_kernel(
    mask, drive, comp, stiff, now, free, cu_now, cu_free, ck, cf,
    a_one, b_one, y_one, da_one, db_one,
    a_two, b_two, y_two, da_two, db_two,
    u_out, cu_out,
    mid, mid_y, mid_low, mid_high, coef, halo, group, coarse_mid,
):
    def emit(c, z, value):
        u_out[c, z] = value

    def emit_coarse(c, value):
        for zc in range(2):
            cu_out[c, zc] = value[4 * zc : 4 * zc + 4]

    join(
        (a_one, b_one, y_one, da_one, db_one), (a_two, b_two, y_two, da_two, db_two),
        mask, drive, comp, stiff, now, free, cu_now, cu_free, ck, cf,
        mid, mid_y, mid_low, mid_high, coef, halo, group, emit, emit_coarse, coarse_mid,
    )


def struct(*shape):
    return jax.ShapeDtypeStruct(shape, F32)


def call(kernel, name, outs, scratch, operands):
    smem = pl.BlockSpec(memory_space=pltpu.SMEM)
    vmem = pl.BlockSpec(memory_space=pltpu.VMEM)
    return pl.pallas_call(
        kernel,
        name=name,
        out_shape=outs,
        in_specs=[smem, smem] + [vmem] * (len(operands) - 2),
        out_specs=[vmem] * len(outs),
        scratch_shapes=scratch,
        compiler_params=pltpu.CompilerParams(vmem_limit_bytes=32 * 1024 * 1024),
    )(*operands)


def exchange(bufs):
    count = lax.axis_size("ax")
    pair_a = [(i, i ^ 1) for i in range(count)]
    pair_b = [(i, i + 1 if i % 2 else i - 1) for i in range(1, count - 1)]

    def across(pairs):
        return [(2 * i + s, 2 * j + 1 - s) for i, j in pairs for s in (0, 1)]

    a, b, y, da, db = bufs
    b = lax.ppermute(b, "ax", pair_b)
    y = lax.ppermute(y, "xs", [(0, 1), (1, 0)])
    a = lax.ppermute(a, "ax", pair_a)
    db = lax.ppermute(db, ("ax", "xs"), across(pair_b))
    da = lax.ppermute(da, ("ax", "xs"), across(pair_a))
    return a, b, y, da, db


def local(displacement, previous, stiffness, tissue_mask, compartment, drive):
    width = displacement.shape[3]
    half = width // 2
    quarter = width // 4
    field = struct(FIELDS, PLANES, ROWS, width)
    coarse = struct(FIELDS, ROWS, half)

    def buffers(fields, with_k):
        plane = fields * width + 3 * half + (quarter if with_k else 0)
        rows = 3 * width + (3 * half if with_k else 2 * half)
        corner = struct(ROWS, half + quarter)
        return [struct(ROWS, plane), struct(ROWS, plane), struct(ROWS, rows), corner, corner]

    coef = pltpu.VMEM((6, PLANES, ROWS, width), F32)
    group = pltpu.VMEM((FIELDS, ROWS, width), F32)
    steps = [
        pltpu.VMEM((FIELDS, PLANES, ROWS, width), F32),
        pltpu.VMEM((FIELDS, PLANES, ROWS, width), F32),
        pltpu.VMEM((FIELDS, ROWS, width), F32),
        pltpu.VMEM((FIELDS, ROWS, width), F32),
        coef,
        pltpu.VMEM((10, ROWS, width), F32),
        group,
        pltpu.VMEM((FIELDS, ROWS, half), F32),
    ]
    fixed = (tissue_mask, drive, compartment, stiffness)
    w, cu, cw, ck, cf, *bufs = call(
        begin_kernel,
        "restrict_and_first_step",
        [field, coarse, coarse, struct(ROWS, half), coarse] + buffers(7, True),
        [coef, group, pltpu.VMEM((half // 128, 10 * ROWS, 128), F32)],
        fixed + (displacement, previous),
    )
    one = exchange(bufs)
    u, w, cu, cw, *bufs = call(
        middle_kernel,
        "two_steps",
        [field, field, coarse, coarse] + buffers(6, False),
        steps,
        fixed + (displacement, w, cu, cw, ck, cf) + one,
    )
    two = exchange(bufs)
    return call(
        end_kernel,
        "last_steps",
        [field, struct(FIELDS, 2, 4, half)],
        steps,
        fixed + (u, w, cu, cw, ck, cf) + one + two,
    )


def solution(mesh):
    placed = (
        P(None, "ax", "xs", None),
        P(None, "ax", "xs", None),
        P("ax", "xs", None),
        P("ax"),
        P("xs", None),
        P(),
    )

    def run(*args):
        return tuple(local(*args))

    return jax.shard_map(
        run,
        mesh=mesh,
        in_specs=placed,
        out_specs=(P(None, "ax", "xs", None), P(None, "ax", "xs", None)),
        check_vma=False,
    )
```

```python
import jax
import jax.numpy as jnp
from jax import lax
from jax.experimental import pallas as pl
from jax.experimental.pallas import tpu as pltpu
from jax.sharding import PartitionSpec as P

TIME_SQUARE = 0.12
FINE_FACE = 0.5 * TIME_SQUARE
COARSE_FACE = 0.25 * 0.5 * TIME_SQUARE
PLANES = 4
ROWS = 8
FIELDS = 3
F32 = jnp.float32


def roll(x, shift, axis):
    return pltpu.roll(x, shift % x.shape[axis], axis)


def place():
    i = lax.axis_index("ax")
    s = lax.axis_index("xs")
    return (lax.rem(i, 2) == 1), (s == 0), (i > 0), (i < lax.axis_size("ax") - 1)


def iota(shape, dim):
    return lax.broadcasted_iota(jnp.int32, shape, dim)


def stiff_coefs(k, face, low_y, high_y, outer_row):
    width = k.shape[1]
    lane = iota(k.shape, 1)
    last = lane == width - 1
    start = lane == 0
    kp = jnp.where(last, 0.0, roll(k, -1, 1))
    km = jnp.where(start, 0.0, roll(k, 1, 1))
    full_p = face * (k + kp)
    full_m = face * (k + km)
    cyp = jnp.where(high_y, face * (k + roll(k, -1, 0)), 0.0)
    cym = jnp.where(low_y, face * (k + roll(k, 1, 0)), 0.0)
    edge = jnp.where(outer_row, face * k, 0.0)
    centre = 2.0 - (full_p + full_m + cyp + cym + edge)
    return jnp.where(last, 0.0, full_p), jnp.where(start, 0.0, full_m), cyp, cym, centre


def fine_coefs(k_ref, first, coef):
    shape = k_ref.shape[1:]
    row = iota(shape, 0)
    for z in range(PLANES - 1):
        coef[5, z] = FINE_FACE * (k_ref[z] + k_ref[z + 1])
    for z in range(PLANES):
        cxp, cxm, cyp, cym, centre = stiff_coefs(
            k_ref[z], FINE_FACE, row > 0, row < ROWS - 1, row == jnp.where(first, 0, ROWS - 1)
        )
        if z > 0:
            centre = centre - coef[5, z - 1]
        if z < PLANES - 1:
            centre = centre - coef[5, z]
        coef[0, z] = cxp
        coef[1, z] = cxm
        coef[2, z] = cyp
        coef[3, z] = cym
        coef[4, z] = centre


def fine_free(u_ref, before, c, z, coef, drive_term):
    u = u_ref[c, z]
    acc = coef[4, z] * u - before
    acc = acc + coef[0, z] * roll(u, -1, 1) + coef[1, z] * roll(u, 1, 1)
    acc = acc + coef[2, z] * roll(u, -1, 0) + coef[3, z] * roll(u, 1, 0)
    if z > 0:
        acc = acc + coef[5, z - 1] * u_ref[c, z - 1]
    if z < PLANES - 1:
        acc = acc + coef[5, z] * u_ref[c, z + 1]
    return acc + drive_term


def coarse_coefs(k, first):
    row = iota(k.shape, 0)
    inner = lax.rem(row, 4)
    cxp, cxm, cyp, cym, centre = stiff_coefs(
        k, COARSE_FACE, inner > 0, inner < 3, inner == jnp.where(first, 0, 3)
    )
    cz = COARSE_FACE * (k + roll(k, 4, 0))
    return cxp, cxm, cyp, cym, centre - cz, cz


def coarse_free(u, before, coefs, force):
    cxp, cxm, cyp, cym, centre, cz = coefs
    return (
        centre * u
        - before
        + cxp * roll(u, -1, 1)
        + cxm * roll(u, 1, 1)
        + cyp * roll(u, -1, 0)
        + cym * roll(u, 1, 0)
        + cz * roll(u, 4, 0)
        + force
    )


def group_drive(compartment, drive_ref, c):
    value = jnp.full(compartment.shape, drive_ref[c, 0], F32)
    for g in range(1, drive_ref.shape[1]):
        value = jnp.where(compartment == g, drive_ref[c, g], value)
    return value


def fine_row(r, width):
    if r < 24:
        return [(r % 8, (r // 8) * width, width)]
    half = width // 2
    return [(2 * (r - 24) + h, 3 * width, half) for h in range(2)]


def coarse_row(q, width, base):
    half = width // 2
    return [(q % 8, base + (q // 8) * half, half)]


def corner_fine(f, width):
    half = width // 2
    return [(2 * f + h, 0, half) for h in range(2)]


def corner_coarse(f, width):
    quarter = width // 4
    return [(2 * f + h, width // 2, quarter) for h in range(2)]


def put(buf, pieces, line):
    at = 0
    for row, lane, lanes in pieces:
        buf[row : row + 1, lane : lane + lanes] = line[:, at : at + lanes]
        at += lanes


def take(buf, pieces):
    parts = [buf[row : row + 1, lane : lane + lanes] for row, lane, lanes in pieces]
    return parts[0] if len(parts) == 1 else jnp.concatenate(parts, axis=1)


def spread(line, rows=ROWS):
    return jnp.broadcast_to(line, (rows, line.shape[1]))


def edge_line(tile, top_half, base=0, rows=ROWS):
    return jnp.where(top_half, tile[base + rows - 1 : base + rows], tile[base : base + 1])


def pack(odd, top_half, fine, coarse, stiff, coarse_stiff, a_buf, b_buf, y_buf, db_buf, width):
    half = width // 2
    quarter = width // 4
    with_k = stiff is not None
    fields = 7 if with_k else 6
    zero = jnp.zeros((2, half), F32)
    upper = iota((ROWS, half), 0) < 4

    def tile(f, z):
        return fine(f, z) if f < 6 else stiff(z)

    base = 3 * width + (half if with_k else 0)
    for f in range(fields):
        for z in range(PLANES):
            t = tile(f, z)
            line = edge_line(t, top_half)
            put(y_buf, fine_row(f * PLANES + z, width), line)
            if z == 0:
                low, low_line = t, line
        a_buf[:, f * width : (f + 1) * width] = jnp.where(odd, low, t)
        b_buf[:, f * width : (f + 1) * width] = jnp.where(odd, t, low)
        g = f if f < 3 else (3 if f == 6 else None)
        if g is not None:
            put(db_buf, corner_fine(g, width), jnp.where(odd, line, low_line))

    for f in range(fields):
        t = coarse(f) if f < 6 else coarse_stiff
        lines = [edge_line(t, top_half, 4 * zc, 4) for zc in range(2)]
        for zc in range(2):
            put(y_buf, coarse_row(2 * f + zc, width, base), lines[zc])
        g = f if f < 3 else (3 if f == 6 else None)
        if g is not None:
            put(db_buf, corner_coarse(g, width), jnp.where(odd, lines[1], lines[0]))
    if with_k:
        y_buf[6:8, base + half : base + 2 * half] = zero
    else:
        y_buf[4:8, base + half : base + 2 * half] = jnp.zeros((4, half), F32)
        db_buf[6:8, :] = jnp.zeros((2, db_buf.shape[1]), F32)

    at = fields * width
    for c in range(FIELDS):
        first, second = coarse(c), coarse(c + 3)
        low = jnp.where(upper, first, roll(second, 4, 0))
        high = jnp.where(upper, roll(first, 4, 0), second)
        a_buf[:, at : at + half] = jnp.where(odd, low, high)
        b_buf[:, at : at + half] = jnp.where(odd, high, low)
        at += half
    if with_k:
        some = iota((ROWS, quarter), 0) < 4
        low, high = coarse_stiff, roll(coarse_stiff, 4, 0)
        low = jnp.where(some, low[:, :quarter], roll(low[:, quarter:], 4, 0))
        high = jnp.where(some, high[:, :quarter], roll(high[:, quarter:], 4, 0))
        a_buf[:, at : at + quarter] = jnp.where(odd, low, high)
        b_buf[:, at : at + quarter] = jnp.where(odd, high, low)


def begin_kernel(
    mask_hbm, drive_hbm, comp_hbm, stiff_hbm, now_hbm, before_hbm,
    y_buf, b_buf, db_buf, a_buf, now, stiff, coef, force, w_out, cu_out, cw_out, ck_out, cf_out,
    mask, drive, comp, before, group, wide, sems,
):
    pairs = (
        (drive_hbm, drive), (mask_hbm, mask), (comp_hbm, comp), (stiff_hbm, stiff),
        (now_hbm, now), (before_hbm, before),
    )
    copies = [pltpu.make_async_copy(src, dst, sems.at[n]) for n, (src, dst) in enumerate(pairs)]
    for copy in copies:
        copy.start()
    odd, top_half, _, _ = place()
    width = stiff.shape[2]
    half = width // 2
    row = iota((ROWS, width), 0)
    even_row = lax.rem(row, 2) == 0

    for copy in copies[:3]:
        copy.wait()
    on = [mask[z].astype(F32) for z in range(PLANES)]
    for c in range(FIELDS):
        group[c] = group_drive(comp[...], drive, c)
    for c in range(FIELDS):
        for z in range(PLANES):
            force[c, z] = group[c] * (TIME_SQUARE * on[z])
    copies[3].wait()
    fine_coefs(stiff, top_half, coef)
    for copy in copies[4:]:
        copy.wait()

    def pooled(first, second):
        first = first + roll(first, -1, 0)
        second = second + roll(second, -1, 0)
        return jnp.where(even_row, first, roll(second, 1, 0))

    tiles = []
    for c in range(FIELDS):
        tiles.append(pooled(now[c, 0] + now[c, 1], now[c, 2] + now[c, 3]))
    for c in range(FIELDS):
        tiles.append(pooled(before[c, 0] + before[c, 1], before[c, 2] + before[c, 3]))
    tiles.append(pooled(stiff[0] + stiff[1], stiff[2] + stiff[3]))
    for c in range(FIELDS):
        tiles.append(pooled(group[c], group[c]))
    stacked = jnp.concatenate(tiles, axis=0)
    pool = jnp.where(iota((256, 128), 0) // 2 == iota((256, 128), 1), 0.125, 0.0)
    for q in range(width // 256):
        wide[q] = lax.dot_general(
            stacked[:, q * 256 : (q + 1) * 256], pool, (((1,), (0,)), ((), ())),
            precision=lax.Precision.HIGHEST, preferred_element_type=F32,
        )

    def coarse_tile(f):
        planes = [
            jnp.concatenate([wide[q, pl.ds(8 * f + zc, 4, stride=2), :] for q in range(half // 128)], axis=1)
            for zc in range(2)
        ]
        return jnp.concatenate(planes, axis=0)

    upper = iota((ROWS, half), 0) < 4
    weight = jnp.where(upper, on[0] + on[1], on[2] + on[3]) * TIME_SQUARE
    ck_out[...] = coarse_tile(6)
    coefs = coarse_coefs(ck_out[...], top_half)
    for c in range(FIELDS):
        cu_out[c] = coarse_tile(c)
        cf_out[c] = coarse_tile(7 + c) * weight
        cw_out[c] = coarse_free(cu_out[c], coarse_tile(3 + c), coefs, cf_out[c])

    for c in range(FIELDS):
        for z in range(PLANES):
            w_out[c, z] = fine_free(now, before[c, z], c, z, coef, force[c, z])
    pack(
        odd, top_half,
        lambda f, z: now[f, z] if f < 3 else w_out[f - 3, z],
        lambda f: cu_out[f] if f < 3 else cw_out[f - 3],
        lambda z: stiff[z], ck_out[...],
        a_buf, b_buf, y_buf, db_buf, width,
    )


class Halo:
    def __init__(self, bufs, with_k, odd, width):
        self.y, self.b, self.db, self.a, self.ya = bufs
        self.odd, self.width, self.with_k = odd, width, with_k
        self.fields = 7 if with_k else 6
        self.base = 3 * width + (width // 2 if with_k else 0)

    def low(self, at, lanes):
        return jnp.where(self.odd, self.a[:, at : at + lanes], self.b[:, at : at + lanes])

    def high(self, at, lanes):
        return jnp.where(self.odd, self.b[:, at : at + lanes], self.a[:, at : at + lanes])

    def plane_low(self, f):
        return self.low(f * self.width, self.width)

    def plane_high(self, f):
        return self.high(f * self.width, self.width)

    def rows(self, f, z):
        return spread(take(self.y, fine_row(f * PLANES + z, self.width)))

    def corners(self, f):
        near = [take(self.ya, fine_row(f * PLANES + z, self.width)) for z in (PLANES - 1, 0)]
        far = take(self.db, corner_fine(3 if f == 6 else f, self.width))
        low = jnp.where(self.odd, near[0], far)
        high = jnp.where(self.odd, far, near[1])
        return spread(low), spread(high)

    def coarse_rows(self, f, upper, buf=None):
        buf = self.y if buf is None else buf
        lines = [take(buf, coarse_row(2 * f + zc, self.width, self.base)) for zc in range(2)]
        return jnp.where(upper, spread(lines[0]), spread(lines[1]))

    def coarse_corner(self, f, upper):
        near = [take(self.ya, coarse_row(2 * f + zc, self.width, self.base)) for zc in (1, 0)]
        far = take(self.db, corner_coarse(3 if f == 6 else f, self.width))
        low = jnp.where(self.odd, near[0], far)
        high = jnp.where(self.odd, far, near[1])
        return jnp.where(upper, spread(low), spread(high))

    def coarse_planes(self, c, upper):
        half = self.width // 2
        at = self.fields * self.width + c * half
        low, high = self.low(at, half), self.high(at, half)
        return (
            jnp.where(upper, low, roll(high, 4, 0)),
            jnp.where(upper, roll(low, 4, 0), high),
        )

    def coarse_stiff_planes(self, upper):
        at = self.fields * self.width + 3 * (self.width // 2)
        low, high = self.low(at, self.width // 4), self.high(at, self.width // 4)
        return jnp.where(
            upper,
            jnp.concatenate([low, roll(low, 4, 0)], axis=1),
            jnp.concatenate([roll(high, 4, 0), high], axis=1),
        )


def faces(got, stiff, ck, halo, coarse_halo, top_half, has_low, has_high):
    shape = stiff.shape[1:]
    half = shape[1] // 2
    edge_row = iota(shape, 0) == jnp.where(top_half, ROWS - 1, 0)
    for z in range(PLANES):
        halo[z] = jnp.where(edge_row, FINE_FACE * (stiff[z] + got.rows(6, z)), 0.0)
    k_low, k_high = got.plane_low(6), got.plane_high(6)
    kd_low, kd_high = got.corners(6)
    halo[4] = FINE_FACE * (stiff[0] + k_low)
    halo[5] = FINE_FACE * (stiff[PLANES - 1] + k_high)
    halo[6] = jnp.where(edge_row, FINE_FACE * (k_low + kd_low), 0.0)
    halo[7] = jnp.where(edge_row, FINE_FACE * (k_high + kd_high), 0.0)
    halo[8] = FINE_FACE * (got.rows(6, 0) + kd_low)
    halo[9] = FINE_FACE * (got.rows(6, PLANES - 1) + kd_high)

    row = iota((ROWS, half), 0)
    upper = row < 4
    edge = lax.rem(row, 4) == jnp.where(top_half, 3, 0)
    k = ck[...]
    kz, ky, kd = got.coarse_stiff_planes(upper), got.coarse_rows(6, upper), got.coarse_corner(6, upper)
    coarse_halo[0] = COARSE_FACE * (k + kz)
    coarse_halo[1] = jnp.where(edge, COARSE_FACE * (k + ky), 0.0)
    coarse_halo[2] = jnp.where(edge, COARSE_FACE * (kz + kd), 0.0)
    coarse_halo[3] = COARSE_FACE * (ky + kd)
    coarse_halo[4] = jnp.where(upper, jnp.where(has_low, 1.0, 0.0), jnp.where(has_high, 1.0, 0.0))


def join(
    got, coef, halo, coarse_halo, force, now, free, cu_now, cu_free, ck, cf,
    mid, mid_y, mid_low, mid_high, coarse_mid, emit, emit_coarse, top_half, has_low, has_high,
):
    for c in range(FIELDS):
        d_low, d_high = got.corners(c)
        for z in range(PLANES):
            u = now[c, z]
            u_y = got.rows(c, z)
            flux = halo[z] * (u_y - u)
            new = free[c, z] + flux
            new_y = got.rows(3 + c, z) - flux
            if z == 0:
                other = got.plane_low(c)
                flux = halo[4] * (other - u)
                new = new + flux
                out = got.plane_low(3 + c) - flux + halo[6] * (d_low - other)
                mid_low[c] = jnp.where(has_low, out, 0.0)
                new_y = new_y + halo[8] * (d_low - u_y)
            if z == PLANES - 1:
                other = got.plane_high(c)
                flux = halo[5] * (other - u)
                new = new + flux
                out = got.plane_high(3 + c) - flux + halo[7] * (d_high - other)
                mid_high[c] = jnp.where(has_high, out, 0.0)
                new_y = new_y + halo[9] * (d_high - u_y)
            mid[c, z] = new
            mid_y[c, z] = new_y

        for z in range(PLANES):
            u = mid[c, z]
            new = fine_free(mid, now[c, z], c, z, coef, force[c, z])
            new = new + halo[z] * (mid_y[c, z] - u)
            if z == 0:
                new = new + halo[4] * (mid_low[c] - u)
            if z == PLANES - 1:
                new = new + halo[5] * (mid_high[c] - u)
            emit(c, z, new)

    upper = iota(cf.shape[1:], 0) < 4
    face_z, face_y, face_zd, face_yd, inside = [coarse_halo[n] for n in range(5)]
    coefs = coarse_coefs(ck[...], top_half)
    for c in range(FIELDS):
        u = cu_now[c]
        u_z, w_z = got.coarse_planes(c, upper)
        u_y = got.coarse_rows(c, upper)
        u_d = got.coarse_corner(c, upper)
        flux_z = face_z * (u_z - u)
        flux_y = face_y * (u_y - u)
        new = cu_free[c] + flux_z + flux_y
        new_z = inside * (w_z - flux_z + face_zd * (u_d - u_z))
        new_y = got.coarse_rows(3 + c, upper) - flux_y + face_yd * (u_d - u_y)
        coarse_mid[c] = new
        after = coarse_free(new, u, coefs, cf[c])
        emit_coarse(c, after + face_z * (new_z - new) + face_y * (new_y - new))
    return coefs


def middle_kernel(
    y_one, b_one, db_one, a_one, ya_one, coef, force, stiff, now, free, cu_now, cu_free, ck, cf,
    y_buf, b_buf, db_buf, a_buf, halo, coarse_halo, u_out, w_out, cu_out, cw_out,
    mid, mid_y, mid_low, mid_high, coarse_mid,
):
    odd, top_half, has_low, has_high = place()
    got = Halo((y_one, b_one, db_one, a_one, ya_one), True, odd, stiff.shape[2])
    faces(got, stiff, ck, halo, coarse_halo, top_half, has_low, has_high)

    def emit(c, z, value):
        u_out[c, z] = value

    def emit_coarse(c, value):
        cu_out[c] = value

    coefs = join(
        got, coef, halo, coarse_halo, force, now, free, cu_now, cu_free, ck, cf,
        mid, mid_y, mid_low, mid_high, coarse_mid, emit, emit_coarse, top_half, has_low, has_high,
    )
    for c in range(FIELDS):
        cw_out[c] = coarse_free(cu_out[c], coarse_mid[c], coefs, cf[c])
        for z in range(PLANES):
            w_out[c, z] = fine_free(u_out, mid[c, z], c, z, coef, force[c, z])
    pack(
        odd, top_half,
        lambda f, z: u_out[f, z] if f < 3 else w_out[f - 3, z],
        lambda f: cu_out[f] if f < 3 else cw_out[f - 3],
        None, None, a_buf, b_buf, y_buf, db_buf, stiff.shape[2],
    )


def end_kernel(
    y_two, b_two, db_two, a_two, ya_two, coef, force, halo, coarse_halo, now, free, cu_now, cu_free, ck, cf,
    u_hbm, cu_hbm,
    mid, mid_y, mid_low, mid_high, coarse_mid, last, coarse_last, sems,
):
    odd, top_half, has_low, has_high = place()
    got = Halo((y_two, b_two, db_two, a_two, ya_two), False, odd, coef.shape[3])
    copies = []

    def emit(c, z, value):
        last[c, z] = value
        if z == PLANES - 1:
            copies.append(pltpu.make_async_copy(last.at[c], u_hbm.at[c], sems.at[c]))
            copies[-1].start()

    def emit_coarse(c, value):
        for zc in range(2):
            coarse_last[c, zc] = value[4 * zc : 4 * zc + 4]

    join(
        got, coef, halo, coarse_halo, force, now, free, cu_now, cu_free, ck, cf,
        mid, mid_y, mid_low, mid_high, coarse_mid, emit, emit_coarse, top_half, has_low, has_high,
    )
    copies.append(pltpu.make_async_copy(coarse_last, cu_hbm, sems.at[FIELDS]))
    copies[-1].start()
    for copy in copies:
        copy.wait()


def struct(*shape):
    return jax.ShapeDtypeStruct(shape, F32)


def call(kernel, name, outs, scratch, operands, in_space=pltpu.VMEM, out_space=pltpu.VMEM, vmem=32):
    return pl.pallas_call(
        kernel,
        name=name,
        out_shape=outs,
        in_specs=[pl.BlockSpec(memory_space=in_space)] * len(operands),
        out_specs=[pl.BlockSpec(memory_space=out_space)] * len(outs),
        scratch_shapes=scratch,
        compiler_params=pltpu.CompilerParams(vmem_limit_bytes=vmem * 1024 * 1024),
    )(*operands)


def exchange(bufs):
    count = lax.axis_size("ax")
    pair_a = [(i, i ^ 1) for i in range(count)]
    pair_b = [(i, i + 1 if i % 2 else i - 1) for i in range(1, count - 1)]
    across = [(2 * i + s, 2 * j + 1 - s) for i, j in pair_b for s in (0, 1)]
    y, b, db, a = bufs
    y = lax.ppermute(y, "xs", [(0, 1), (1, 0)])
    b = lax.ppermute(b, "ax", pair_b)
    db = lax.ppermute(db, ("ax", "xs"), across)
    a = lax.ppermute(a, "ax", pair_a)
    y, db = lax.optimization_barrier((y, db))
    ya = lax.ppermute(y, "ax", pair_a)
    return y, b, db, a, ya


def local(displacement, previous, stiffness, tissue_mask, compartment, drive):
    width = displacement.shape[3]
    half = width // 2
    quarter = width // 4
    field = struct(FIELDS, PLANES, ROWS, width)
    coarse = struct(FIELDS, ROWS, half)

    def buffers(fields, with_k):
        plane = fields * width + 3 * half + (quarter if with_k else 0)
        rows = 3 * width + (3 * half if with_k else 2 * half)
        return [struct(ROWS, rows), struct(ROWS, plane), struct(ROWS, half + quarter), struct(ROWS, plane)]

    whole = pltpu.VMEM(field.shape, F32)
    tile = pltpu.VMEM((FIELDS, ROWS, width), F32)
    small = pltpu.VMEM(coarse.shape, F32)
    y, b, db, a, now, stiff, coef, force, w, cu, cw, ck, cf = call(
        begin_kernel,
        "restrict_and_first_step",
        buffers(7, True)
        + [field, struct(*stiffness.shape), struct(6, PLANES, ROWS, width), field, field]
        + [coarse, coarse, struct(ROWS, half), coarse],
        [
            pltpu.SMEM(tissue_mask.shape, jnp.int32),
            pltpu.SMEM(drive.shape, F32),
            pltpu.VMEM(compartment.shape, jnp.int32),
            whole,
            tile,
            pltpu.VMEM((half // 128, 10 * ROWS, 128), F32),
            pltpu.SemaphoreType.DMA((6,)),
        ],
        [
            pltpu.with_memory_space_constraint(x, pltpu.HBM)
            for x in (tissue_mask, drive, compartment, stiffness, displacement, previous)
        ],
        in_space=pltpu.HBM,
    )
    one = exchange((y, b, db, a))
    steps = [whole, whole, tile, tile, small]
    y, b, db, a, halo, coarse_halo, u, w, cu, cw = call(
        middle_kernel,
        "two_steps",
        buffers(6, False)
        + [struct(10, ROWS, width), struct(5, ROWS, half), field, field, coarse, coarse],
        steps,
        one + (coef, force, stiff, now, w, cu, cw, ck, cf),
    )
    two = exchange((y, b, db, a))
    return call(
        end_kernel,
        "last_steps",
        [field, struct(FIELDS, 2, 4, half)],
        steps + [whole, pltpu.VMEM((FIELDS, 2, 4, half), F32), pltpu.SemaphoreType.DMA((FIELDS + 1,))],
        two + (coef, force, halo, coarse_halo, u, w, cu, cw, ck, cf),
        out_space=pltpu.HBM,
    )


def solution(mesh):
    placed = (
        P(None, "ax", "xs", None),
        P(None, "ax", "xs", None),
        P("ax", "xs", None),
        P("ax"),
        P("xs", None),
        P(),
    )

    def run(*args):
        return tuple(local(*args))

    return jax.shard_map(
        run,
        mesh=mesh,
        in_specs=placed,
        out_specs=(P(None, "ax", "xs", None), P(None, "ax", "xs", None)),
        check_vma=False,
    )
```

```python
import jax
import jax.numpy as jnp
from jax import lax
from jax.experimental import pallas as pl
from jax.experimental.pallas import tpu as pltpu
from jax.sharding import PartitionSpec as P

TIME_SQUARE = 0.12
FINE_FACE = 0.5 * TIME_SQUARE
COARSE_FACE = 0.25 * 0.5 * TIME_SQUARE
PLANES = 4
ROWS = 8
FIELDS = 3
F32 = jnp.float32
PAD = 128


def roll(x, shift, axis):
    return pltpu.roll(x, shift % x.shape[axis], axis)


def place():
    i = lax.axis_index("ax")
    s = lax.axis_index("xs")
    return (lax.rem(i, 2) == 1), (s == 0), (i > 0), (i < lax.axis_size("ax") - 1)


def iota(shape, dim):
    return lax.broadcasted_iota(jnp.int32, shape, dim)


def stiff_coefs(k, face, low_y, high_y, outer_row):
    width = k.shape[1]
    lane = iota(k.shape, 1)
    last = lane == width - 1
    start = lane == 0
    kp = jnp.where(last, 0.0, roll(k, -1, 1))
    km = jnp.where(start, 0.0, roll(k, 1, 1))
    full_p = face * (k + kp)
    full_m = face * (k + km)
    cyp = jnp.where(high_y, face * (k + roll(k, -1, 0)), 0.0)
    cym = jnp.where(low_y, face * (k + roll(k, 1, 0)), 0.0)
    edge = jnp.where(outer_row, face * k, 0.0)
    centre = 2.0 - (full_p + full_m + cyp + cym + edge)
    return jnp.where(last, 0.0, full_p), jnp.where(start, 0.0, full_m), cyp, cym, centre


def fine_coefs(k_ref, first, coef):
    shape = k_ref.shape[1:]
    row = iota(shape, 0)
    for z in range(PLANES - 1):
        coef[5, z] = FINE_FACE * (k_ref[z] + k_ref[z + 1])
    for z in range(PLANES):
        cxp, cxm, cyp, cym, centre = stiff_coefs(
            k_ref[z], FINE_FACE, row > 0, row < ROWS - 1, row == jnp.where(first, 0, ROWS - 1)
        )
        if z > 0:
            centre = centre - coef[5, z - 1]
        if z < PLANES - 1:
            centre = centre - coef[5, z]
        coef[0, z] = cxp
        coef[1, z] = cxm
        coef[2, z] = cyp
        coef[3, z] = cym
        coef[4, z] = centre


def fine_free(u_ref, before, c, z, coef, drive_term):
    u = u_ref[c, z]
    acc = coef[4, z] * u - before
    acc = acc + coef[0, z] * roll(u, -1, 1) + coef[1, z] * roll(u, 1, 1)
    acc = acc + coef[2, z] * roll(u, -1, 0) + coef[3, z] * roll(u, 1, 0)
    if z > 0:
        acc = acc + coef[5, z - 1] * u_ref[c, z - 1]
    if z < PLANES - 1:
        acc = acc + coef[5, z] * u_ref[c, z + 1]
    return acc + drive_term


def coarse_coefs(k, first):
    row = iota(k.shape, 0)
    inner = lax.rem(row, 4)
    cxp, cxm, cyp, cym, centre = stiff_coefs(
        k, COARSE_FACE, inner > 0, inner < 3, inner == jnp.where(first, 0, 3)
    )
    cz = COARSE_FACE * (k + roll(k, 4, 0))
    return cxp, cxm, cyp, cym, centre - cz, cz


def coarse_free(u, before, coefs, force):
    cxp, cxm, cyp, cym, centre, cz = coefs
    return (
        centre * u
        - before
        + cxp * roll(u, -1, 1)
        + cxm * roll(u, 1, 1)
        + cyp * roll(u, -1, 0)
        + cym * roll(u, 1, 0)
        + cz * roll(u, 4, 0)
        + force
    )


def group_drive(compartment, drive_ref, c):
    value = jnp.full(compartment.shape, drive_ref[c, 0], F32)
    for g in range(1, drive_ref.shape[1]):
        value = jnp.where(compartment == g, drive_ref[c, g], value)
    return value


def fine_row(r, width):
    if r < 24:
        return [(r % 8, (r // 8) * width, width)]
    half = width // 2
    return [(2 * (r - 24) + h, 3 * width, half) for h in range(2)]


def coarse_row(q, width, base):
    half = width // 2
    return [(q % 8, base + (q // 8) * half, half)]


def corner_fine(f, width, base=0):
    half = width // 2
    return [(2 * f + h, base, half) for h in range(2)]


def corner_coarse(f, width, base=0):
    quarter = width // 4
    return [(2 * f + h, base + width // 2, quarter) for h in range(2)]


def put(buf, pieces, line):
    at = 0
    for row, lane, lanes in pieces:
        buf[row : row + 1, lane : lane + lanes] = line[:, at : at + lanes]
        at += lanes


def take(buf, pieces):
    parts = [buf[row : row + 1, lane : lane + lanes] for row, lane, lanes in pieces]
    return parts[0] if len(parts) == 1 else jnp.concatenate(parts, axis=1)


def spread(line, rows=ROWS):
    return jnp.broadcast_to(line, (rows, line.shape[1]))


def edge_line(tile, top_half, base=0, rows=ROWS):
    return jnp.where(top_half, tile[base + rows - 1 : base + rows], tile[base : base + 1])


def pack(odd, top_half, fine, coarse, stiff, coarse_stiff, a_buf, b_buf, y_buf, db_buf, width):
    half = width // 2
    quarter = width // 4
    with_k = stiff is not None
    fields = 7 if with_k else 6
    zero = jnp.zeros((2, half), F32)
    upper = iota((ROWS, half), 0) < 4

    def tile(f, z):
        return fine(f, z) if f < 6 else stiff(z)

    base = 3 * width + (half if with_k else 0)
    tail = base + 2 * half
    for f in range(fields):
        for z in range(PLANES):
            t = tile(f, z)
            line = edge_line(t, top_half)
            put(y_buf, fine_row(f * PLANES + z, width), line)
            if z == 0:
                low, low_line = t, line
        a_buf[:, f * width : (f + 1) * width] = jnp.where(odd, low, t)
        b_buf[:, f * width : (f + 1) * width] = jnp.where(odd, t, low)
        g = f if f < 3 else (3 if f == 6 else None)
        if g is not None:
            put(db_buf, corner_fine(g, width), jnp.where(odd, line, low_line))
            put(y_buf, corner_fine(g, width, tail), jnp.where(odd, low_line, line))

    for f in range(fields):
        t = coarse(f) if f < 6 else coarse_stiff
        lines = [edge_line(t, top_half, 4 * zc, 4) for zc in range(2)]
        for zc in range(2):
            put(y_buf, coarse_row(2 * f + zc, width, base), lines[zc])
        g = f if f < 3 else (3 if f == 6 else None)
        if g is not None:
            put(db_buf, corner_coarse(g, width), jnp.where(odd, lines[1], lines[0]))
            put(y_buf, corner_coarse(g, width, tail), jnp.where(odd, lines[0], lines[1]))
    db_buf[:, half + quarter :] = jnp.zeros((ROWS, db_buf.shape[1] - half - quarter), F32)
    if with_k:
        y_buf[6:8, base + half : base + 2 * half] = zero
    else:
        y_buf[4:8, base + half : base + 2 * half] = jnp.zeros((4, half), F32)
        y_buf[6:8, tail:] = jnp.zeros((2, half + quarter), F32)
        db_buf[6:8, :] = jnp.zeros((2, db_buf.shape[1]), F32)

    at = fields * width
    for c in range(FIELDS):
        first, second = coarse(c), coarse(c + 3)
        low = jnp.where(upper, first, roll(second, 4, 0))
        high = jnp.where(upper, roll(first, 4, 0), second)
        a_buf[:, at : at + half] = jnp.where(odd, low, high)
        b_buf[:, at : at + half] = jnp.where(odd, high, low)
        at += half
    if with_k:
        some = iota((ROWS, quarter), 0) < 4
        low, high = coarse_stiff, roll(coarse_stiff, 4, 0)
        low = jnp.where(some, low[:, :quarter], roll(low[:, quarter:], 4, 0))
        high = jnp.where(some, high[:, :quarter], roll(high[:, quarter:], 4, 0))
        a_buf[:, at : at + quarter] = jnp.where(odd, low, high)
        b_buf[:, at : at + quarter] = jnp.where(odd, high, low)


def begin_kernel(
    mask_hbm, drive_hbm, comp_hbm, stiff_hbm, now_hbm, before_hbm,
    y_buf, b_buf, db_buf, a_buf, now, stiff, coef, force, w_out, cu_out, cw_out, ck_out, cf_out,
    mask, drive, comp, before, group, wide, sems,
):
    pairs = (
        (drive_hbm, drive), (mask_hbm, mask), (comp_hbm, comp), (stiff_hbm, stiff),
        (now_hbm, now), (before_hbm, before),
    )
    copies = [pltpu.make_async_copy(src, dst, sems.at[n]) for n, (src, dst) in enumerate(pairs)]
    for copy in copies:
        copy.start()
    odd, top_half, _, _ = place()
    width = stiff.shape[2]
    half = width // 2
    row = iota((ROWS, width), 0)
    even_row = lax.rem(row, 2) == 0

    for copy in copies[:3]:
        copy.wait()
    on = [mask[z].astype(F32) for z in range(PLANES)]
    for c in range(FIELDS):
        group[c] = group_drive(comp[...], drive, c)
    for c in range(FIELDS):
        for z in range(PLANES):
            force[c, z] = group[c] * (TIME_SQUARE * on[z])
    copies[3].wait()
    fine_coefs(stiff, top_half, coef)
    for copy in copies[4:]:
        copy.wait()

    def pooled(first, second):
        first = first + roll(first, -1, 0)
        second = second + roll(second, -1, 0)
        return jnp.where(even_row, first, roll(second, 1, 0))

    tiles = []
    for c in range(FIELDS):
        tiles.append(pooled(now[c, 0] + now[c, 1], now[c, 2] + now[c, 3]))
    for c in range(FIELDS):
        tiles.append(pooled(before[c, 0] + before[c, 1], before[c, 2] + before[c, 3]))
    tiles.append(pooled(stiff[0] + stiff[1], stiff[2] + stiff[3]))
    for c in range(FIELDS):
        tiles.append(pooled(group[c], group[c]))
    stacked = jnp.concatenate(tiles, axis=0)
    pool = jnp.where(iota((256, 128), 0) // 2 == iota((256, 128), 1), 0.125, 0.0)
    for q in range(width // 256):
        wide[q] = lax.dot_general(
            stacked[:, q * 256 : (q + 1) * 256], pool, (((1,), (0,)), ((), ())),
            precision=lax.Precision.HIGHEST, preferred_element_type=F32,
        )

    def coarse_tile(f):
        planes = [
            jnp.concatenate([wide[q, pl.ds(8 * f + zc, 4, stride=2), :] for q in range(half // 128)], axis=1)
            for zc in range(2)
        ]
        return jnp.concatenate(planes, axis=0)

    upper = iota((ROWS, half), 0) < 4
    weight = jnp.where(upper, on[0] + on[1], on[2] + on[3]) * TIME_SQUARE
    ck_out[...] = coarse_tile(6)
    coefs = coarse_coefs(ck_out[...], top_half)
    for c in range(FIELDS):
        cu_out[c] = coarse_tile(c)
        cf_out[c] = coarse_tile(7 + c) * weight
        cw_out[c] = coarse_free(cu_out[c], coarse_tile(3 + c), coefs, cf_out[c])

    for c in range(FIELDS):
        for z in range(PLANES):
            w_out[c, z] = fine_free(now, before[c, z], c, z, coef, force[c, z])
    pack(
        odd, top_half,
        lambda f, z: now[f, z] if f < 3 else w_out[f - 3, z],
        lambda f: cu_out[f] if f < 3 else cw_out[f - 3],
        lambda z: stiff[z], ck_out[...],
        a_buf, b_buf, y_buf, db_buf, width,
    )


class Halo:
    def __init__(self, bufs, with_k, odd, width):
        self.y, self.b, self.db, self.a, self.ya = bufs
        self.odd, self.width, self.with_k = odd, width, with_k
        self.fields = 7 if with_k else 6
        self.base = 3 * width + (width // 2 if with_k else 0)

    def low(self, at, lanes):
        return jnp.where(self.odd, self.a[:, at : at + lanes], self.b[:, at : at + lanes])

    def high(self, at, lanes):
        return jnp.where(self.odd, self.b[:, at : at + lanes], self.a[:, at : at + lanes])

    def plane_low(self, f):
        return self.low(f * self.width, self.width)

    def plane_high(self, f):
        return self.high(f * self.width, self.width)

    def rows(self, f, z):
        return spread(take(self.y, fine_row(f * PLANES + z, self.width)))

    def corners(self, f):
        pieces = corner_fine(3 if f == 6 else f, self.width)
        near, far = take(self.ya, pieces), take(self.db, pieces)
        low, high = jnp.where(self.odd, near, far), jnp.where(self.odd, far, near)
        return spread(low), spread(high)

    def coarse_rows(self, f, upper, buf=None):
        buf = self.y if buf is None else buf
        lines = [take(buf, coarse_row(2 * f + zc, self.width, self.base)) for zc in range(2)]
        return jnp.where(upper, spread(lines[0]), spread(lines[1]))

    def coarse_corner(self, f, upper):
        pieces = corner_coarse(3 if f == 6 else f, self.width)
        near, far = take(self.ya, pieces), take(self.db, pieces)
        low, high = jnp.where(self.odd, near, far), jnp.where(self.odd, far, near)
        return jnp.where(upper, spread(low), spread(high))

    def coarse_planes(self, c, upper):
        half = self.width // 2
        at = self.fields * self.width + c * half
        low, high = self.low(at, half), self.high(at, half)
        return (
            jnp.where(upper, low, roll(high, 4, 0)),
            jnp.where(upper, roll(low, 4, 0), high),
        )

    def coarse_stiff_planes(self, upper):
        at = self.fields * self.width + 3 * (self.width // 2)
        low, high = self.low(at, self.width // 4), self.high(at, self.width // 4)
        return jnp.where(
            upper,
            jnp.concatenate([low, roll(low, 4, 0)], axis=1),
            jnp.concatenate([roll(high, 4, 0), high], axis=1),
        )


def faces(got, stiff, ck, halo, coarse_halo, top_half, has_low, has_high):
    shape = stiff.shape[1:]
    half = shape[1] // 2
    edge_row = iota(shape, 0) == jnp.where(top_half, ROWS - 1, 0)
    for z in range(PLANES):
        halo[z] = jnp.where(edge_row, FINE_FACE * (stiff[z] + got.rows(6, z)), 0.0)
    k_low, k_high = got.plane_low(6), got.plane_high(6)
    kd_low, kd_high = got.corners(6)
    halo[4] = FINE_FACE * (stiff[0] + k_low)
    halo[5] = FINE_FACE * (stiff[PLANES - 1] + k_high)
    halo[6] = jnp.where(edge_row, FINE_FACE * (k_low + kd_low), 0.0)
    halo[7] = jnp.where(edge_row, FINE_FACE * (k_high + kd_high), 0.0)
    halo[8] = FINE_FACE * (got.rows(6, 0) + kd_low)
    halo[9] = FINE_FACE * (got.rows(6, PLANES - 1) + kd_high)

    row = iota((ROWS, half), 0)
    upper = row < 4
    edge = lax.rem(row, 4) == jnp.where(top_half, 3, 0)
    k = ck[...]
    kz, ky, kd = got.coarse_stiff_planes(upper), got.coarse_rows(6, upper), got.coarse_corner(6, upper)
    coarse_halo[0] = COARSE_FACE * (k + kz)
    coarse_halo[1] = jnp.where(edge, COARSE_FACE * (k + ky), 0.0)
    coarse_halo[2] = jnp.where(edge, COARSE_FACE * (kz + kd), 0.0)
    coarse_halo[3] = COARSE_FACE * (ky + kd)
    coarse_halo[4] = jnp.where(upper, jnp.where(has_low, 1.0, 0.0), jnp.where(has_high, 1.0, 0.0))


def join(
    got, coef, halo, coarse_halo, force, now, free, cu_now, cu_free, ck, cf,
    mid, mid_y, mid_low, mid_high, coarse_mid, emit, emit_coarse, top_half, has_low, has_high,
):
    for c in range(FIELDS):
        d_low, d_high = got.corners(c)
        for z in range(PLANES):
            u = now[c, z]
            u_y = got.rows(c, z)
            flux = halo[z] * (u_y - u)
            new = free[c, z] + flux
            new_y = got.rows(3 + c, z) - flux
            if z == 0:
                other = got.plane_low(c)
                flux = halo[4] * (other - u)
                new = new + flux
                out = got.plane_low(3 + c) - flux + halo[6] * (d_low - other)
                mid_low[c] = jnp.where(has_low, out, 0.0)
                new_y = new_y + halo[8] * (d_low - u_y)
            if z == PLANES - 1:
                other = got.plane_high(c)
                flux = halo[5] * (other - u)
                new = new + flux
                out = got.plane_high(3 + c) - flux + halo[7] * (d_high - other)
                mid_high[c] = jnp.where(has_high, out, 0.0)
                new_y = new_y + halo[9] * (d_high - u_y)
            mid[c, z] = new
            mid_y[c, z] = new_y

        for z in range(PLANES):
            u = mid[c, z]
            new = fine_free(mid, now[c, z], c, z, coef, force[c, z])
            new = new + halo[z] * (mid_y[c, z] - u)
            if z == 0:
                new = new + halo[4] * (mid_low[c] - u)
            if z == PLANES - 1:
                new = new + halo[5] * (mid_high[c] - u)
            emit(c, z, new)

    upper = iota(cf.shape[1:], 0) < 4
    face_z, face_y, face_zd, face_yd, inside = [coarse_halo[n] for n in range(5)]
    coefs = coarse_coefs(ck[...], top_half)
    for c in range(FIELDS):
        u = cu_now[c]
        u_z, w_z = got.coarse_planes(c, upper)
        u_y = got.coarse_rows(c, upper)
        u_d = got.coarse_corner(c, upper)
        flux_z = face_z * (u_z - u)
        flux_y = face_y * (u_y - u)
        new = cu_free[c] + flux_z + flux_y
        new_z = inside * (w_z - flux_z + face_zd * (u_d - u_z))
        new_y = got.coarse_rows(3 + c, upper) - flux_y + face_yd * (u_d - u_y)
        coarse_mid[c] = new
        after = coarse_free(new, u, coefs, cf[c])
        emit_coarse(c, after + face_z * (new_z - new) + face_y * (new_y - new))
    return coefs


def middle_kernel(
    y_one, b_one, db_one, a_one, ya_one, coef, force, stiff, now, free, cu_now, cu_free, ck, cf,
    y_buf, b_buf, db_buf, a_buf, halo, coarse_halo, u_out, w_out, cu_out, cw_out,
    mid, mid_y, mid_low, mid_high, coarse_mid,
):
    odd, top_half, has_low, has_high = place()
    got = Halo((y_one, b_one, db_one, a_one, ya_one), True, odd, stiff.shape[2])
    faces(got, stiff, ck, halo, coarse_halo, top_half, has_low, has_high)

    def emit(c, z, value):
        u_out[c, z] = value

    def emit_coarse(c, value):
        cu_out[c] = value

    coefs = join(
        got, coef, halo, coarse_halo, force, now, free, cu_now, cu_free, ck, cf,
        mid, mid_y, mid_low, mid_high, coarse_mid, emit, emit_coarse, top_half, has_low, has_high,
    )
    for c in range(FIELDS):
        cw_out[c] = coarse_free(cu_out[c], coarse_mid[c], coefs, cf[c])
        for z in range(PLANES):
            w_out[c, z] = fine_free(u_out, mid[c, z], c, z, coef, force[c, z])
    pack(
        odd, top_half,
        lambda f, z: u_out[f, z] if f < 3 else w_out[f - 3, z],
        lambda f: cu_out[f] if f < 3 else cw_out[f - 3],
        None, None, a_buf, b_buf, y_buf, db_buf, stiff.shape[2],
    )


def end_kernel(
    y_two, b_two, db_two, a_two, ya_two, coef, force, halo, coarse_halo, now, free, cu_now, cu_free, ck, cf,
    u_hbm, cu_hbm,
    mid, mid_y, mid_low, mid_high, coarse_mid, last, coarse_last, sems,
):
    odd, top_half, has_low, has_high = place()
    got = Halo((y_two, b_two, db_two, a_two, ya_two), False, odd, coef.shape[3])
    copies = []

    def emit(c, z, value):
        last[c, z] = value
        if z == PLANES - 1:
            copies.append(pltpu.make_async_copy(last.at[c], u_hbm.at[c], sems.at[c]))
            copies[-1].start()

    def emit_coarse(c, value):
        for zc in range(2):
            coarse_last[c, zc] = value[4 * zc : 4 * zc + 4]

    join(
        got, coef, halo, coarse_halo, force, now, free, cu_now, cu_free, ck, cf,
        mid, mid_y, mid_low, mid_high, coarse_mid, emit, emit_coarse, top_half, has_low, has_high,
    )
    copies.append(pltpu.make_async_copy(coarse_last, cu_hbm, sems.at[FIELDS]))
    copies[-1].start()
    for copy in copies:
        copy.wait()


def struct(*shape):
    return jax.ShapeDtypeStruct(shape, F32)


def call(kernel, name, outs, scratch, operands, in_space=pltpu.VMEM, out_space=pltpu.VMEM, vmem=32):
    return pl.pallas_call(
        kernel,
        name=name,
        out_shape=outs,
        in_specs=[pl.BlockSpec(memory_space=in_space)] * len(operands),
        out_specs=[pl.BlockSpec(memory_space=out_space)] * len(outs),
        scratch_shapes=scratch,
        compiler_params=pltpu.CompilerParams(vmem_limit_bytes=vmem * 1024 * 1024),
    )(*operands)


def exchange(bufs, corner):
    count = lax.axis_size("ax")
    pair_a = [(i, i ^ 1) for i in range(count)]
    pair_b = [(i, i + 1 if i % 2 else i - 1) for i in range(1, count - 1)]
    across = [(2 * i + s, 2 * j + 1 - s) for i, j in pair_b for s in (0, 1)]
    y, b, db, a = bufs
    y = lax.ppermute(y, "xs", [(0, 1), (1, 0)])
    b = lax.ppermute(b, "ax", pair_b)
    db = lax.ppermute(db, ("ax", "xs"), across)
    a = lax.ppermute(a, "ax", pair_a)
    ya = lax.ppermute(y[:, y.shape[1] - corner :], "ax", pair_a)
    return y, b, db, a, ya


def local(displacement, previous, stiffness, tissue_mask, compartment, drive):
    width = displacement.shape[3]
    half = width // 2
    quarter = width // 4
    field = struct(FIELDS, PLANES, ROWS, width)
    coarse = struct(FIELDS, ROWS, half)

    def buffers(fields, with_k):
        plane = fields * width + 3 * half + (quarter if with_k else 0)
        rows = 3 * width + (3 * half if with_k else 2 * half) + half + quarter
        return [struct(ROWS, rows), struct(ROWS, plane), struct(ROWS, half + quarter + PAD), struct(ROWS, plane)]

    whole = pltpu.VMEM(field.shape, F32)
    tile = pltpu.VMEM((FIELDS, ROWS, width), F32)
    small = pltpu.VMEM(coarse.shape, F32)
    y, b, db, a, now, stiff, coef, force, w, cu, cw, ck, cf = call(
        begin_kernel,
        "restrict_and_first_step",
        buffers(7, True)
        + [field, struct(*stiffness.shape), struct(6, PLANES, ROWS, width), field, field]
        + [coarse, coarse, struct(ROWS, half), coarse],
        [
            pltpu.SMEM(tissue_mask.shape, jnp.int32),
            pltpu.SMEM(drive.shape, F32),
            pltpu.VMEM(compartment.shape, jnp.int32),
            whole,
            tile,
            pltpu.VMEM((half // 128, 10 * ROWS, 128), F32),
            pltpu.SemaphoreType.DMA((6,)),
        ],
        [
            pltpu.with_memory_space_constraint(x, pltpu.HBM)
            for x in (tissue_mask, drive, compartment, stiffness, displacement, previous)
        ],
        in_space=pltpu.HBM,
    )
    one = exchange((y, b, db, a), half + quarter)
    steps = [whole, whole, tile, tile, small]
    y, b, db, a, halo, coarse_halo, u, w, cu, cw = call(
        middle_kernel,
        "two_steps",
        buffers(6, False)
        + [struct(10, ROWS, width), struct(5, ROWS, half), field, field, coarse, coarse],
        steps,
        one + (coef, force, stiff, now, w, cu, cw, ck, cf),
    )
    two = exchange((y, b, db, a), half + quarter)
    return call(
        end_kernel,
        "last_steps",
        [field, struct(FIELDS, 2, 4, half)],
        steps + [whole, pltpu.VMEM((FIELDS, 2, 4, half), F32), pltpu.SemaphoreType.DMA((FIELDS + 1,))],
        two + (coef, force, halo, coarse_halo, u, w, cu, cw, ck, cf),
        out_space=pltpu.HBM,
    )


def solution(mesh):
    placed = (
        P(None, "ax", "xs", None),
        P(None, "ax", "xs", None),
        P("ax", "xs", None),
        P("ax"),
        P("xs", None),
        P(),
    )

    def run(*args):
        return tuple(local(*args))

    return jax.shard_map(
        run,
        mesh=mesh,
        in_specs=placed,
        out_specs=(P(None, "ax", "xs", None), P(None, "ax", "xs", None)),
        check_vma=False,
    )
```

```python
import functools

import jax
import jax.numpy as jnp
from jax import lax
from jax.experimental import pallas as pl
from jax.experimental.pallas import tpu as pltpu
from jax.sharding import PartitionSpec as P

TIME_SQUARE = 0.12
FINE_FACE = 0.5 * TIME_SQUARE
COARSE_FACE = 0.25 * 0.5 * TIME_SQUARE
PLANES = 4
ROWS = 8
FIELDS = 3
F32 = jnp.float32


def roll(x, shift, axis):
    return pltpu.roll(x, shift % x.shape[axis], axis)


def place():
    i = lax.axis_index("ax")
    s = lax.axis_index("xs")
    return (lax.rem(i, 2) == 1), (s == 0), (i > 0), (i < lax.axis_size("ax") - 1)


def iota(shape, dim):
    return lax.broadcasted_iota(jnp.int32, shape, dim)


def stiff_coefs(k, face, low_y, high_y, outer_row):
    width = k.shape[1]
    lane = iota(k.shape, 1)
    last = lane == width - 1
    start = lane == 0
    kp = jnp.where(last, 0.0, roll(k, -1, 1))
    km = jnp.where(start, 0.0, roll(k, 1, 1))
    full_p = face * (k + kp)
    full_m = face * (k + km)
    cyp = jnp.where(high_y, face * (k + roll(k, -1, 0)), 0.0)
    cym = jnp.where(low_y, face * (k + roll(k, 1, 0)), 0.0)
    edge = jnp.where(outer_row, face * k, 0.0)
    centre = 2.0 - (full_p + full_m + cyp + cym + edge)
    return jnp.where(last, 0.0, full_p), jnp.where(start, 0.0, full_m), cyp, cym, centre


def fine_coefs(k_ref, first, coef):
    shape = k_ref.shape[1:]
    row = iota(shape, 0)
    for z in range(PLANES - 1):
        coef[5, z] = FINE_FACE * (k_ref[z] + k_ref[z + 1])
    for z in range(PLANES):
        cxp, cxm, cyp, cym, centre = stiff_coefs(
            k_ref[z], FINE_FACE, row > 0, row < ROWS - 1, row == jnp.where(first, 0, ROWS - 1)
        )
        if z > 0:
            centre = centre - coef[5, z - 1]
        if z < PLANES - 1:
            centre = centre - coef[5, z]
        coef[0, z] = cxp
        coef[1, z] = cxm
        coef[2, z] = cyp
        coef[3, z] = cym
        coef[4, z] = centre


def fine_free(u_ref, before, c, z, coef, drive_term):
    u = u_ref[c, z]
    acc = coef[4, z] * u - before
    acc = acc + coef[0, z] * roll(u, -1, 1) + coef[1, z] * roll(u, 1, 1)
    acc = acc + coef[2, z] * roll(u, -1, 0) + coef[3, z] * roll(u, 1, 0)
    if z > 0:
        acc = acc + coef[5, z - 1] * u_ref[c, z - 1]
    if z < PLANES - 1:
        acc = acc + coef[5, z] * u_ref[c, z + 1]
    return acc + drive_term


def coarse_coefs(k, first):
    row = iota(k.shape, 0)
    inner = lax.rem(row, 4)
    cxp, cxm, cyp, cym, centre = stiff_coefs(
        k, COARSE_FACE, inner > 0, inner < 3, inner == jnp.where(first, 0, 3)
    )
    cz = COARSE_FACE * (k + roll(k, 4, 0))
    return cxp, cxm, cyp, cym, centre - cz, cz


def coarse_free(u, before, coefs, force):
    cxp, cxm, cyp, cym, centre, cz = coefs
    return (
        centre * u
        - before
        + cxp * roll(u, -1, 1)
        + cxm * roll(u, 1, 1)
        + cyp * roll(u, -1, 0)
        + cym * roll(u, 1, 0)
        + cz * roll(u, 4, 0)
        + force
    )


def group_drive(compartment, drive_ref, c):
    value = jnp.full(compartment.shape, drive_ref[c, 0], F32)
    for g in range(1, drive_ref.shape[1]):
        value = jnp.where(compartment == g, drive_ref[c, g], value)
    return value


def fine_row(r, width):
    if r < 24:
        return [(r % 8, (r // 8) * width, width)]
    half = width // 2
    return [(2 * (r - 24) + h, 3 * width, half) for h in range(2)]


def coarse_row(q, width, base):
    half = width // 2
    return [(q % 8, base + (q // 8) * half, half)]


def corner_fine(f, width):
    half = width // 2
    return [(2 * f + h, 0, half) for h in range(2)]


def corner_coarse(f, width):
    quarter = width // 4
    return [(2 * f + h, width // 2, quarter) for h in range(2)]


def put(buf, pieces, line):
    at = 0
    for row, lane, lanes in pieces:
        buf[row : row + 1, lane : lane + lanes] = line[:, at : at + lanes]
        at += lanes


def take(buf, pieces):
    parts = [buf[row : row + 1, lane : lane + lanes] for row, lane, lanes in pieces]
    return parts[0] if len(parts) == 1 else jnp.concatenate(parts, axis=1)


def spread(line, rows=ROWS):
    return jnp.broadcast_to(line, (rows, line.shape[1]))


def edge_line(tile, top_half, base=0, rows=ROWS):
    return jnp.where(top_half, tile[base + rows - 1 : base + rows], tile[base : base + 1])


def pack(odd, top_half, fine, coarse, stiff, coarse_stiff, a_buf, b_buf, y_buf, db_buf, width):
    half = width // 2
    quarter = width // 4
    with_k = stiff is not None
    fields = 7 if with_k else 6
    zero = jnp.zeros((2, half), F32)
    upper = iota((ROWS, half), 0) < 4

    def tile(f, z):
        return fine(f, z) if f < 6 else stiff(z)

    base = 3 * width + (half if with_k else 0)
    for f in range(fields):
        for z in range(PLANES):
            t = tile(f, z)
            line = edge_line(t, top_half)
            put(y_buf, fine_row(f * PLANES + z, width), line)
            if z == 0:
                low, low_line = t, line
        a_buf[:, f * width : (f + 1) * width] = jnp.where(odd, low, t)
        b_buf[:, f * width : (f + 1) * width] = jnp.where(odd, t, low)
        g = f if f < 3 else (3 if f == 6 else None)
        if g is not None:
            put(db_buf, corner_fine(g, width), jnp.where(odd, line, low_line))

    for f in range(fields):
        t = coarse(f) if f < 6 else coarse_stiff
        lines = [edge_line(t, top_half, 4 * zc, 4) for zc in range(2)]
        for zc in range(2):
            put(y_buf, coarse_row(2 * f + zc, width, base), lines[zc])
        g = f if f < 3 else (3 if f == 6 else None)
        if g is not None:
            put(db_buf, corner_coarse(g, width), jnp.where(odd, lines[1], lines[0]))
    if with_k:
        y_buf[6:8, base + half : base + 2 * half] = zero
    else:
        y_buf[4:8, base + half : base + 2 * half] = jnp.zeros((4, half), F32)
        db_buf[6:8, :] = jnp.zeros((2, db_buf.shape[1]), F32)

    at = fields * width
    for c in range(FIELDS):
        first, second = coarse(c), coarse(c + 3)
        low = jnp.where(upper, first, roll(second, 4, 0))
        high = jnp.where(upper, roll(first, 4, 0), second)
        a_buf[:, at : at + half] = jnp.where(odd, low, high)
        b_buf[:, at : at + half] = jnp.where(odd, high, low)
        at += half
    if with_k:
        some = iota((ROWS, quarter), 0) < 4
        low, high = coarse_stiff, roll(coarse_stiff, 4, 0)
        low = jnp.where(some, low[:, :quarter], roll(low[:, quarter:], 4, 0))
        high = jnp.where(some, high[:, :quarter], roll(high[:, quarter:], 4, 0))
        a_buf[:, at : at + quarter] = jnp.where(odd, low, high)
        b_buf[:, at : at + quarter] = jnp.where(odd, high, low)


def begin_kernel(
    mask_hbm, drive_hbm, comp_hbm, stiff_hbm, now_hbm, before_hbm,
    y_buf, b_buf, db_buf, a_buf, now, stiff, coef, force, w_out, cu_out, cw_out, ck_out, cf_out,
    mask, drive, comp, before, group, wide, sems,
):
    pairs = (
        (drive_hbm, drive), (mask_hbm, mask), (comp_hbm, comp), (stiff_hbm, stiff),
        (now_hbm, now), (before_hbm, before),
    )
    copies = [pltpu.make_async_copy(src, dst, sems.at[n]) for n, (src, dst) in enumerate(pairs)]
    for copy in copies:
        copy.start()
    odd, top_half, _, _ = place()
    width = stiff.shape[2]
    half = width // 2
    row = iota((ROWS, width), 0)
    even_row = lax.rem(row, 2) == 0

    for copy in copies[:3]:
        copy.wait()
    on = [mask[z].astype(F32) for z in range(PLANES)]
    for c in range(FIELDS):
        group[c] = group_drive(comp[...], drive, c)
    for c in range(FIELDS):
        for z in range(PLANES):
            force[c, z] = group[c] * (TIME_SQUARE * on[z])
    copies[3].wait()
    fine_coefs(stiff, top_half, coef)
    for copy in copies[4:]:
        copy.wait()

    def pooled(first, second):
        first = first + roll(first, -1, 0)
        second = second + roll(second, -1, 0)
        return jnp.where(even_row, first, roll(second, 1, 0))

    tiles = []
    for c in range(FIELDS):
        tiles.append(pooled(now[c, 0] + now[c, 1], now[c, 2] + now[c, 3]))
    for c in range(FIELDS):
        tiles.append(pooled(before[c, 0] + before[c, 1], before[c, 2] + before[c, 3]))
    tiles.append(pooled(stiff[0] + stiff[1], stiff[2] + stiff[3]))
    for c in range(FIELDS):
        tiles.append(pooled(group[c], group[c]))
    stacked = jnp.concatenate(tiles, axis=0)
    pool = jnp.where(iota((256, 128), 0) // 2 == iota((256, 128), 1), 0.125, 0.0)
    for q in range(width // 256):
        wide[q] = lax.dot_general(
            stacked[:, q * 256 : (q + 1) * 256], pool, (((1,), (0,)), ((), ())),
            precision=lax.Precision.HIGHEST, preferred_element_type=F32,
        )

    def coarse_tile(f):
        planes = [
            jnp.concatenate([wide[q, pl.ds(8 * f + zc, 4, stride=2), :] for q in range(half // 128)], axis=1)
            for zc in range(2)
        ]
        return jnp.concatenate(planes, axis=0)

    upper = iota((ROWS, half), 0) < 4
    weight = jnp.where(upper, on[0] + on[1], on[2] + on[3]) * TIME_SQUARE
    ck_out[...] = coarse_tile(6)
    coefs = coarse_coefs(ck_out[...], top_half)
    for c in range(FIELDS):
        cu_out[c] = coarse_tile(c)
        cf_out[c] = coarse_tile(7 + c) * weight
        cw_out[c] = coarse_free(cu_out[c], coarse_tile(3 + c), coefs, cf_out[c])

    for c in range(FIELDS):
        for z in range(PLANES):
            w_out[c, z] = fine_free(now, before[c, z], c, z, coef, force[c, z])
    pack(
        odd, top_half,
        lambda f, z: now[f, z] if f < 3 else w_out[f - 3, z],
        lambda f: cu_out[f] if f < 3 else cw_out[f - 3],
        lambda z: stiff[z], ck_out[...],
        a_buf, b_buf, y_buf, db_buf, width,
    )


class Halo:
    def __init__(self, bufs, with_k, odd, width):
        self.y, self.b, self.db, self.a, self.ya = bufs
        self.odd, self.width, self.with_k = odd, width, with_k
        self.fields = 7 if with_k else 6
        self.base = 3 * width + (width // 2 if with_k else 0)

    def low(self, at, lanes):
        return jnp.where(self.odd, self.a[:, at : at + lanes], self.b[:, at : at + lanes])

    def high(self, at, lanes):
        return jnp.where(self.odd, self.b[:, at : at + lanes], self.a[:, at : at + lanes])

    def plane_low(self, f):
        return self.low(f * self.width, self.width)

    def plane_high(self, f):
        return self.high(f * self.width, self.width)

    def rows(self, f, z):
        return spread(take(self.y, fine_row(f * PLANES + z, self.width)))

    def corners(self, f):
        pieces = corner_fine(3 if f == 6 else f, self.width)
        near, far = take(self.ya, pieces), take(self.db, pieces)
        low, high = jnp.where(self.odd, near, far), jnp.where(self.odd, far, near)
        return spread(low), spread(high)

    def coarse_rows(self, f, upper, buf=None):
        buf = self.y if buf is None else buf
        lines = [take(buf, coarse_row(2 * f + zc, self.width, self.base)) for zc in range(2)]
        return jnp.where(upper, spread(lines[0]), spread(lines[1]))

    def coarse_corner(self, f, upper):
        pieces = corner_coarse(3 if f == 6 else f, self.width)
        near, far = take(self.ya, pieces), take(self.db, pieces)
        low, high = jnp.where(self.odd, near, far), jnp.where(self.odd, far, near)
        return jnp.where(upper, spread(low), spread(high))

    def coarse_planes(self, c, upper):
        half = self.width // 2
        at = self.fields * self.width + c * half
        low, high = self.low(at, half), self.high(at, half)
        return (
            jnp.where(upper, low, roll(high, 4, 0)),
            jnp.where(upper, roll(low, 4, 0), high),
        )

    def coarse_stiff_planes(self, upper):
        at = self.fields * self.width + 3 * (self.width // 2)
        low, high = self.low(at, self.width // 4), self.high(at, self.width // 4)
        return jnp.where(
            upper,
            jnp.concatenate([low, roll(low, 4, 0)], axis=1),
            jnp.concatenate([roll(high, 4, 0), high], axis=1),
        )


def faces(got, stiff, ck, halo, coarse_halo, top_half, has_low, has_high):
    shape = stiff.shape[1:]
    half = shape[1] // 2
    edge_row = iota(shape, 0) == jnp.where(top_half, ROWS - 1, 0)
    for z in range(PLANES):
        halo[z] = jnp.where(edge_row, FINE_FACE * (stiff[z] + got.rows(6, z)), 0.0)
    k_low, k_high = got.plane_low(6), got.plane_high(6)
    kd_low, kd_high = got.corners(6)
    halo[4] = FINE_FACE * (stiff[0] + k_low)
    halo[5] = FINE_FACE * (stiff[PLANES - 1] + k_high)
    halo[6] = jnp.where(edge_row, FINE_FACE * (k_low + kd_low), 0.0)
    halo[7] = jnp.where(edge_row, FINE_FACE * (k_high + kd_high), 0.0)
    halo[8] = FINE_FACE * (got.rows(6, 0) + kd_low)
    halo[9] = FINE_FACE * (got.rows(6, PLANES - 1) + kd_high)

    row = iota((ROWS, half), 0)
    upper = row < 4
    edge = lax.rem(row, 4) == jnp.where(top_half, 3, 0)
    k = ck[...]
    kz, ky, kd = got.coarse_stiff_planes(upper), got.coarse_rows(6, upper), got.coarse_corner(6, upper)
    coarse_halo[0] = COARSE_FACE * (k + kz)
    coarse_halo[1] = jnp.where(edge, COARSE_FACE * (k + ky), 0.0)
    coarse_halo[2] = jnp.where(edge, COARSE_FACE * (kz + kd), 0.0)
    coarse_halo[3] = COARSE_FACE * (ky + kd)
    coarse_halo[4] = jnp.where(upper, jnp.where(has_low, 1.0, 0.0), jnp.where(has_high, 1.0, 0.0))


def join(
    got, coef, halo, coarse_halo, force, now, free, cu_now, cu_free, ck, cf,
    mid, mid_y, mid_low, mid_high, coarse_mid, emit, emit_coarse, top_half, has_low, has_high,
):
    for c in range(FIELDS):
        d_low, d_high = got.corners(c)
        for z in range(PLANES):
            u = now[c, z]
            u_y = got.rows(c, z)
            flux = halo[z] * (u_y - u)
            new = free[c, z] + flux
            new_y = got.rows(3 + c, z) - flux
            if z == 0:
                other = got.plane_low(c)
                flux = halo[4] * (other - u)
                new = new + flux
                out = got.plane_low(3 + c) - flux + halo[6] * (d_low - other)
                mid_low[c] = jnp.where(has_low, out, 0.0)
                new_y = new_y + halo[8] * (d_low - u_y)
            if z == PLANES - 1:
                other = got.plane_high(c)
                flux = halo[5] * (other - u)
                new = new + flux
                out = got.plane_high(3 + c) - flux + halo[7] * (d_high - other)
                mid_high[c] = jnp.where(has_high, out, 0.0)
                new_y = new_y + halo[9] * (d_high - u_y)
            mid[c, z] = new
            mid_y[c, z] = new_y

        for z in range(PLANES):
            u = mid[c, z]
            new = fine_free(mid, now[c, z], c, z, coef, force[c, z])
            new = new + halo[z] * (mid_y[c, z] - u)
            if z == 0:
                new = new + halo[4] * (mid_low[c] - u)
            if z == PLANES - 1:
                new = new + halo[5] * (mid_high[c] - u)
            emit(c, z, new)

    upper = iota(cf.shape[1:], 0) < 4
    face_z, face_y, face_zd, face_yd, inside = [coarse_halo[n] for n in range(5)]
    coefs = coarse_coefs(ck[...], top_half)
    for c in range(FIELDS):
        u = cu_now[c]
        u_z, w_z = got.coarse_planes(c, upper)
        u_y = got.coarse_rows(c, upper)
        u_d = got.coarse_corner(c, upper)
        flux_z = face_z * (u_z - u)
        flux_y = face_y * (u_y - u)
        new = cu_free[c] + flux_z + flux_y
        new_z = inside * (w_z - flux_z + face_zd * (u_d - u_z))
        new_y = got.coarse_rows(3 + c, upper) - flux_y + face_yd * (u_d - u_y)
        coarse_mid[c] = new
        after = coarse_free(new, u, coefs, cf[c])
        emit_coarse(c, after + face_z * (new_z - new) + face_y * (new_y - new))
    return coefs


def middle_kernel(
    y_one, b_one, db_one, a_one, ya_one, coef, force, stiff, now, free, cu_now, cu_free, ck, cf,
    y_buf, b_buf, db_buf, a_buf, halo, coarse_halo, u_out, w_out, cu_out, cw_out,
    mid, mid_y, mid_low, mid_high, coarse_mid,
):
    odd, top_half, has_low, has_high = place()
    got = Halo((y_one, b_one, db_one, a_one, ya_one), True, odd, stiff.shape[2])
    faces(got, stiff, ck, halo, coarse_halo, top_half, has_low, has_high)

    def emit(c, z, value):
        u_out[c, z] = value

    def emit_coarse(c, value):
        cu_out[c] = value

    coefs = join(
        got, coef, halo, coarse_halo, force, now, free, cu_now, cu_free, ck, cf,
        mid, mid_y, mid_low, mid_high, coarse_mid, emit, emit_coarse, top_half, has_low, has_high,
    )
    for c in range(FIELDS):
        cw_out[c] = coarse_free(cu_out[c], coarse_mid[c], coefs, cf[c])
        for z in range(PLANES):
            w_out[c, z] = fine_free(u_out, mid[c, z], c, z, coef, force[c, z])
    pack(
        odd, top_half,
        lambda f, z: u_out[f, z] if f < 3 else w_out[f - 3, z],
        lambda f: cu_out[f] if f < 3 else cw_out[f - 3],
        None, None, a_buf, b_buf, y_buf, db_buf, stiff.shape[2],
    )


def end_kernel(
    y_two, b_two, db_two, a_two, ya_two, coef, force, halo, coarse_halo, now, free, cu_now, cu_free, ck, cf,
    u_hbm, cu_hbm,
    mid, mid_y, mid_low, mid_high, coarse_mid, last, coarse_last, sems,
):
    odd, top_half, has_low, has_high = place()
    got = Halo((y_two, b_two, db_two, a_two, ya_two), False, odd, coef.shape[3])
    copies = []

    def emit(c, z, value):
        last[c, z] = value
        if z == PLANES - 1:
            copies.append(pltpu.make_async_copy(last.at[c], u_hbm.at[c], sems.at[c]))
            copies[-1].start()

    def emit_coarse(c, value):
        for zc in range(2):
            coarse_last[c, zc] = value[4 * zc : 4 * zc + 4]

    join(
        got, coef, halo, coarse_halo, force, now, free, cu_now, cu_free, ck, cf,
        mid, mid_y, mid_low, mid_high, coarse_mid, emit, emit_coarse, top_half, has_low, has_high,
    )
    copies.append(pltpu.make_async_copy(coarse_last, cu_hbm, sems.at[FIELDS]))
    copies[-1].start()
    for copy in copies:
        copy.wait()


def struct(*shape):
    return jax.ShapeDtypeStruct(shape, F32)


def call(kernel, name, outs, scratch, operands, in_space=pltpu.VMEM, out_space=pltpu.VMEM, vmem=32):
    return pl.pallas_call(
        kernel,
        name=name,
        out_shape=outs,
        in_specs=[pl.BlockSpec(memory_space=in_space)] * len(operands),
        out_specs=[pl.BlockSpec(memory_space=out_space)] * len(outs),
        scratch_shapes=scratch,
        compiler_params=pltpu.CompilerParams(vmem_limit_bytes=vmem * 1024 * 1024),
    )(*operands)


def corner_kernel(width, with_k, y_ref, out_ref):
    odd = place()[0]
    base = 3 * width + (width // 2 if with_k else 0)
    for g in range(4 if with_k else 3):
        f = 6 if g == 3 else g
        fine = [take(y_ref, fine_row(f * PLANES + z, width)) for z in (0, PLANES - 1)]
        coarse = [take(y_ref, coarse_row(2 * f + zc, width, base)) for zc in range(2)]
        put(out_ref, corner_fine(g, width), jnp.where(odd, fine[0], fine[1]))
        put(out_ref, corner_coarse(g, width), jnp.where(odd, coarse[0], coarse[1]))
    if not with_k:
        out_ref[6:8, :] = jnp.zeros((2, out_ref.shape[1]), F32)


def corner_lines(y, width, with_k):
    vmem = pl.BlockSpec(memory_space=pltpu.VMEM)
    return pl.pallas_call(
        functools.partial(corner_kernel, width, with_k),
        name="corner_lines",
        out_shape=struct(ROWS, width // 2 + width // 4),
        in_specs=[vmem],
        out_specs=vmem,
        cost_estimate=pl.CostEstimate(flops=2_000_000_000, bytes_accessed=1024, transcendentals=0),
        compiler_params=pltpu.CompilerParams(vmem_limit_bytes=16 * 1024 * 1024),
    )(y)


def exchange(bufs, width, with_k):
    count = lax.axis_size("ax")
    pair_a = [(i, i ^ 1) for i in range(count)]
    pair_b = [(i, i + 1 if i % 2 else i - 1) for i in range(1, count - 1)]
    across = [(2 * i + s, 2 * j + 1 - s) for i, j in pair_b for s in (0, 1)]
    y, b, db, a = bufs
    y = lax.ppermute(y, "xs", [(0, 1), (1, 0)])
    b = lax.ppermute(b, "ax", pair_b)
    db = lax.ppermute(db, ("ax", "xs"), across)
    a = lax.ppermute(a, "ax", pair_a)
    ya = lax.ppermute(corner_lines(y, width, with_k), "ax", pair_a)
    return y, b, db, a, ya


def local(displacement, previous, stiffness, tissue_mask, compartment, drive):
    width = displacement.shape[3]
    half = width // 2
    quarter = width // 4
    field = struct(FIELDS, PLANES, ROWS, width)
    coarse = struct(FIELDS, ROWS, half)

    def buffers(fields, with_k):
        plane = fields * width + 3 * half + (quarter if with_k else 0)
        rows = 3 * width + (3 * half if with_k else 2 * half)
        return [struct(ROWS, rows), struct(ROWS, plane), struct(ROWS, half + quarter), struct(ROWS, plane)]

    whole = pltpu.VMEM(field.shape, F32)
    tile = pltpu.VMEM((FIELDS, ROWS, width), F32)
    small = pltpu.VMEM(coarse.shape, F32)
    y, b, db, a, now, stiff, coef, force, w, cu, cw, ck, cf = call(
        begin_kernel,
        "restrict_and_first_step",
        buffers(7, True)
        + [field, struct(*stiffness.shape), struct(6, PLANES, ROWS, width), field, field]
        + [coarse, coarse, struct(ROWS, half), coarse],
        [
            pltpu.SMEM(tissue_mask.shape, jnp.int32),
            pltpu.SMEM(drive.shape, F32),
            pltpu.VMEM(compartment.shape, jnp.int32),
            whole,
            tile,
            pltpu.VMEM((half // 128, 10 * ROWS, 128), F32),
            pltpu.SemaphoreType.DMA((6,)),
        ],
        [
            pltpu.with_memory_space_constraint(x, pltpu.HBM)
            for x in (tissue_mask, drive, compartment, stiffness, displacement, previous)
        ],
        in_space=pltpu.HBM,
    )
    one = exchange((y, b, db, a), width, True)
    steps = [whole, whole, tile, tile, small]
    y, b, db, a, halo, coarse_halo, u, w, cu, cw = call(
        middle_kernel,
        "two_steps",
        buffers(6, False)
        + [struct(10, ROWS, width), struct(5, ROWS, half), field, field, coarse, coarse],
        steps,
        one + (coef, force, stiff, now, w, cu, cw, ck, cf),
    )
    two = exchange((y, b, db, a), width, False)
    return call(
        end_kernel,
        "last_steps",
        [field, struct(FIELDS, 2, 4, half)],
        steps + [whole, pltpu.VMEM((FIELDS, 2, 4, half), F32), pltpu.SemaphoreType.DMA((FIELDS + 1,))],
        two + (coef, force, halo, coarse_halo, u, w, cu, cw, ck, cf),
        out_space=pltpu.HBM,
    )


def solution(mesh):
    placed = (
        P(None, "ax", "xs", None),
        P(None, "ax", "xs", None),
        P("ax", "xs", None),
        P("ax"),
        P("xs", None),
        P(),
    )

    def run(*args):
        return tuple(local(*args))

    return jax.shard_map(
        run,
        mesh=mesh,
        in_specs=placed,
        out_specs=(P(None, "ax", "xs", None), P(None, "ax", "xs", None)),
        check_vma=False,
    )
```

```python
import functools

import jax
import jax.numpy as jnp
from jax import lax
from jax.experimental import pallas as pl
from jax.experimental.pallas import tpu as pltpu
from jax.sharding import PartitionSpec as P

TIME_SQUARE = 0.12
FINE_FACE = 0.5 * TIME_SQUARE
COARSE_FACE = 0.25 * 0.5 * TIME_SQUARE
PLANES = 4
ROWS = 8
FIELDS = 3
F32 = jnp.float32
PAD = 128


def roll(x, shift, axis):
    return pltpu.roll(x, shift % x.shape[axis], axis)


def place():
    i = lax.axis_index("ax")
    odd = lax.rem(i, 2) == 1
    has_far = jnp.logical_and(i > 0, i < lax.axis_size("ax") - 1)

    def plane(n, count=PLANES):
        return jnp.where(odd, count - 1 - n, n)

    return lax.axis_index("xs") == 0, has_far, plane


def iota(shape, dim):
    return lax.broadcasted_iota(jnp.int32, shape, dim)


def stiff_coefs(k, face, low_y, high_y, outer_row):
    width = k.shape[1]
    lane = iota(k.shape, 1)
    last = lane == width - 1
    start = lane == 0
    kp = jnp.where(last, 0.0, roll(k, -1, 1))
    km = jnp.where(start, 0.0, roll(k, 1, 1))
    full_p = face * (k + kp)
    full_m = face * (k + km)
    cyp = jnp.where(high_y, face * (k + roll(k, -1, 0)), 0.0)
    cym = jnp.where(low_y, face * (k + roll(k, 1, 0)), 0.0)
    edge = jnp.where(outer_row, face * k, 0.0)
    centre = 2.0 - (full_p + full_m + cyp + cym + edge)
    return jnp.where(last, 0.0, full_p), jnp.where(start, 0.0, full_m), cyp, cym, centre


def fine_coefs(k_ref, first, coef):
    shape = k_ref.shape[1:]
    row = iota(shape, 0)
    for z in range(PLANES - 1):
        coef[5, z] = FINE_FACE * (k_ref[z] + k_ref[z + 1])
    for z in range(PLANES):
        cxp, cxm, cyp, cym, centre = stiff_coefs(
            k_ref[z], FINE_FACE, row > 0, row < ROWS - 1, row == jnp.where(first, 0, ROWS - 1)
        )
        if z > 0:
            centre = centre - coef[5, z - 1]
        if z < PLANES - 1:
            centre = centre - coef[5, z]
        coef[0, z] = cxp
        coef[1, z] = cxm
        coef[2, z] = cyp
        coef[3, z] = cym
        coef[4, z] = centre


def fine_free(field, before, z, coef, drive_term):
    u = field(z)
    acc = coef[4, z] * u - before
    acc = acc + coef[0, z] * roll(u, -1, 1) + coef[1, z] * roll(u, 1, 1)
    acc = acc + coef[2, z] * roll(u, -1, 0) + coef[3, z] * roll(u, 1, 0)
    if z > 0:
        acc = acc + coef[5, z - 1] * field(z - 1)
    if z < PLANES - 1:
        acc = acc + coef[5, z] * field(z + 1)
    return acc + drive_term


def coarse_coefs(k, first):
    row = iota(k.shape, 0)
    inner = lax.rem(row, 4)
    cxp, cxm, cyp, cym, centre = stiff_coefs(
        k, COARSE_FACE, inner > 0, inner < 3, inner == jnp.where(first, 0, 3)
    )
    cz = COARSE_FACE * (k + roll(k, 4, 0))
    return cxp, cxm, cyp, cym, centre - cz, cz


def coarse_free(u, before, coefs, force):
    cxp, cxm, cyp, cym, centre, cz = coefs
    return (
        centre * u
        - before
        + cxp * roll(u, -1, 1)
        + cxm * roll(u, 1, 1)
        + cyp * roll(u, -1, 0)
        + cym * roll(u, 1, 0)
        + cz * roll(u, 4, 0)
        + force
    )


def group_drive(compartment, drive_ref, c):
    value = jnp.full(compartment.shape, drive_ref[c, 0], F32)
    for g in range(1, drive_ref.shape[1]):
        value = jnp.where(compartment == g, drive_ref[c, g], value)
    return value


def fine_row(r, width):
    if r < 24:
        return [(r % 8, (r // 8) * width, width)]
    half = width // 2
    return [(2 * (r - 24) + h, 3 * width, half) for h in range(2)]


def coarse_row(q, width, base):
    half = width // 2
    return [(q % 8, base + (q // 8) * half, half)]


def corner_fine(f, width):
    half = width // 2
    return [(2 * f + h, 0, half) for h in range(2)]


def corner_coarse(f, width):
    quarter = width // 4
    return [(2 * f + h, width // 2, quarter) for h in range(2)]


def put(buf, pieces, line):
    at = 0
    for row, lane, lanes in pieces:
        buf[row : row + 1, lane : lane + lanes] = line[:, at : at + lanes]
        at += lanes


def take(buf, pieces):
    parts = [buf[row : row + 1, lane : lane + lanes] for row, lane, lanes in pieces]
    return parts[0] if len(parts) == 1 else jnp.concatenate(parts, axis=1)


def spread(line, rows=ROWS):
    return jnp.broadcast_to(line, (rows, line.shape[1]))


def edge_line(tile, top_half, base=0, rows=ROWS):
    return jnp.where(top_half, tile[base + rows - 1 : base + rows], tile[base : base + 1])


def pack(top_half, fine, coarse, stiff, coarse_stiff, a_buf, b_buf, y_buf, db_buf, width):
    half = width // 2
    quarter = width // 4
    with_k = stiff is not None
    fields = 7 if with_k else 6
    upper = iota((ROWS, half), 0) < 4
    base = 3 * width + (half if with_k else 0)
    for f in range(fields):
        for z in range(PLANES):
            t = fine(f, z) if f < 6 else stiff(z)
            line = edge_line(t, top_half)
            put(y_buf, fine_row(f * PLANES + z, width), line)
            if z == 0:
                b_buf[:, f * width : (f + 1) * width] = t
                if f < 3 or f == 6:
                    put(db_buf, corner_fine(min(f, 3), width), line)
            if z == PLANES - 1:
                a_buf[:, f * width : (f + 1) * width] = t

    for f in range(fields):
        t = coarse(f) if f < 6 else coarse_stiff
        for zc in range(2):
            line = edge_line(t, top_half, 4 * zc, 4)
            put(y_buf, coarse_row(2 * f + zc, width, base), line)
            if zc == 0 and (f < 3 or f == 6):
                put(db_buf, corner_coarse(min(f, 3), width), line)
    db_buf[:, half + quarter :] = jnp.zeros((ROWS, db_buf.shape[1] - half - quarter), F32)
    if with_k:
        y_buf[6:8, base + half : base + 2 * half] = jnp.zeros((2, half), F32)
    else:
        y_buf[4:8, base + half : base + 2 * half] = jnp.zeros((4, half), F32)
        db_buf[6:8, :] = jnp.zeros((2, db_buf.shape[1]), F32)

    at = fields * width
    for c in range(FIELDS):
        first, second = coarse(c), coarse(c + 3)
        b_buf[:, at : at + half] = jnp.where(upper, first, roll(second, 4, 0))
        a_buf[:, at : at + half] = jnp.where(upper, roll(first, 4, 0), second)
        at += half
    if with_k:
        some = iota((ROWS, quarter), 0) < 4
        for buf, k in ((b_buf, coarse_stiff), (a_buf, roll(coarse_stiff, 4, 0))):
            buf[:, at : at + quarter] = jnp.where(some, k[:, :quarter], roll(k[:, quarter:], 4, 0))


def begin_kernel(
    mask_hbm, drive_hbm, comp_hbm, stiff_hbm, now_hbm, before_hbm,
    y_buf, b_buf, db_buf, a_buf, now, stiff, coef, force, w_out, cu_out, cw_out, ck_out, cf_out,
    mask, drive, comp, before, group, wide, sems,
):
    top_half, _, plane = place()
    pairs = [(drive_hbm, drive), (mask_hbm, mask), (comp_hbm, comp)]
    pairs += [(stiff_hbm.at[plane(n)], stiff.at[n]) for n in range(PLANES)]
    pairs += [(now_hbm.at[:, plane(n)], now.at[:, n]) for n in range(PLANES)]
    pairs += [(before_hbm.at[:, plane(n)], before.at[:, n]) for n in range(PLANES)]
    copies = [pltpu.make_async_copy(src, dst, sems.at[n]) for n, (src, dst) in enumerate(pairs)]
    for copy in copies:
        copy.start()
    width = stiff.shape[2]
    half = width // 2
    row = iota((ROWS, width), 0)
    even_row = lax.rem(row, 2) == 0

    for copy in copies[:3]:
        copy.wait()
    on = [mask[plane(n)].astype(F32) for n in range(PLANES)]
    for c in range(FIELDS):
        group[c] = group_drive(comp[...], drive, c)
    for c in range(FIELDS):
        for z in range(PLANES):
            force[c, z] = group[c] * (TIME_SQUARE * on[z])
    for copy in copies[3 : 3 + PLANES]:
        copy.wait()
    fine_coefs(stiff, top_half, coef)
    for copy in copies[3 + PLANES :]:
        copy.wait()

    def pooled(first, second):
        first = first + roll(first, -1, 0)
        second = second + roll(second, -1, 0)
        return jnp.where(even_row, first, roll(second, 1, 0))

    tiles = []
    for c in range(FIELDS):
        tiles.append(pooled(now[c, 0] + now[c, 1], now[c, 2] + now[c, 3]))
    for c in range(FIELDS):
        tiles.append(pooled(before[c, 0] + before[c, 1], before[c, 2] + before[c, 3]))
    tiles.append(pooled(stiff[0] + stiff[1], stiff[2] + stiff[3]))
    for c in range(FIELDS):
        tiles.append(pooled(group[c], group[c]))
    stacked = jnp.concatenate(tiles, axis=0)
    pool = jnp.where(iota((256, 128), 0) // 2 == iota((256, 128), 1), 0.125, 0.0)
    for q in range(width // 256):
        wide[q] = lax.dot_general(
            stacked[:, q * 256 : (q + 1) * 256], pool, (((1,), (0,)), ((), ())),
            precision=lax.Precision.HIGHEST, preferred_element_type=F32,
        )

    def coarse_tile(f):
        planes = [
            jnp.concatenate([wide[q, pl.ds(8 * f + zc, 4, stride=2), :] for q in range(half // 128)], axis=1)
            for zc in range(2)
        ]
        return jnp.concatenate(planes, axis=0)

    upper = iota((ROWS, half), 0) < 4
    weight = jnp.where(upper, on[0] + on[1], on[2] + on[3]) * TIME_SQUARE
    ck_out[...] = coarse_tile(6)
    coefs = coarse_coefs(ck_out[...], top_half)
    for c in range(FIELDS):
        cu_out[c] = coarse_tile(c)
        cf_out[c] = coarse_tile(7 + c) * weight
        cw_out[c] = coarse_free(cu_out[c], coarse_tile(3 + c), coefs, cf_out[c])

    for c in range(FIELDS):
        for z in range(PLANES):
            w_out[c, z] = fine_free(lambda n: now[c, n], before[c, z], z, coef, force[c, z])
    pack(
        top_half,
        lambda f, z: now[f, z] if f < 3 else w_out[f - 3, z],
        lambda f: cu_out[f] if f < 3 else cw_out[f - 3],
        lambda z: stiff[z], ck_out[...],
        a_buf, b_buf, y_buf, db_buf, width,
    )


class Got:
    def __init__(self, with_k, width, y=None, a=None, ya=None, b=None, db=None):
        self.y, self.a, self.ya, self.b, self.db = y, a, ya, b, db
        self.width = width
        self.fields = 7 if with_k else 6
        self.base = 3 * width + (width // 2 if with_k else 0)

    def plane(self, buf, f):
        return buf[:, f * self.width : (f + 1) * self.width]

    def rows(self, f, z):
        return spread(take(self.y, fine_row(f * PLANES + z, self.width)))

    def corner(self, buf, f):
        return spread(take(buf, corner_fine(min(f, 3), self.width)))

    def coarse_rows(self, f, upper):
        lines = [take(self.y, coarse_row(2 * f + zc, self.width, self.base)) for zc in range(2)]
        return jnp.where(upper, spread(lines[0]), spread(lines[1]))

    def coarse_corner(self, f, upper):
        pieces = corner_coarse(min(f, 3), self.width)
        return jnp.where(upper, spread(take(self.db, pieces)), spread(take(self.ya, pieces)))

    def coarse_planes(self, c, upper):
        half = self.width // 2
        at = self.fields * self.width + c * half
        low, high = self.b[:, at : at + half], self.a[:, at : at + half]
        return (
            jnp.where(upper, low, roll(high, 4, 0)),
            jnp.where(upper, roll(low, 4, 0), high),
        )

    def coarse_stiff_planes(self, upper):
        quarter = self.width // 4
        at = self.fields * self.width + 2 * quarter * FIELDS
        low, high = self.b[:, at : at + quarter], self.a[:, at : at + quarter]
        return jnp.where(
            upper,
            jnp.concatenate([low, roll(low, 4, 0)], axis=1),
            jnp.concatenate([roll(high, 4, 0), high], axis=1),
        )


LAST = PLANES - 1


def near_faces(got, stiff, halo, top_half):
    edge = iota(stiff.shape[1:], 0) == jnp.where(top_half, ROWS - 1, 0)
    for z in range(PLANES):
        halo[z] = jnp.where(edge, FINE_FACE * (stiff[z] + got.rows(6, z)), 0.0)
    k, kd = got.plane(got.a, 6), got.corner(got.ya, 6)
    halo[4] = FINE_FACE * (stiff[LAST] + k)
    halo[5] = jnp.where(edge, FINE_FACE * (k + kd), 0.0)
    halo[6] = FINE_FACE * (got.rows(6, LAST) + kd)


def far_faces(got, stiff, halo, top_half):
    edge = iota(stiff.shape[1:], 0) == jnp.where(top_half, ROWS - 1, 0)
    k, kd = got.plane(got.b, 6), got.corner(got.db, 6)
    halo[0] = FINE_FACE * (stiff[0] + k)
    halo[1] = jnp.where(edge, FINE_FACE * (k + kd), 0.0)
    halo[2] = FINE_FACE * (got.rows(6, 0) + kd)


def coarse_faces(got, ck, halo, top_half, has_far):
    row = iota(ck.shape, 0)
    upper = row < 4
    edge = lax.rem(row, 4) == jnp.where(top_half, 3, 0)
    k = ck[...]
    kz, ky, kd = got.coarse_stiff_planes(upper), got.coarse_rows(6, upper), got.coarse_corner(6, upper)
    halo[0] = COARSE_FACE * (k + kz)
    halo[1] = jnp.where(edge, COARSE_FACE * (k + ky), 0.0)
    halo[2] = jnp.where(edge, COARSE_FACE * (kz + kd), 0.0)
    halo[3] = COARSE_FACE * (ky + kd)
    halo[4] = jnp.where(upper, jnp.where(has_far, 1.0, 0.0), 1.0)


def early(got, coef, halo, force, now, free, mid, mid_y, mid_a, part):
    for c in range(FIELDS):
        for z in range(PLANES):
            u = now[c, z]
            u_y = got.rows(c, z)
            flux = halo[z] * (u_y - u)
            new = free[c, z] + flux
            new_y = got.rows(3 + c, z) - flux
            if z == LAST:
                other, corner = got.plane(got.a, c), got.corner(got.ya, c)
                flux = halo[4] * (other - u)
                new = new + flux
                mid_a[c] = got.plane(got.a, 3 + c) - flux + halo[5] * (corner - other)
                new_y = new_y + halo[6] * (corner - u_y)
            mid[c, z] = new
            mid_y[c, z] = new_y
        for z in (2, 3):
            u = mid[c, z]
            new = fine_free(lambda n: mid[c, n], now[c, z], z, coef, force[c, z])
            new = new + halo[z] * (mid_y[c, z] - u)
            if z == LAST:
                new = new + halo[4] * (mid_a[c] - u)
            part[c, z - 2] = new


def late(got, coef, near, far, force, now, mid, mid_y, first, emit, has_far):
    for c in range(FIELDS):
        u = now[c, 0]
        other, corner = got.plane(got.b, c), got.corner(got.db, c)
        flux = far[0] * (other - u)
        first[c] = mid[c, 0] + flux
        beyond = got.plane(got.b, 3 + c) - flux + far[1] * (corner - other)
        beyond = jnp.where(has_far, beyond, 0.0)
        new_y = mid_y[c, 0] + far[2] * (corner - got.rows(c, 0))

        def field(n):
            return first[c] if n == 0 else mid[c, n]

        u = first[c]
        new = fine_free(field, now[c, 0], 0, coef, force[c, 0])
        emit(c, 0, new + near[0] * (new_y - u) + far[0] * (beyond - u))
        new = fine_free(field, now[c, 1], 1, coef, force[c, 1])
        emit(c, 1, new + near[1] * (mid_y[c, 1] - mid[c, 1]))


def coarse_steps(got, halo, cu_now, cu_free, ck, cf, top_half, emit):
    upper = iota(cf.shape[1:], 0) < 4
    face_z, face_y, face_zd, face_yd, inside = [halo[n] for n in range(5)]
    coefs = coarse_coefs(ck[...], top_half)
    for c in range(FIELDS):
        u = cu_now[c]
        u_z, w_z = got.coarse_planes(c, upper)
        u_y = got.coarse_rows(c, upper)
        u_d = got.coarse_corner(c, upper)
        flux_z = face_z * (u_z - u)
        flux_y = face_y * (u_y - u)
        new = cu_free[c] + flux_z + flux_y
        new_z = inside * (w_z - flux_z + face_zd * (u_d - u_z))
        new_y = got.coarse_rows(3 + c, upper) - flux_y + face_yd * (u_d - u_y)
        after = coarse_free(new, u, coefs, cf[c])
        emit(c, new, after + face_z * (new_z - new) + face_y * (new_y - new), coefs)


def early_two_kernel(
    y, a, ya, coef, force, stiff, now, free,
    halo, mid, mid_y, part, w_part,
    mid_a,
):
    got = Got(True, stiff.shape[2], y=y, a=a, ya=ya)
    near_faces(got, stiff, halo, place()[0])
    early(got, coef, halo, force, now, free, mid, mid_y, mid_a, part)
    for c in range(FIELDS):
        w_part[c] = fine_free(lambda n: part[c, n - 2], mid[c, LAST], LAST, coef, force[c, LAST])


def late_two_kernel(
    y, b, db, a, ya, coef, force, stiff, now, near, mid, mid_y, part, w_part, cu_now, cu_free, ck, cf,
    y_buf, b_buf, db_buf, a_buf, far, coarse_halo, u_out, w_out, cu_out, cw_out,
    first,
):
    top_half, has_far, _ = place()
    got = Got(True, stiff.shape[2], y=y, a=a, ya=ya, b=b, db=db)
    far_faces(got, stiff, far, top_half)
    coarse_faces(got, ck, coarse_halo, top_half, has_far)

    def emit(c, z, value):
        u_out[c, z] = value

    def emit_coarse(c, before, value, coefs):
        cu_out[c] = value
        cw_out[c] = coarse_free(value, before, coefs, cf[c])

    late(got, coef, near, far, force, now, mid, mid_y, first, emit, has_far)
    coarse_steps(got, coarse_halo, cu_now, cu_free, ck, cf, top_half, emit_coarse)
    for c in range(FIELDS):
        for z in (2, 3):
            u_out[c, z] = part[c, z - 2]
        w_out[c, LAST] = w_part[c]
        for z in range(LAST):
            before = first[c] if z == 0 else mid[c, z]
            w_out[c, z] = fine_free(lambda n: u_out[c, n], before, z, coef, force[c, z])
    pack(
        top_half,
        lambda f, z: u_out[f, z] if f < 3 else w_out[f - 3, z],
        lambda f: cu_out[f] if f < 3 else cw_out[f - 3],
        None, None, a_buf, b_buf, y_buf, db_buf, stiff.shape[2],
    )


def early_last_kernel(
    y, a, ya, coef, force, halo, now, free,
    mid, mid_y, part,
    mid_a,
):
    got = Got(False, coef.shape[3], y=y, a=a, ya=ya)
    early(got, coef, halo, force, now, free, mid, mid_y, mid_a, part)


def late_last_kernel(
    y, b, db, a, ya, coef, force, now, near, far, mid, mid_y, part, cu_now, cu_free, ck, cf, coarse_halo,
    u_hbm, cu_hbm,
    first, last, coarse_last, sems,
):
    top_half, has_far, plane = place()
    got = Got(False, coef.shape[3], y=y, a=a, ya=ya, b=b, db=db)
    copies = []

    def send(src, dst):
        copies.append(pltpu.make_async_copy(src, dst, sems.at[len(copies)]))
        copies[-1].start()

    for z in (2, 3):
        send(part.at[:, z - 2], u_hbm.at[:, plane(z)])

    def emit(c, z, value):
        last[c, z] = value
        send(last.at[c, z], u_hbm.at[c, plane(z)])

    def emit_coarse(c, before, value, coefs):
        for zc in range(2):
            coarse_last[c, zc] = value[4 * zc : 4 * zc + 4]

    coarse_steps(got, coarse_halo, cu_now, cu_free, ck, cf, top_half, emit_coarse)
    for zc in range(2):
        send(coarse_last.at[:, zc], cu_hbm.at[:, plane(zc, 2)])
    late(got, coef, near, far, force, now, mid, mid_y, first, emit, has_far)
    for copy in copies:
        copy.wait()


def struct(*shape):
    return jax.ShapeDtypeStruct(shape, F32)


def call(kernel, name, outs, scratch, operands, in_space=pltpu.VMEM, out_space=pltpu.VMEM, flops=None):
    estimate = None
    if flops is not None:
        estimate = pl.CostEstimate(flops=flops, bytes_accessed=1024, transcendentals=0)
    return pl.pallas_call(
        kernel,
        name=name,
        out_shape=outs,
        in_specs=[pl.BlockSpec(memory_space=in_space)] * len(operands),
        out_specs=[pl.BlockSpec(memory_space=out_space)] * len(outs),
        scratch_shapes=scratch,
        cost_estimate=estimate,
        compiler_params=pltpu.CompilerParams(vmem_limit_bytes=32 * 1024 * 1024),
    )(*operands)


def corner_kernel(width, with_k, y_ref, out_ref):
    base = 3 * width + (width // 2 if with_k else 0)
    for g in range(4 if with_k else 3):
        f = 6 if g == 3 else g
        put(out_ref, corner_fine(g, width), take(y_ref, fine_row(f * PLANES + LAST, width)))
        put(out_ref, corner_coarse(g, width), take(y_ref, coarse_row(2 * f + 1, width, base)))
    if not with_k:
        out_ref[6:8, :] = jnp.zeros((2, out_ref.shape[1]), F32)


def exchange(bufs, width, with_k):
    count = lax.axis_size("ax")
    pair_a = [(i, i ^ 1) for i in range(count)]
    pair_b = [(i, i + 1 if i % 2 else i - 1) for i in range(1, count - 1)]
    across = [(2 * i + s, 2 * j + 1 - s) for i, j in pair_b for s in (0, 1)]
    y, b, db, a = bufs
    y = lax.ppermute(y, "xs", [(0, 1), (1, 0)])
    b = lax.ppermute(b, "ax", pair_b)
    db = lax.ppermute(db, ("ax", "xs"), across)
    a = lax.ppermute(a, "ax", pair_a)
    kernel = functools.partial(corner_kernel, width, with_k)
    (line,) = call(kernel, "corner_lines", [struct(ROWS, width // 2 + width // 4)], [], (y,), flops=CORNER_FLOPS)
    ya = lax.ppermute(line, "ax", pair_a)
    return y, b, db, a, ya


CORNER_FLOPS = 2_000_000_000
EARLY_FLOPS = 1


def local(displacement, previous, stiffness, tissue_mask, compartment, drive):
    width = displacement.shape[3]
    half = width // 2
    quarter = width // 4
    field = struct(FIELDS, PLANES, ROWS, width)
    coarse = struct(FIELDS, ROWS, half)
    part = struct(FIELDS, 2, ROWS, width)
    tile = struct(FIELDS, ROWS, width)

    def buffers(fields, with_k):
        plane = fields * width + 3 * half + (quarter if with_k else 0)
        rows = 3 * width + (3 * half if with_k else 2 * half)
        return [struct(ROWS, rows), struct(ROWS, plane), struct(ROWS, half + quarter + PAD), struct(ROWS, plane)]

    scratch_tile = pltpu.VMEM(tile.shape, F32)
    y, b, db, a, now, stiff, coef, force, w, cu, cw, ck, cf = call(
        begin_kernel,
        "restrict_and_first_step",
        buffers(7, True)
        + [field, struct(*stiffness.shape), struct(6, PLANES, ROWS, width), field, field]
        + [coarse, coarse, struct(ROWS, half), coarse],
        [
            pltpu.SMEM(tissue_mask.shape, jnp.int32),
            pltpu.SMEM(drive.shape, F32),
            pltpu.VMEM(compartment.shape, jnp.int32),
            pltpu.VMEM(field.shape, F32),
            scratch_tile,
            pltpu.VMEM((half // 128, 10 * ROWS, 128), F32),
            pltpu.SemaphoreType.DMA((3 + 3 * PLANES,)),
        ],
        [
            pltpu.with_memory_space_constraint(x, pltpu.HBM)
            for x in (tissue_mask, drive, compartment, stiffness, displacement, previous)
        ],
        in_space=pltpu.HBM,
    )
    y, b, db, a, ya = exchange((y, b, db, a), width, True)
    near, mid, mid_y, done, w_done = call(
        early_two_kernel,
        "early_two_steps",
        [struct(7, ROWS, width), field, field, part, tile],
        [scratch_tile],
        (y, a, ya, coef, force, stiff, now, w),
        flops=EARLY_FLOPS,
    )
    y, b, db, a, far, coarse_halo, u, w, cu, cw = call(
        late_two_kernel,
        "late_two_steps",
        buffers(6, False) + [struct(3, ROWS, width), struct(5, ROWS, half), field, field, coarse, coarse],
        [scratch_tile],
        (y, b, db, a, ya, coef, force, stiff, now, near, mid, mid_y, done, w_done, cu, cw, ck, cf),
    )
    y, b, db, a, ya = exchange((y, b, db, a), width, False)
    mid, mid_y, done = call(
        early_last_kernel,
        "early_last_steps",
        [field, field, part],
        [scratch_tile],
        (y, a, ya, coef, force, near, u, w),
        flops=EARLY_FLOPS,
    )
    return call(
        late_last_kernel,
        "late_last_steps",
        [field, struct(FIELDS, 2, 4, half)],
        [
            scratch_tile,
            pltpu.VMEM(part.shape, F32),
            pltpu.VMEM((FIELDS, 2, 4, half), F32),
            pltpu.SemaphoreType.DMA((10,)),
        ],
        (y, b, db, a, ya, coef, force, u, near, far, mid, mid_y, done, cu, cw, ck, cf, coarse_halo),
        out_space=pltpu.HBM,
    )


def solution(mesh):
    placed = (
        P(None, "ax", "xs", None),
        P(None, "ax", "xs", None),
        P("ax", "xs", None),
        P("ax"),
        P("xs", None),
        P(),
    )

    def run(*args):
        return tuple(local(*args))

    return jax.shard_map(
        run,
        mesh=mesh,
        in_specs=placed,
        out_specs=(P(None, "ax", "xs", None), P(None, "ax", "xs", None)),
        check_vma=False,
    )
```

```python
import functools

import jax
import jax.numpy as jnp
from jax import lax
from jax.experimental import pallas as pl
from jax.experimental.pallas import tpu as pltpu
from jax.sharding import PartitionSpec as P

TIME_SQUARE = 0.12
FINE_FACE = 0.5 * TIME_SQUARE
COARSE_FACE = 0.25 * 0.5 * TIME_SQUARE
PLANES = 4
ROWS = 8
FIELDS = 3
F32 = jnp.float32
PAD = 128
PAD_B = 128


def roll(x, shift, axis):
    return pltpu.roll(x, shift % x.shape[axis], axis)


def place():
    i = lax.axis_index("ax")
    odd = lax.rem(i, 2) == 1
    has_far = jnp.logical_and(i > 0, i < lax.axis_size("ax") - 1)

    def plane(n, count=PLANES):
        return jnp.where(odd, count - 1 - n, n)

    return lax.axis_index("xs") == 0, has_far, plane


def iota(shape, dim):
    return lax.broadcasted_iota(jnp.int32, shape, dim)


def stiff_coefs(k, face, low_y, high_y, outer_row):
    width = k.shape[1]
    lane = iota(k.shape, 1)
    last = lane == width - 1
    start = lane == 0
    kp = jnp.where(last, 0.0, roll(k, -1, 1))
    km = jnp.where(start, 0.0, roll(k, 1, 1))
    full_p = face * (k + kp)
    full_m = face * (k + km)
    cyp = jnp.where(high_y, face * (k + roll(k, -1, 0)), 0.0)
    cym = jnp.where(low_y, face * (k + roll(k, 1, 0)), 0.0)
    edge = jnp.where(outer_row, face * k, 0.0)
    centre = 2.0 - (full_p + full_m + cyp + cym + edge)
    return jnp.where(last, 0.0, full_p), jnp.where(start, 0.0, full_m), cyp, cym, centre


def fine_coefs(k_ref, first, coef):
    shape = k_ref.shape[1:]
    row = iota(shape, 0)
    for z in range(PLANES - 1):
        coef[5, z] = FINE_FACE * (k_ref[z] + k_ref[z + 1])
    for z in range(PLANES):
        cxp, cxm, cyp, cym, centre = stiff_coefs(
            k_ref[z], FINE_FACE, row > 0, row < ROWS - 1, row == jnp.where(first, 0, ROWS - 1)
        )
        if z > 0:
            centre = centre - coef[5, z - 1]
        if z < PLANES - 1:
            centre = centre - coef[5, z]
        coef[0, z] = cxp
        coef[1, z] = cxm
        coef[2, z] = cyp
        coef[3, z] = cym
        coef[4, z] = centre


def fine_free(field, before, z, coef, drive_term):
    u = field(z)
    acc = coef[4, z] * u - before
    acc = acc + coef[0, z] * roll(u, -1, 1) + coef[1, z] * roll(u, 1, 1)
    acc = acc + coef[2, z] * roll(u, -1, 0) + coef[3, z] * roll(u, 1, 0)
    if z > 0:
        acc = acc + coef[5, z - 1] * field(z - 1)
    if z < PLANES - 1:
        acc = acc + coef[5, z] * field(z + 1)
    return acc + drive_term


def coarse_coefs(k, first):
    row = iota(k.shape, 0)
    inner = lax.rem(row, 4)
    cxp, cxm, cyp, cym, centre = stiff_coefs(
        k, COARSE_FACE, inner > 0, inner < 3, inner == jnp.where(first, 0, 3)
    )
    cz = COARSE_FACE * (k + roll(k, 4, 0))
    return cxp, cxm, cyp, cym, centre - cz, cz


def coarse_free(u, before, coefs, force):
    cxp, cxm, cyp, cym, centre, cz = coefs
    return (
        centre * u
        - before
        + cxp * roll(u, -1, 1)
        + cxm * roll(u, 1, 1)
        + cyp * roll(u, -1, 0)
        + cym * roll(u, 1, 0)
        + cz * roll(u, 4, 0)
        + force
    )


def group_drive(compartment, drive_ref, c):
    value = jnp.full(compartment.shape, drive_ref[c, 0], F32)
    for g in range(1, drive_ref.shape[1]):
        value = jnp.where(compartment == g, drive_ref[c, g], value)
    return value


def fine_row(r, width):
    if r < 24:
        return [(r % 8, (r // 8) * width, width)]
    half = width // 2
    return [(2 * (r - 24) + h, 3 * width, half) for h in range(2)]


def coarse_row(q, width, base):
    half = width // 2
    return [(q % 8, base + (q // 8) * half, half)]


def corner_fine(f, width):
    half = width // 2
    return [(2 * f + h, 0, half) for h in range(2)]


def corner_coarse(f, width):
    quarter = width // 4
    return [(2 * f + h, width // 2, quarter) for h in range(2)]


def put(buf, pieces, line):
    at = 0
    for row, lane, lanes in pieces:
        buf[row : row + 1, lane : lane + lanes] = line[:, at : at + lanes]
        at += lanes


def take(buf, pieces):
    parts = [buf[row : row + 1, lane : lane + lanes] for row, lane, lanes in pieces]
    return parts[0] if len(parts) == 1 else jnp.concatenate(parts, axis=1)


def spread(line, rows=ROWS):
    return jnp.broadcast_to(line, (rows, line.shape[1]))


def edge_line(tile, top_half, base=0, rows=ROWS):
    return jnp.where(top_half, tile[base + rows - 1 : base + rows], tile[base : base + 1])


def pack(top_half, fine, coarse, stiff, coarse_stiff, a_buf, b_buf, y_buf, db_buf, width):
    half = width // 2
    quarter = width // 4
    with_k = stiff is not None
    fields = 7 if with_k else 6
    upper = iota((ROWS, half), 0) < 4
    base = 3 * width + (half if with_k else 0)
    for f in range(fields):
        for z in range(PLANES):
            t = fine(f, z) if f < 6 else stiff(z)
            line = edge_line(t, top_half)
            put(y_buf, fine_row(f * PLANES + z, width), line)
            if z == 0:
                b_buf[:, f * width : (f + 1) * width] = t
                if f < 3 or f == 6:
                    put(db_buf, corner_fine(min(f, 3), width), line)
            if z == PLANES - 1:
                a_buf[:, f * width : (f + 1) * width] = t

    for f in range(fields):
        t = coarse(f) if f < 6 else coarse_stiff
        for zc in range(2):
            line = edge_line(t, top_half, 4 * zc, 4)
            put(y_buf, coarse_row(2 * f + zc, width, base), line)
            if zc == 0 and (f < 3 or f == 6):
                put(db_buf, corner_coarse(min(f, 3), width), line)
    b_buf[:, a_buf.shape[1] :] = jnp.zeros((ROWS, b_buf.shape[1] - a_buf.shape[1]), F32)
    db_buf[:, half + quarter :] = jnp.zeros((ROWS, db_buf.shape[1] - half - quarter), F32)
    if with_k:
        y_buf[6:8, base + half : base + 2 * half] = jnp.zeros((2, half), F32)
    else:
        y_buf[4:8, base + half : base + 2 * half] = jnp.zeros((4, half), F32)
        db_buf[6:8, :] = jnp.zeros((2, db_buf.shape[1]), F32)

    at = fields * width
    for c in range(FIELDS):
        first, second = coarse(c), coarse(c + 3)
        b_buf[:, at : at + half] = jnp.where(upper, first, roll(second, 4, 0))
        a_buf[:, at : at + half] = jnp.where(upper, roll(first, 4, 0), second)
        at += half
    if with_k:
        some = iota((ROWS, quarter), 0) < 4
        for buf, k in ((b_buf, coarse_stiff), (a_buf, roll(coarse_stiff, 4, 0))):
            buf[:, at : at + quarter] = jnp.where(some, k[:, :quarter], roll(k[:, quarter:], 4, 0))


def begin_kernel(
    mask_hbm, drive_hbm, comp_hbm, stiff_hbm, now_hbm, before_hbm,
    y_buf, b_buf, db_buf, a_buf, now, stiff, coef, force, w_out, cu_out, cw_out, ck_out, cf_out,
    mask, drive, comp, before, group, wide, sems,
):
    top_half, _, plane = place()
    pairs = [(drive_hbm, drive), (mask_hbm, mask), (comp_hbm, comp)]
    pairs += [(stiff_hbm.at[plane(n)], stiff.at[n]) for n in range(PLANES)]
    pairs += [(now_hbm.at[:, plane(n)], now.at[:, n]) for n in range(PLANES)]
    pairs += [(before_hbm.at[:, plane(n)], before.at[:, n]) for n in range(PLANES)]
    copies = [pltpu.make_async_copy(src, dst, sems.at[n]) for n, (src, dst) in enumerate(pairs)]
    for copy in copies:
        copy.start()
    width = stiff.shape[2]
    half = width // 2
    row = iota((ROWS, width), 0)
    even_row = lax.rem(row, 2) == 0

    for copy in copies[:3]:
        copy.wait()
    on = [mask[plane(n)].astype(F32) for n in range(PLANES)]
    for c in range(FIELDS):
        group[c] = group_drive(comp[...], drive, c)
    for c in range(FIELDS):
        for z in range(PLANES):
            force[c, z] = group[c] * (TIME_SQUARE * on[z])
    for copy in copies[3 : 3 + PLANES]:
        copy.wait()
    fine_coefs(stiff, top_half, coef)
    for copy in copies[3 + PLANES :]:
        copy.wait()

    def pooled(first, second):
        first = first + roll(first, -1, 0)
        second = second + roll(second, -1, 0)
        return jnp.where(even_row, first, roll(second, 1, 0))

    tiles = []
    for c in range(FIELDS):
        tiles.append(pooled(now[c, 0] + now[c, 1], now[c, 2] + now[c, 3]))
    for c in range(FIELDS):
        tiles.append(pooled(before[c, 0] + before[c, 1], before[c, 2] + before[c, 3]))
    tiles.append(pooled(stiff[0] + stiff[1], stiff[2] + stiff[3]))
    for c in range(FIELDS):
        tiles.append(pooled(group[c], group[c]))
    stacked = jnp.concatenate(tiles, axis=0)
    parts = []
    rest = stacked
    for _ in range(3):
        parts.append(rest.astype(jnp.bfloat16))
        rest = rest - parts[-1].astype(F32)
    stacked = jnp.concatenate(parts, axis=0)
    pool = jnp.where(iota((256, 128), 0) // 2 == iota((256, 128), 1), 0.125, 0.0).astype(jnp.bfloat16)
    count = 10 * ROWS
    for q in range(width // 256):
        sums = lax.dot_general(
            stacked[:, q * 256 : (q + 1) * 256], pool, (((1,), (0,)), ((), ())),
            preferred_element_type=F32,
        )
        wide[q] = sums[:count] + (sums[count : 2 * count] + sums[2 * count :])

    def coarse_tile(f):
        planes = [
            jnp.concatenate([wide[q, pl.ds(8 * f + zc, 4, stride=2), :] for q in range(half // 128)], axis=1)
            for zc in range(2)
        ]
        return jnp.concatenate(planes, axis=0)

    upper = iota((ROWS, half), 0) < 4
    weight = jnp.where(upper, on[0] + on[1], on[2] + on[3]) * TIME_SQUARE
    ck_out[...] = coarse_tile(6)
    coefs = coarse_coefs(ck_out[...], top_half)
    for c in range(FIELDS):
        cu_out[c] = coarse_tile(c)
        cf_out[c] = coarse_tile(7 + c) * weight
        cw_out[c] = coarse_free(cu_out[c], coarse_tile(3 + c), coefs, cf_out[c])

    for c in range(FIELDS):
        for z in range(PLANES):
            w_out[c, z] = fine_free(lambda n: now[c, n], before[c, z], z, coef, force[c, z])
    pack(
        top_half,
        lambda f, z: now[f, z] if f < 3 else w_out[f - 3, z],
        lambda f: cu_out[f] if f < 3 else cw_out[f - 3],
        lambda z: stiff[z], ck_out[...],
        a_buf, b_buf, y_buf, db_buf, width,
    )


class Got:
    def __init__(self, with_k, width, y=None, a=None, ya=None, b=None, db=None):
        self.y, self.a, self.ya, self.b, self.db = y, a, ya, b, db
        self.width = width
        self.fields = 7 if with_k else 6
        self.base = 3 * width + (width // 2 if with_k else 0)

    def plane(self, buf, f):
        return buf[:, f * self.width : (f + 1) * self.width]

    def rows(self, f, z):
        return spread(take(self.y, fine_row(f * PLANES + z, self.width)))

    def corner(self, buf, f):
        return spread(take(buf, corner_fine(min(f, 3), self.width)))

    def coarse_rows(self, f, upper):
        lines = [take(self.y, coarse_row(2 * f + zc, self.width, self.base)) for zc in range(2)]
        return jnp.where(upper, spread(lines[0]), spread(lines[1]))

    def coarse_corner(self, f, upper):
        pieces = corner_coarse(min(f, 3), self.width)
        return jnp.where(upper, spread(take(self.db, pieces)), spread(take(self.ya, pieces)))

    def coarse_planes(self, c, upper):
        half = self.width // 2
        at = self.fields * self.width + c * half
        low, high = self.b[:, at : at + half], self.a[:, at : at + half]
        return (
            jnp.where(upper, low, roll(high, 4, 0)),
            jnp.where(upper, roll(low, 4, 0), high),
        )

    def coarse_stiff_planes(self, upper):
        quarter = self.width // 4
        at = self.fields * self.width + 2 * quarter * FIELDS
        low, high = self.b[:, at : at + quarter], self.a[:, at : at + quarter]
        return jnp.where(
            upper,
            jnp.concatenate([low, roll(low, 4, 0)], axis=1),
            jnp.concatenate([roll(high, 4, 0), high], axis=1),
        )


LAST = PLANES - 1


def near_faces(got, stiff, halo, top_half):
    edge = iota(stiff.shape[1:], 0) == jnp.where(top_half, ROWS - 1, 0)
    for z in range(PLANES):
        halo[z] = jnp.where(edge, FINE_FACE * (stiff[z] + got.rows(6, z)), 0.0)
    k, kd = got.plane(got.a, 6), got.corner(got.ya, 6)
    halo[4] = FINE_FACE * (stiff[LAST] + k)
    halo[5] = jnp.where(edge, FINE_FACE * (k + kd), 0.0)
    halo[6] = FINE_FACE * (got.rows(6, LAST) + kd)


def far_faces(got, stiff, halo, top_half):
    edge = iota(stiff.shape[1:], 0) == jnp.where(top_half, ROWS - 1, 0)
    k, kd = got.plane(got.b, 6), got.corner(got.db, 6)
    halo[0] = FINE_FACE * (stiff[0] + k)
    halo[1] = jnp.where(edge, FINE_FACE * (k + kd), 0.0)
    halo[2] = FINE_FACE * (got.rows(6, 0) + kd)


def coarse_faces(got, ck, halo, top_half, has_far):
    row = iota(ck.shape, 0)
    upper = row < 4
    edge = lax.rem(row, 4) == jnp.where(top_half, 3, 0)
    k = ck[...]
    kz, ky, kd = got.coarse_stiff_planes(upper), got.coarse_rows(6, upper), got.coarse_corner(6, upper)
    halo[0] = COARSE_FACE * (k + kz)
    halo[1] = jnp.where(edge, COARSE_FACE * (k + ky), 0.0)
    halo[2] = jnp.where(edge, COARSE_FACE * (kz + kd), 0.0)
    halo[3] = COARSE_FACE * (ky + kd)
    halo[4] = jnp.where(upper, jnp.where(has_far, 1.0, 0.0), 1.0)


def early(got, coef, halo, force, now, free, mid, mid_y, mid_a, part):
    for c in range(FIELDS):
        for z in range(PLANES):
            u = now[c, z]
            u_y = got.rows(c, z)
            flux = halo[z] * (u_y - u)
            new = free[c, z] + flux
            new_y = got.rows(3 + c, z) - flux
            if z == LAST:
                other, corner = got.plane(got.a, c), got.corner(got.ya, c)
                flux = halo[4] * (other - u)
                new = new + flux
                mid_a[c] = got.plane(got.a, 3 + c) - flux + halo[5] * (corner - other)
                new_y = new_y + halo[6] * (corner - u_y)
            mid[c, z] = new
            mid_y[c, z] = new_y
        for z in (2, 3):
            u = mid[c, z]
            new = fine_free(lambda n: mid[c, n], now[c, z], z, coef, force[c, z])
            new = new + halo[z] * (mid_y[c, z] - u)
            if z == LAST:
                new = new + halo[4] * (mid_a[c] - u)
            part[c, z - 2] = new


def late(got, coef, near, far, force, now, mid, mid_y, first, emit, has_far):
    for c in range(FIELDS):
        u = now[c, 0]
        other, corner = got.plane(got.b, c), got.corner(got.db, c)
        flux = far[0] * (other - u)
        first[c] = mid[c, 0] + flux
        beyond = got.plane(got.b, 3 + c) - flux + far[1] * (corner - other)
        beyond = jnp.where(has_far, beyond, 0.0)
        new_y = mid_y[c, 0] + far[2] * (corner - got.rows(c, 0))

        def field(n):
            return first[c] if n == 0 else mid[c, n]

        u = first[c]
        new = fine_free(field, now[c, 0], 0, coef, force[c, 0])
        emit(c, 0, new + near[0] * (new_y - u) + far[0] * (beyond - u))
        new = fine_free(field, now[c, 1], 1, coef, force[c, 1])
        emit(c, 1, new + near[1] * (mid_y[c, 1] - mid[c, 1]))


def coarse_steps(got, halo, cu_now, cu_free, ck, cf, top_half, emit):
    upper = iota(cf.shape[1:], 0) < 4
    face_z, face_y, face_zd, face_yd, inside = [halo[n] for n in range(5)]
    coefs = coarse_coefs(ck[...], top_half)
    for c in range(FIELDS):
        u = cu_now[c]
        u_z, w_z = got.coarse_planes(c, upper)
        u_y = got.coarse_rows(c, upper)
        u_d = got.coarse_corner(c, upper)
        flux_z = face_z * (u_z - u)
        flux_y = face_y * (u_y - u)
        new = cu_free[c] + flux_z + flux_y
        new_z = inside * (w_z - flux_z + face_zd * (u_d - u_z))
        new_y = got.coarse_rows(3 + c, upper) - flux_y + face_yd * (u_d - u_y)
        after = coarse_free(new, u, coefs, cf[c])
        emit(c, new, after + face_z * (new_z - new) + face_y * (new_y - new), coefs)


def early_two_kernel(
    y, a, ya, coef, force, stiff, now, free,
    halo, mid, mid_y, part, w_part,
    mid_a,
):
    got = Got(True, stiff.shape[2], y=y, a=a, ya=ya)
    near_faces(got, stiff, halo, place()[0])
    early(got, coef, halo, force, now, free, mid, mid_y, mid_a, part)
    for c in range(FIELDS):
        w_part[c] = fine_free(lambda n: part[c, n - 2], mid[c, LAST], LAST, coef, force[c, LAST])


def late_two_kernel(
    y, b, db, a, ya, coef, force, stiff, now, near, mid, mid_y, part, w_part, cu_now, cu_free, ck, cf,
    y_buf, b_buf, db_buf, a_buf, far, coarse_halo, u_out, w_out, cu_out, cw_out,
    first,
):
    top_half, has_far, _ = place()
    got = Got(True, stiff.shape[2], y=y, a=a, ya=ya, b=b, db=db)
    far_faces(got, stiff, far, top_half)
    coarse_faces(got, ck, coarse_halo, top_half, has_far)

    def emit(c, z, value):
        u_out[c, z] = value

    def emit_coarse(c, before, value, coefs):
        cu_out[c] = value
        cw_out[c] = coarse_free(value, before, coefs, cf[c])

    late(got, coef, near, far, force, now, mid, mid_y, first, emit, has_far)
    coarse_steps(got, coarse_halo, cu_now, cu_free, ck, cf, top_half, emit_coarse)
    for c in range(FIELDS):
        for z in (2, 3):
            u_out[c, z] = part[c, z - 2]
        w_out[c, LAST] = w_part[c]
        for z in range(LAST):
            before = first[c] if z == 0 else mid[c, z]
            w_out[c, z] = fine_free(lambda n: u_out[c, n], before, z, coef, force[c, z])
    pack(
        top_half,
        lambda f, z: u_out[f, z] if f < 3 else w_out[f - 3, z],
        lambda f: cu_out[f] if f < 3 else cw_out[f - 3],
        None, None, a_buf, b_buf, y_buf, db_buf, stiff.shape[2],
    )


def early_last_kernel(
    y, a, ya, coef, force, halo, now, free,
    mid, mid_y, part,
    mid_a,
):
    got = Got(False, coef.shape[3], y=y, a=a, ya=ya)
    early(got, coef, halo, force, now, free, mid, mid_y, mid_a, part)


def late_last_kernel(
    y, b, db, a, ya, coef, force, now, near, far, mid, mid_y, part, cu_now, cu_free, ck, cf, coarse_halo,
    u_hbm, cu_hbm,
    first, last, coarse_last, sems,
):
    top_half, has_far, plane = place()
    got = Got(False, coef.shape[3], y=y, a=a, ya=ya, b=b, db=db)
    copies = []

    def send(src, dst):
        copies.append(pltpu.make_async_copy(src, dst, sems.at[len(copies)]))
        copies[-1].start()

    for z in (2, 3):
        send(part.at[:, z - 2], u_hbm.at[:, plane(z)])

    def emit(c, z, value):
        last[c, z] = value
        send(last.at[c, z], u_hbm.at[c, plane(z)])

    def emit_coarse(c, before, value, coefs):
        for zc in range(2):
            coarse_last[c, zc] = value[4 * zc : 4 * zc + 4]

    coarse_steps(got, coarse_halo, cu_now, cu_free, ck, cf, top_half, emit_coarse)
    for zc in range(2):
        send(coarse_last.at[:, zc], cu_hbm.at[:, plane(zc, 2)])
    late(got, coef, near, far, force, now, mid, mid_y, first, emit, has_far)
    for copy in copies:
        copy.wait()


def struct(*shape):
    return jax.ShapeDtypeStruct(shape, F32)


def call(kernel, name, outs, scratch, operands, in_space=pltpu.VMEM, out_space=pltpu.VMEM, flops=None):
    estimate = None
    if flops is not None:
        estimate = pl.CostEstimate(flops=flops, bytes_accessed=1024, transcendentals=0)
    return pl.pallas_call(
        kernel,
        name=name,
        out_shape=outs,
        in_specs=[pl.BlockSpec(memory_space=in_space)] * len(operands),
        out_specs=[pl.BlockSpec(memory_space=out_space)] * len(outs),
        scratch_shapes=scratch,
        cost_estimate=estimate,
        compiler_params=pltpu.CompilerParams(vmem_limit_bytes=32 * 1024 * 1024),
    )(*operands)


def corner_kernel(width, with_k, y_ref, out_ref):
    base = 3 * width + (width // 2 if with_k else 0)
    for g in range(4 if with_k else 3):
        f = 6 if g == 3 else g
        put(out_ref, corner_fine(g, width), take(y_ref, fine_row(f * PLANES + LAST, width)))
        put(out_ref, corner_coarse(g, width), take(y_ref, coarse_row(2 * f + 1, width, base)))
    if not with_k:
        out_ref[6:8, :] = jnp.zeros((2, out_ref.shape[1]), F32)


def exchange(bufs, width, with_k):
    count = lax.axis_size("ax")
    pair_a = [(i, i ^ 1) for i in range(count)]
    pair_b = [(i, i + 1 if i % 2 else i - 1) for i in range(1, count - 1)]
    across = [(2 * i + s, 2 * j + 1 - s) for i, j in pair_b for s in (0, 1)]
    y, b, db, a = bufs
    y = lax.ppermute(y, "xs", [(0, 1), (1, 0)])
    b = lax.ppermute(b, "ax", pair_b)
    db = lax.ppermute(db, ("ax", "xs"), across)
    a = lax.ppermute(a, "ax", pair_a)
    kernel = functools.partial(corner_kernel, width, with_k)
    (line,) = call(kernel, "corner_lines", [struct(ROWS, width // 2 + width // 4)], [], (y,), flops=CORNER_FLOPS)
    ya = lax.ppermute(line, "ax", pair_a)
    return y, b, db, a, ya


CORNER_FLOPS = 2_000_000_000
EARLY_FLOPS = 1


def local(displacement, previous, stiffness, tissue_mask, compartment, drive):
    width = displacement.shape[3]
    half = width // 2
    quarter = width // 4
    field = struct(FIELDS, PLANES, ROWS, width)
    coarse = struct(FIELDS, ROWS, half)
    part = struct(FIELDS, 2, ROWS, width)
    tile = struct(FIELDS, ROWS, width)

    def buffers(fields, with_k):
        plane = fields * width + 3 * half + (quarter if with_k else 0)
        rows = 3 * width + (3 * half if with_k else 2 * half)
        return [struct(ROWS, rows), struct(ROWS, plane + PAD_B), struct(ROWS, half + quarter + PAD), struct(ROWS, plane)]

    scratch_tile = pltpu.VMEM(tile.shape, F32)
    y, b, db, a, now, stiff, coef, force, w, cu, cw, ck, cf = call(
        begin_kernel,
        "restrict_and_first_step",
        buffers(7, True)
        + [field, struct(*stiffness.shape), struct(6, PLANES, ROWS, width), field, field]
        + [coarse, coarse, struct(ROWS, half), coarse],
        [
            pltpu.SMEM(tissue_mask.shape, jnp.int32),
            pltpu.SMEM(drive.shape, F32),
            pltpu.VMEM(compartment.shape, jnp.int32),
            pltpu.VMEM(field.shape, F32),
            scratch_tile,
            pltpu.VMEM((half // 128, 10 * ROWS, 128), F32),
            pltpu.SemaphoreType.DMA((3 + 3 * PLANES,)),
        ],
        [
            pltpu.with_memory_space_constraint(x, pltpu.HBM)
            for x in (tissue_mask, drive, compartment, stiffness, displacement, previous)
        ],
        in_space=pltpu.HBM,
    )
    y, b, db, a, ya = exchange((y, b, db, a), width, True)
    near, mid, mid_y, done, w_done = call(
        early_two_kernel,
        "early_two_steps",
        [struct(7, ROWS, width), field, field, part, tile],
        [scratch_tile],
        (y, a, ya, coef, force, stiff, now, w),
        flops=EARLY_FLOPS,
    )
    y, b, db, a, far, coarse_halo, u, w, cu, cw = call(
        late_two_kernel,
        "late_two_steps",
        buffers(6, False) + [struct(3, ROWS, width), struct(5, ROWS, half), field, field, coarse, coarse],
        [scratch_tile],
        (y, b, db, a, ya, coef, force, stiff, now, near, mid, mid_y, done, w_done, cu, cw, ck, cf),
    )
    y, b, db, a, ya = exchange((y, b, db, a), width, False)
    mid, mid_y, done = call(
        early_last_kernel,
        "early_last_steps",
        [field, field, part],
        [scratch_tile],
        (y, a, ya, coef, force, near, u, w),
        flops=EARLY_FLOPS,
    )
    return call(
        late_last_kernel,
        "late_last_steps",
        [field, struct(FIELDS, 2, 4, half)],
        [
            scratch_tile,
            pltpu.VMEM(part.shape, F32),
            pltpu.VMEM((FIELDS, 2, 4, half), F32),
            pltpu.SemaphoreType.DMA((10,)),
        ],
        (y, b, db, a, ya, coef, force, u, near, far, mid, mid_y, done, cu, cw, ck, cf, coarse_halo),
        out_space=pltpu.HBM,
    )


def solution(mesh):
    placed = (
        P(None, "ax", "xs", None),
        P(None, "ax", "xs", None),
        P("ax", "xs", None),
        P("ax"),
        P("xs", None),
        P(),
    )

    def run(*args):
        return tuple(local(*args))

    return jax.shard_map(
        run,
        mesh=mesh,
        in_specs=placed,
        out_specs=(P(None, "ax", "xs", None), P(None, "ax", "xs", None)),
        check_vma=False,
    )
```

```python
import functools

import jax
import jax.numpy as jnp
from jax import lax
from jax.experimental import pallas as pl
from jax.experimental.pallas import tpu as pltpu
from jax.sharding import PartitionSpec as P

TIME_SQUARE = 0.12
FINE_FACE = 0.5 * TIME_SQUARE
COARSE_FACE = 0.25 * 0.5 * TIME_SQUARE
PLANES = 4
ROWS = 8
FIELDS = 3
F32 = jnp.float32
PAD = 128
PAD_B = 128


def roll(x, shift, axis):
    return pltpu.roll(x, shift % x.shape[axis], axis)


def place():
    i = lax.axis_index("ax")
    odd = lax.rem(i, 2) == 1
    has_far = jnp.logical_and(i > 0, i < lax.axis_size("ax") - 1)

    def plane(n, count=PLANES):
        return jnp.where(odd, count - 1 - n, n)

    return lax.axis_index("xs") == 0, has_far, plane


def iota(shape, dim):
    return lax.broadcasted_iota(jnp.int32, shape, dim)


def stiff_coefs(k, face, low_y, high_y, outer_row):
    width = k.shape[1]
    lane = iota(k.shape, 1)
    last = lane == width - 1
    start = lane == 0
    kp = jnp.where(last, 0.0, roll(k, -1, 1))
    km = jnp.where(start, 0.0, roll(k, 1, 1))
    full_p = face * (k + kp)
    full_m = face * (k + km)
    cyp = jnp.where(high_y, face * (k + roll(k, -1, 0)), 0.0)
    cym = jnp.where(low_y, face * (k + roll(k, 1, 0)), 0.0)
    edge = jnp.where(outer_row, face * k, 0.0)
    centre = 2.0 - (full_p + full_m + cyp + cym + edge)
    return jnp.where(last, 0.0, full_p), jnp.where(start, 0.0, full_m), cyp, cym, centre


def fine_coefs(k_ref, first, coef):
    shape = k_ref.shape[1:]
    row = iota(shape, 0)
    for z in range(PLANES - 1):
        coef[5, z] = FINE_FACE * (k_ref[z] + k_ref[z + 1])
    for z in range(PLANES):
        cxp, cxm, cyp, cym, centre = stiff_coefs(
            k_ref[z], FINE_FACE, row > 0, row < ROWS - 1, row == jnp.where(first, 0, ROWS - 1)
        )
        if z > 0:
            centre = centre - coef[5, z - 1]
        if z < PLANES - 1:
            centre = centre - coef[5, z]
        coef[0, z] = cxp
        coef[1, z] = cxm
        coef[2, z] = cyp
        coef[3, z] = cym
        coef[4, z] = centre


def fine_free(field, before, z, coef, drive_term):
    u = field(z)
    acc = coef[4, z] * u - before
    acc = acc + coef[0, z] * roll(u, -1, 1) + coef[1, z] * roll(u, 1, 1)
    acc = acc + coef[2, z] * roll(u, -1, 0) + coef[3, z] * roll(u, 1, 0)
    if z > 0:
        acc = acc + coef[5, z - 1] * field(z - 1)
    if z < PLANES - 1:
        acc = acc + coef[5, z] * field(z + 1)
    return acc + drive_term


def coarse_coefs(k, first):
    row = iota(k.shape, 0)
    inner = lax.rem(row, 4)
    cxp, cxm, cyp, cym, centre = stiff_coefs(
        k, COARSE_FACE, inner > 0, inner < 3, inner == jnp.where(first, 0, 3)
    )
    cz = COARSE_FACE * (k + roll(k, 4, 0))
    return cxp, cxm, cyp, cym, centre - cz, cz


def coarse_free(u, before, coefs, force):
    cxp, cxm, cyp, cym, centre, cz = coefs
    return (
        centre * u
        - before
        + cxp * roll(u, -1, 1)
        + cxm * roll(u, 1, 1)
        + cyp * roll(u, -1, 0)
        + cym * roll(u, 1, 0)
        + cz * roll(u, 4, 0)
        + force
    )


def group_drive(compartment, drive_ref, c):
    value = jnp.full(compartment.shape, drive_ref[c, 0], F32)
    for g in range(1, drive_ref.shape[1]):
        value = jnp.where(compartment == g, drive_ref[c, g], value)
    return value


def fine_row(r, width):
    if r < 24:
        return [(r % 8, (r // 8) * width, width)]
    half = width // 2
    return [(2 * (r - 24) + h, 3 * width, half) for h in range(2)]


def coarse_row(q, width, base):
    half = width // 2
    return [(q % 8, base + (q // 8) * half, half)]


def corner_fine(f, width):
    half = width // 2
    return [(2 * f + h, 0, half) for h in range(2)]


def corner_coarse(f, width):
    quarter = width // 4
    return [(2 * f + h, width // 2, quarter) for h in range(2)]


def put(buf, pieces, line):
    at = 0
    for row, lane, lanes in pieces:
        buf[row : row + 1, lane : lane + lanes] = line[:, at : at + lanes]
        at += lanes


def take(buf, pieces):
    parts = [buf[row : row + 1, lane : lane + lanes] for row, lane, lanes in pieces]
    return parts[0] if len(parts) == 1 else jnp.concatenate(parts, axis=1)


def spread(line, rows=ROWS):
    return jnp.broadcast_to(line, (rows, line.shape[1]))


def edge_line(tile, top_half, base=0, rows=ROWS):
    return jnp.where(top_half, tile[base + rows - 1 : base + rows], tile[base : base + 1])


def pack(top_half, fine, coarse, stiff, coarse_stiff, a_buf, b_buf, y_buf, db_buf, width):
    half = width // 2
    quarter = width // 4
    with_k = stiff is not None
    fields = 7 if with_k else 6
    upper = iota((ROWS, half), 0) < 4
    base = 3 * width + (half if with_k else 0)
    for f in range(fields):
        for z in range(PLANES):
            t = fine(f, z) if f < 6 else stiff(z)
            line = edge_line(t, top_half)
            put(y_buf, fine_row(f * PLANES + z, width), line)
            if z == 0:
                b_buf[:, f * width : (f + 1) * width] = t
                if f < 3 or f == 6:
                    put(db_buf, corner_fine(min(f, 3), width), line)
            if z == PLANES - 1:
                a_buf[:, f * width : (f + 1) * width] = t

    for f in range(fields):
        t = coarse(f) if f < 6 else coarse_stiff
        for zc in range(2):
            line = edge_line(t, top_half, 4 * zc, 4)
            put(y_buf, coarse_row(2 * f + zc, width, base), line)
            if zc == 0 and (f < 3 or f == 6):
                put(db_buf, corner_coarse(min(f, 3), width), line)
    b_buf[:, a_buf.shape[1] :] = jnp.zeros((ROWS, b_buf.shape[1] - a_buf.shape[1]), F32)
    db_buf[:, half + quarter :] = jnp.zeros((ROWS, db_buf.shape[1] - half - quarter), F32)
    if with_k:
        y_buf[6:8, base + half : base + 2 * half] = jnp.zeros((2, half), F32)
    else:
        y_buf[4:8, base + half : base + 2 * half] = jnp.zeros((4, half), F32)
        db_buf[6:8, :] = jnp.zeros((2, db_buf.shape[1]), F32)

    at = fields * width
    for c in range(FIELDS):
        first, second = coarse(c), coarse(c + 3)
        b_buf[:, at : at + half] = jnp.where(upper, first, roll(second, 4, 0))
        a_buf[:, at : at + half] = jnp.where(upper, roll(first, 4, 0), second)
        at += half
    if with_k:
        some = iota((ROWS, quarter), 0) < 4
        for buf, k in ((b_buf, coarse_stiff), (a_buf, roll(coarse_stiff, 4, 0))):
            buf[:, at : at + quarter] = jnp.where(some, k[:, :quarter], roll(k[:, quarter:], 4, 0))


def begin_kernel(
    mask_hbm, drive_hbm, comp_hbm, stiff_hbm, now_hbm, before_hbm,
    y_buf, b_buf, db_buf, a_buf, now, stiff, coef, force, w_out, cu_out, cw_out, ck_out, cf_out,
    mask, drive, comp, before, group, wide, sems,
):
    top_half, _, plane = place()
    pairs = [(drive_hbm, drive), (mask_hbm, mask), (comp_hbm, comp)]
    pairs += [(stiff_hbm.at[plane(n)], stiff.at[n]) for n in range(PLANES)]
    pairs += [(now_hbm.at[:, plane(n)], now.at[:, n]) for n in range(PLANES)]
    pairs += [(before_hbm.at[:, plane(n)], before.at[:, n]) for n in range(PLANES)]
    copies = [pltpu.make_async_copy(src, dst, sems.at[n]) for n, (src, dst) in enumerate(pairs)]
    for copy in copies:
        copy.start()
    width = stiff.shape[2]
    half = width // 2
    row = iota((ROWS, width), 0)
    even_row = lax.rem(row, 2) == 0

    for copy in copies[:3]:
        copy.wait()
    on = [mask[plane(n)].astype(F32) for n in range(PLANES)]
    for c in range(FIELDS):
        group[c] = group_drive(comp[...], drive, c)
    for c in range(FIELDS):
        for z in range(PLANES):
            force[c, z] = group[c] * (TIME_SQUARE * on[z])
    for copy in copies[3 : 3 + PLANES]:
        copy.wait()
    fine_coefs(stiff, top_half, coef)
    for copy in copies[3 + PLANES : 3 + 2 * PLANES]:
        copy.wait()

    def pooled(first, second):
        first = first + roll(first, -1, 0)
        second = second + roll(second, -1, 0)
        return jnp.where(even_row, first, roll(second, 1, 0))

    tiles = []
    for c in range(FIELDS):
        tiles.append(pooled(now[c, 0] + now[c, 1], now[c, 2] + now[c, 3]))
        for z in range(PLANES):
            w_out[c, z] = fine_free(lambda n: now[c, n], 0.0, z, coef, force[c, z])
    for copy in copies[3 + 2 * PLANES :]:
        copy.wait()
    for c in range(FIELDS):
        tiles.append(pooled(before[c, 0] + before[c, 1], before[c, 2] + before[c, 3]))
    tiles.append(pooled(stiff[0] + stiff[1], stiff[2] + stiff[3]))
    for c in range(FIELDS):
        tiles.append(pooled(group[c], group[c]))
    stacked = jnp.concatenate(tiles, axis=0)
    parts = []
    rest = stacked
    for _ in range(3):
        parts.append(rest.astype(jnp.bfloat16))
        rest = rest - parts[-1].astype(F32)
    stacked = jnp.concatenate(parts, axis=0)
    pool = jnp.where(iota((256, 128), 0) // 2 == iota((256, 128), 1), 0.125, 0.0).astype(jnp.bfloat16)
    count = 10 * ROWS
    for q in range(width // 256):
        sums = lax.dot_general(
            stacked[:, q * 256 : (q + 1) * 256], pool, (((1,), (0,)), ((), ())),
            preferred_element_type=F32,
        )
        wide[q] = sums[:count] + (sums[count : 2 * count] + sums[2 * count :])

    def coarse_tile(f):
        planes = [
            jnp.concatenate([wide[q, pl.ds(8 * f + zc, 4, stride=2), :] for q in range(half // 128)], axis=1)
            for zc in range(2)
        ]
        return jnp.concatenate(planes, axis=0)

    upper = iota((ROWS, half), 0) < 4
    weight = jnp.where(upper, on[0] + on[1], on[2] + on[3]) * TIME_SQUARE
    ck_out[...] = coarse_tile(6)
    coefs = coarse_coefs(ck_out[...], top_half)
    for c in range(FIELDS):
        cu_out[c] = coarse_tile(c)
        cf_out[c] = coarse_tile(7 + c) * weight
        cw_out[c] = coarse_free(cu_out[c], coarse_tile(3 + c), coefs, cf_out[c])

    for c in range(FIELDS):
        for z in range(PLANES):
            w_out[c, z] = w_out[c, z] - before[c, z]
    pack(
        top_half,
        lambda f, z: now[f, z] if f < 3 else w_out[f - 3, z],
        lambda f: cu_out[f] if f < 3 else cw_out[f - 3],
        lambda z: stiff[z], ck_out[...],
        a_buf, b_buf, y_buf, db_buf, width,
    )


class Got:
    def __init__(self, with_k, width, y=None, a=None, ya=None, b=None, db=None):
        self.y, self.a, self.ya, self.b, self.db = y, a, ya, b, db
        self.width = width
        self.fields = 7 if with_k else 6
        self.base = 3 * width + (width // 2 if with_k else 0)

    def plane(self, buf, f):
        return buf[:, f * self.width : (f + 1) * self.width]

    def rows(self, f, z):
        return spread(take(self.y, fine_row(f * PLANES + z, self.width)))

    def corner(self, buf, f):
        return spread(take(buf, corner_fine(min(f, 3), self.width)))

    def coarse_rows(self, f, upper):
        lines = [take(self.y, coarse_row(2 * f + zc, self.width, self.base)) for zc in range(2)]
        return jnp.where(upper, spread(lines[0]), spread(lines[1]))

    def coarse_corner(self, f, upper):
        pieces = corner_coarse(min(f, 3), self.width)
        return jnp.where(upper, spread(take(self.db, pieces)), spread(take(self.ya, pieces)))

    def coarse_planes(self, c, upper):
        half = self.width // 2
        at = self.fields * self.width + c * half
        low, high = self.b[:, at : at + half], self.a[:, at : at + half]
        return (
            jnp.where(upper, low, roll(high, 4, 0)),
            jnp.where(upper, roll(low, 4, 0), high),
        )

    def coarse_stiff_planes(self, upper):
        quarter = self.width // 4
        at = self.fields * self.width + 2 * quarter * FIELDS
        low, high = self.b[:, at : at + quarter], self.a[:, at : at + quarter]
        return jnp.where(
            upper,
            jnp.concatenate([low, roll(low, 4, 0)], axis=1),
            jnp.concatenate([roll(high, 4, 0), high], axis=1),
        )


LAST = PLANES - 1


def near_faces(got, stiff, halo, top_half):
    edge = iota(stiff.shape[1:], 0) == jnp.where(top_half, ROWS - 1, 0)
    for z in range(PLANES):
        halo[z] = jnp.where(edge, FINE_FACE * (stiff[z] + got.rows(6, z)), 0.0)
    k, kd = got.plane(got.a, 6), got.corner(got.ya, 6)
    halo[4] = FINE_FACE * (stiff[LAST] + k)
    halo[5] = jnp.where(edge, FINE_FACE * (k + kd), 0.0)
    halo[6] = FINE_FACE * (got.rows(6, LAST) + kd)


def far_faces(got, stiff, halo, top_half):
    edge = iota(stiff.shape[1:], 0) == jnp.where(top_half, ROWS - 1, 0)
    k, kd = got.plane(got.b, 6), got.corner(got.db, 6)
    halo[0] = FINE_FACE * (stiff[0] + k)
    halo[1] = jnp.where(edge, FINE_FACE * (k + kd), 0.0)
    halo[2] = FINE_FACE * (got.rows(6, 0) + kd)


def coarse_faces(got, ck, halo, top_half, has_far):
    row = iota(ck.shape, 0)
    upper = row < 4
    edge = lax.rem(row, 4) == jnp.where(top_half, 3, 0)
    k = ck[...]
    kz, ky, kd = got.coarse_stiff_planes(upper), got.coarse_rows(6, upper), got.coarse_corner(6, upper)
    halo[0] = COARSE_FACE * (k + kz)
    halo[1] = jnp.where(edge, COARSE_FACE * (k + ky), 0.0)
    halo[2] = jnp.where(edge, COARSE_FACE * (kz + kd), 0.0)
    halo[3] = COARSE_FACE * (ky + kd)
    halo[4] = jnp.where(upper, jnp.where(has_far, 1.0, 0.0), 1.0)


def early(got, coef, halo, force, now, free, mid, mid_y, mid_a, part):
    for c in range(FIELDS):
        for z in range(PLANES):
            u = now[c, z]
            u_y = got.rows(c, z)
            flux = halo[z] * (u_y - u)
            new = free[c, z] + flux
            new_y = got.rows(3 + c, z) - flux
            if z == LAST:
                other, corner = got.plane(got.a, c), got.corner(got.ya, c)
                flux = halo[4] * (other - u)
                new = new + flux
                mid_a[c] = got.plane(got.a, 3 + c) - flux + halo[5] * (corner - other)
                new_y = new_y + halo[6] * (corner - u_y)
            mid[c, z] = new
            mid_y[c, z] = new_y
        for z in (2, 3):
            u = mid[c, z]
            new = fine_free(lambda n: mid[c, n], now[c, z], z, coef, force[c, z])
            new = new + halo[z] * (mid_y[c, z] - u)
            if z == LAST:
                new = new + halo[4] * (mid_a[c] - u)
            part[c, z - 2] = new


def late(got, coef, near, far, force, now, mid, mid_y, first, emit, has_far):
    for c in range(FIELDS):
        u = now[c, 0]
        other, corner = got.plane(got.b, c), got.corner(got.db, c)
        flux = far[0] * (other - u)
        first[c] = mid[c, 0] + flux
        beyond = got.plane(got.b, 3 + c) - flux + far[1] * (corner - other)
        beyond = jnp.where(has_far, beyond, 0.0)
        new_y = mid_y[c, 0] + far[2] * (corner - got.rows(c, 0))

        def field(n):
            return first[c] if n == 0 else mid[c, n]

        u = first[c]
        new = fine_free(field, now[c, 0], 0, coef, force[c, 0])
        emit(c, 0, new + near[0] * (new_y - u) + far[0] * (beyond - u))
        new = fine_free(field, now[c, 1], 1, coef, force[c, 1])
        emit(c, 1, new + near[1] * (mid_y[c, 1] - mid[c, 1]))


def coarse_steps(got, halo, cu_now, cu_free, ck, cf, top_half, emit):
    upper = iota(cf.shape[1:], 0) < 4
    face_z, face_y, face_zd, face_yd, inside = [halo[n] for n in range(5)]
    coefs = coarse_coefs(ck[...], top_half)
    for c in range(FIELDS):
        u = cu_now[c]
        u_z, w_z = got.coarse_planes(c, upper)
        u_y = got.coarse_rows(c, upper)
        u_d = got.coarse_corner(c, upper)
        flux_z = face_z * (u_z - u)
        flux_y = face_y * (u_y - u)
        new = cu_free[c] + flux_z + flux_y
        new_z = inside * (w_z - flux_z + face_zd * (u_d - u_z))
        new_y = got.coarse_rows(3 + c, upper) - flux_y + face_yd * (u_d - u_y)
        after = coarse_free(new, u, coefs, cf[c])
        emit(c, new, after + face_z * (new_z - new) + face_y * (new_y - new), coefs)


def early_two_kernel(
    y, a, ya, coef, force, stiff, now, free,
    halo, mid, mid_y, part, w_part,
    mid_a,
):
    got = Got(True, stiff.shape[2], y=y, a=a, ya=ya)
    near_faces(got, stiff, halo, place()[0])
    early(got, coef, halo, force, now, free, mid, mid_y, mid_a, part)
    for c in range(FIELDS):
        w_part[c] = fine_free(lambda n: part[c, n - 2], mid[c, LAST], LAST, coef, force[c, LAST])


def late_two_kernel(
    y, b, db, a, ya, coef, force, stiff, now, near, mid, mid_y, part, w_part, cu_now, cu_free, ck, cf,
    y_buf, b_buf, db_buf, a_buf, far, coarse_halo, u_out, w_out, cu_out, cw_out,
    first,
):
    top_half, has_far, _ = place()
    got = Got(True, stiff.shape[2], y=y, a=a, ya=ya, b=b, db=db)
    far_faces(got, stiff, far, top_half)
    coarse_faces(got, ck, coarse_halo, top_half, has_far)

    def emit(c, z, value):
        u_out[c, z] = value

    def emit_coarse(c, before, value, coefs):
        cu_out[c] = value
        cw_out[c] = coarse_free(value, before, coefs, cf[c])

    late(got, coef, near, far, force, now, mid, mid_y, first, emit, has_far)
    coarse_steps(got, coarse_halo, cu_now, cu_free, ck, cf, top_half, emit_coarse)
    for c in range(FIELDS):
        for z in (2, 3):
            u_out[c, z] = part[c, z - 2]
        w_out[c, LAST] = w_part[c]
        for z in range(LAST):
            before = first[c] if z == 0 else mid[c, z]
            w_out[c, z] = fine_free(lambda n: u_out[c, n], before, z, coef, force[c, z])
    pack(
        top_half,
        lambda f, z: u_out[f, z] if f < 3 else w_out[f - 3, z],
        lambda f: cu_out[f] if f < 3 else cw_out[f - 3],
        None, None, a_buf, b_buf, y_buf, db_buf, stiff.shape[2],
    )


def early_last_kernel(
    y, a, ya, coef, force, halo, now, free,
    mid, mid_y, part,
    mid_a,
):
    got = Got(False, coef.shape[3], y=y, a=a, ya=ya)
    early(got, coef, halo, force, now, free, mid, mid_y, mid_a, part)


def late_last_kernel(
    y, b, db, a, ya, coef, force, now, near, far, mid, mid_y, part, cu_now, cu_free, ck, cf, coarse_halo,
    u_hbm, cu_hbm,
    first, last, coarse_last, sems,
):
    top_half, has_far, plane = place()
    got = Got(False, coef.shape[3], y=y, a=a, ya=ya, b=b, db=db)
    copies = []

    def send(src, dst):
        copies.append(pltpu.make_async_copy(src, dst, sems.at[len(copies)]))
        copies[-1].start()

    for z in (2, 3):
        send(part.at[:, z - 2], u_hbm.at[:, plane(z)])

    def emit(c, z, value):
        last[c, z] = value
        send(last.at[c, z], u_hbm.at[c, plane(z)])

    def emit_coarse(c, before, value, coefs):
        for zc in range(2):
            coarse_last[c, zc] = value[4 * zc : 4 * zc + 4]

    coarse_steps(got, coarse_halo, cu_now, cu_free, ck, cf, top_half, emit_coarse)
    for zc in range(2):
        send(coarse_last.at[:, zc], cu_hbm.at[:, plane(zc, 2)])
    late(got, coef, near, far, force, now, mid, mid_y, first, emit, has_far)
    for copy in copies:
        copy.wait()


def struct(*shape):
    return jax.ShapeDtypeStruct(shape, F32)


def call(kernel, name, outs, scratch, operands, in_space=pltpu.VMEM, out_space=pltpu.VMEM, flops=None):
    estimate = None
    if flops is not None:
        estimate = pl.CostEstimate(flops=flops, bytes_accessed=1024, transcendentals=0)
    return pl.pallas_call(
        kernel,
        name=name,
        out_shape=outs,
        in_specs=[pl.BlockSpec(memory_space=in_space)] * len(operands),
        out_specs=[pl.BlockSpec(memory_space=out_space)] * len(outs),
        scratch_shapes=scratch,
        cost_estimate=estimate,
        compiler_params=pltpu.CompilerParams(vmem_limit_bytes=32 * 1024 * 1024),
    )(*operands)


def corner_kernel(width, with_k, y_ref, out_ref):
    base = 3 * width + (width // 2 if with_k else 0)
    for g in range(4 if with_k else 3):
        f = 6 if g == 3 else g
        put(out_ref, corner_fine(g, width), take(y_ref, fine_row(f * PLANES + LAST, width)))
        put(out_ref, corner_coarse(g, width), take(y_ref, coarse_row(2 * f + 1, width, base)))
    if not with_k:
        out_ref[6:8, :] = jnp.zeros((2, out_ref.shape[1]), F32)


def exchange(bufs, width, with_k):
    count = lax.axis_size("ax")
    pair_a = [(i, i ^ 1) for i in range(count)]
    pair_b = [(i, i + 1 if i % 2 else i - 1) for i in range(1, count - 1)]
    across = [(2 * i + s, 2 * j + 1 - s) for i, j in pair_b for s in (0, 1)]
    y, b, db, a = bufs
    y = lax.ppermute(y, "xs", [(0, 1), (1, 0)])
    b = lax.ppermute(b, "ax", pair_b)
    db = lax.ppermute(db, ("ax", "xs"), across)
    a = lax.ppermute(a, "ax", pair_a)
    kernel = functools.partial(corner_kernel, width, with_k)
    (line,) = call(kernel, "corner_lines", [struct(ROWS, width // 2 + width // 4)], [], (y,), flops=CORNER_FLOPS)
    ya = lax.ppermute(line, "ax", pair_a)
    return y, b, db, a, ya


CORNER_FLOPS = 2_000_000_000
EARLY_FLOPS = 1


def local(displacement, previous, stiffness, tissue_mask, compartment, drive):
    width = displacement.shape[3]
    half = width // 2
    quarter = width // 4
    field = struct(FIELDS, PLANES, ROWS, width)
    coarse = struct(FIELDS, ROWS, half)
    part = struct(FIELDS, 2, ROWS, width)
    tile = struct(FIELDS, ROWS, width)

    def buffers(fields, with_k):
        plane = fields * width + 3 * half + (quarter if with_k else 0)
        rows = 3 * width + (3 * half if with_k else 2 * half)
        return [struct(ROWS, rows), struct(ROWS, plane + PAD_B), struct(ROWS, half + quarter + PAD), struct(ROWS, plane)]

    scratch_tile = pltpu.VMEM(tile.shape, F32)
    y, b, db, a, now, stiff, coef, force, w, cu, cw, ck, cf = call(
        begin_kernel,
        "restrict_and_first_step",
        buffers(7, True)
        + [field, struct(*stiffness.shape), struct(6, PLANES, ROWS, width), field, field]
        + [coarse, coarse, struct(ROWS, half), coarse],
        [
            pltpu.SMEM(tissue_mask.shape, jnp.int32),
            pltpu.SMEM(drive.shape, F32),
            pltpu.VMEM(compartment.shape, jnp.int32),
            pltpu.VMEM(field.shape, F32),
            scratch_tile,
            pltpu.VMEM((half // 128, 10 * ROWS, 128), F32),
            pltpu.SemaphoreType.DMA((3 + 3 * PLANES,)),
        ],
        [
            pltpu.with_memory_space_constraint(x, pltpu.HBM)
            for x in (tissue_mask, drive, compartment, stiffness, displacement, previous)
        ],
        in_space=pltpu.HBM,
    )
    y, b, db, a, ya = exchange((y, b, db, a), width, True)
    near, mid, mid_y, done, w_done = call(
        early_two_kernel,
        "early_two_steps",
        [struct(7, ROWS, width), field, field, part, tile],
        [scratch_tile],
        (y, a, ya, coef, force, stiff, now, w),
        flops=EARLY_FLOPS,
    )
    y, b, db, a, far, coarse_halo, u, w, cu, cw = call(
        late_two_kernel,
        "late_two_steps",
        buffers(6, False) + [struct(3, ROWS, width), struct(5, ROWS, half), field, field, coarse, coarse],
        [scratch_tile],
        (y, b, db, a, ya, coef, force, stiff, now, near, mid, mid_y, done, w_done, cu, cw, ck, cf),
    )
    y, b, db, a, ya = exchange((y, b, db, a), width, False)
    mid, mid_y, done = call(
        early_last_kernel,
        "early_last_steps",
        [field, field, part],
        [scratch_tile],
        (y, a, ya, coef, force, near, u, w),
        flops=EARLY_FLOPS,
    )
    return call(
        late_last_kernel,
        "late_last_steps",
        [field, struct(FIELDS, 2, 4, half)],
        [
            scratch_tile,
            pltpu.VMEM(part.shape, F32),
            pltpu.VMEM((FIELDS, 2, 4, half), F32),
            pltpu.SemaphoreType.DMA((10,)),
        ],
        (y, b, db, a, ya, coef, force, u, near, far, mid, mid_y, done, cu, cw, ck, cf, coarse_halo),
        out_space=pltpu.HBM,
    )


def solution(mesh):
    placed = (
        P(None, "ax", "xs", None),
        P(None, "ax", "xs", None),
        P("ax", "xs", None),
        P("ax"),
        P("xs", None),
        P(),
    )

    def run(*args):
        return tuple(local(*args))

    return jax.shard_map(
        run,
        mesh=mesh,
        in_specs=placed,
        out_specs=(P(None, "ax", "xs", None), P(None, "ax", "xs", None)),
        check_vma=False,
    )
```

```python
import functools

import jax
import jax.numpy as jnp
from jax import lax
from jax.experimental import pallas as pl
from jax.experimental.pallas import tpu as pltpu
from jax.sharding import PartitionSpec as P

TIME_SQUARE = 0.12
FINE_FACE = 0.5 * TIME_SQUARE
COARSE_FACE = 0.25 * 0.5 * TIME_SQUARE
PLANES = 4
ROWS = 8
FIELDS = 3
F32 = jnp.float32
PAD = 128
PAD_B = 128


def roll(x, shift, axis):
    return pltpu.roll(x, shift % x.shape[axis], axis)


def place():
    i = lax.axis_index("ax")
    odd = lax.rem(i, 2) == 1
    has_far = jnp.logical_and(i > 0, i < lax.axis_size("ax") - 1)

    def plane(n, count=PLANES):
        return jnp.where(odd, count - 1 - n, n)

    return lax.axis_index("xs") == 0, has_far, plane


def iota(shape, dim):
    return lax.broadcasted_iota(jnp.int32, shape, dim)


def stiff_coefs(k, face, low_y, high_y, outer_row):
    width = k.shape[1]
    lane = iota(k.shape, 1)
    last = lane == width - 1
    start = lane == 0
    kp = jnp.where(last, 0.0, roll(k, -1, 1))
    km = jnp.where(start, 0.0, roll(k, 1, 1))
    full_p = face * (k + kp)
    full_m = face * (k + km)
    cyp = jnp.where(high_y, face * (k + roll(k, -1, 0)), 0.0)
    cym = jnp.where(low_y, face * (k + roll(k, 1, 0)), 0.0)
    edge = jnp.where(outer_row, face * k, 0.0)
    centre = 2.0 - (full_p + full_m + cyp + cym + edge)
    return jnp.where(last, 0.0, full_p), jnp.where(start, 0.0, full_m), cyp, cym, centre


def fine_coefs(k_ref, first, coef):
    shape = k_ref.shape[1:]
    row = iota(shape, 0)
    for z in range(PLANES - 1):
        coef[5, z] = FINE_FACE * (k_ref[z] + k_ref[z + 1])
    for z in range(PLANES):
        cxp, cxm, cyp, cym, centre = stiff_coefs(
            k_ref[z], FINE_FACE, row > 0, row < ROWS - 1, row == jnp.where(first, 0, ROWS - 1)
        )
        if z > 0:
            centre = centre - coef[5, z - 1]
        if z < PLANES - 1:
            centre = centre - coef[5, z]
        coef[0, z] = cxp
        coef[1, z] = cxm
        coef[2, z] = cyp
        coef[3, z] = cym
        coef[4, z] = centre


def fine_free(field, before, z, coef, drive_term):
    u = field(z)
    acc = coef[4, z] * u - before
    acc = acc + coef[0, z] * roll(u, -1, 1) + coef[1, z] * roll(u, 1, 1)
    acc = acc + coef[2, z] * roll(u, -1, 0) + coef[3, z] * roll(u, 1, 0)
    if z > 0:
        acc = acc + coef[5, z - 1] * field(z - 1)
    if z < PLANES - 1:
        acc = acc + coef[5, z] * field(z + 1)
    return acc + drive_term


def coarse_coefs(k, first):
    row = iota(k.shape, 0)
    inner = lax.rem(row, 4)
    cxp, cxm, cyp, cym, centre = stiff_coefs(
        k, COARSE_FACE, inner > 0, inner < 3, inner == jnp.where(first, 0, 3)
    )
    cz = COARSE_FACE * (k + roll(k, 4, 0))
    return cxp, cxm, cyp, cym, centre - cz, cz


def coarse_free(u, before, coefs, force):
    cxp, cxm, cyp, cym, centre, cz = coefs
    return (
        centre * u
        - before
        + cxp * roll(u, -1, 1)
        + cxm * roll(u, 1, 1)
        + cyp * roll(u, -1, 0)
        + cym * roll(u, 1, 0)
        + cz * roll(u, 4, 0)
        + force
    )


def group_drive(compartment, drive_ref, c):
    value = jnp.full(compartment.shape, drive_ref[c, 0], F32)
    for g in range(1, drive_ref.shape[1]):
        value = jnp.where(compartment == g, drive_ref[c, g], value)
    return value


def fine_row(r, width):
    if r < 24:
        return [(r % 8, (r // 8) * width, width)]
    half = width // 2
    return [(2 * (r - 24) + h, 3 * width, half) for h in range(2)]


def coarse_row(q, width, base):
    half = width // 2
    if q >= 8 and base == 3 * width:
        return [(2 * (q - 8) + h, base + half, half // 2) for h in range(2)]
    return [(q % 8, base + (q // 8) * half, half)]


def corner_fine(f, width):
    half = width // 2
    return [(2 * f + h, 0, half) for h in range(2)]


def corner_coarse(f, width):
    quarter = width // 4
    return [(2 * f + h, width // 2, quarter) for h in range(2)]


def put(buf, pieces, line):
    at = 0
    for row, lane, lanes in pieces:
        buf[row : row + 1, lane : lane + lanes] = line[:, at : at + lanes]
        at += lanes


def take(buf, pieces):
    parts = [buf[row : row + 1, lane : lane + lanes] for row, lane, lanes in pieces]
    return parts[0] if len(parts) == 1 else jnp.concatenate(parts, axis=1)


def spread(line, rows=ROWS):
    return jnp.broadcast_to(line, (rows, line.shape[1]))


def edge_line(tile, top_half, base=0, rows=ROWS):
    return jnp.where(top_half, tile[base + rows - 1 : base + rows], tile[base : base + 1])


def pack(top_half, fine, coarse, stiff, coarse_stiff, a_buf, b_buf, y_buf, db_buf, width):
    half = width // 2
    quarter = width // 4
    with_k = stiff is not None
    fields = 7 if with_k else 6
    upper = iota((ROWS, half), 0) < 4
    base = 3 * width + (half if with_k else 0)
    for f in range(fields):
        for z in range(PLANES):
            t = fine(f, z) if f < 6 else stiff(z)
            line = edge_line(t, top_half)
            put(y_buf, fine_row(f * PLANES + z, width), line)
            if z == 0:
                b_buf[:, f * width : (f + 1) * width] = t
                if f < 3 or f == 6:
                    put(db_buf, corner_fine(min(f, 3), width), line)
            if z == PLANES - 1:
                a_buf[:, f * width : (f + 1) * width] = t

    for f in range(fields):
        t = coarse(f) if f < 6 else coarse_stiff
        for zc in range(2):
            line = edge_line(t, top_half, 4 * zc, 4)
            put(y_buf, coarse_row(2 * f + zc, width, base), line)
            if zc == 0 and (f < 3 or f == 6):
                put(db_buf, corner_coarse(min(f, 3), width), line)
    b_buf[:, a_buf.shape[1] :] = jnp.zeros((ROWS, b_buf.shape[1] - a_buf.shape[1]), F32)
    db_buf[:, half + quarter :] = jnp.zeros((ROWS, db_buf.shape[1] - half - quarter), F32)
    if with_k:
        y_buf[6:8, base + half : base + 2 * half] = jnp.zeros((2, half), F32)
    else:
        db_buf[6:8, :] = jnp.zeros((2, db_buf.shape[1]), F32)

    at = fields * width
    for c in range(FIELDS):
        first, second = coarse(c), coarse(c + 3)
        b_buf[:, at : at + half] = jnp.where(upper, first, roll(second, 4, 0))
        a_buf[:, at : at + half] = jnp.where(upper, roll(first, 4, 0), second)
        at += half
    if with_k:
        some = iota((ROWS, quarter), 0) < 4
        for buf, k in ((b_buf, coarse_stiff), (a_buf, roll(coarse_stiff, 4, 0))):
            buf[:, at : at + quarter] = jnp.where(some, k[:, :quarter], roll(k[:, quarter:], 4, 0))


def begin_kernel(
    mask_hbm, drive_hbm, comp_hbm, stiff_hbm, now_hbm, before_hbm,
    y_buf, b_buf, db_buf, a_buf, now, stiff, coef, force, w_out, cu_out, cw_out, ck_out, cf_out,
    mask, drive, comp, before, group, wide, sems,
):
    top_half, _, plane = place()
    pairs = [(drive_hbm, drive), (mask_hbm, mask), (comp_hbm, comp)]
    pairs += [(stiff_hbm.at[plane(n)], stiff.at[n]) for n in range(PLANES)]
    pairs += [(now_hbm.at[:, plane(n)], now.at[:, n]) for n in range(PLANES)]
    pairs += [(before_hbm.at[:, plane(n)], before.at[:, n]) for n in range(PLANES)]
    copies = [pltpu.make_async_copy(src, dst, sems.at[n]) for n, (src, dst) in enumerate(pairs)]
    for copy in copies:
        copy.start()
    width = stiff.shape[2]
    half = width // 2
    row = iota((ROWS, width), 0)
    even_row = lax.rem(row, 2) == 0

    for copy in copies[:3]:
        copy.wait()
    on = [mask[plane(n)].astype(F32) for n in range(PLANES)]
    for c in range(FIELDS):
        group[c] = group_drive(comp[...], drive, c)
    for c in range(FIELDS):
        for z in range(PLANES):
            force[c, z] = group[c] * (TIME_SQUARE * on[z])
    for copy in copies[3 : 3 + PLANES]:
        copy.wait()
    fine_coefs(stiff, top_half, coef)
    for copy in copies[3 + PLANES : 3 + 2 * PLANES]:
        copy.wait()

    def pooled(first, second):
        first = first + roll(first, -1, 0)
        second = second + roll(second, -1, 0)
        return jnp.where(even_row, first, roll(second, 1, 0))

    tiles = []
    for c in range(FIELDS):
        tiles.append(pooled(now[c, 0] + now[c, 1], now[c, 2] + now[c, 3]))
        for z in range(PLANES):
            w_out[c, z] = fine_free(lambda n: now[c, n], 0.0, z, coef, force[c, z])
    for copy in copies[3 + 2 * PLANES :]:
        copy.wait()
    for c in range(FIELDS):
        tiles.append(pooled(before[c, 0] + before[c, 1], before[c, 2] + before[c, 3]))
    tiles.append(pooled(stiff[0] + stiff[1], stiff[2] + stiff[3]))
    for c in range(FIELDS):
        tiles.append(pooled(group[c], group[c]))
    stacked = jnp.concatenate(tiles, axis=0)
    parts = []
    rest = stacked
    for _ in range(3):
        parts.append(rest.astype(jnp.bfloat16))
        rest = rest - parts[-1].astype(F32)
    stacked = jnp.concatenate(parts, axis=0)
    pool = jnp.where(iota((256, 128), 0) // 2 == iota((256, 128), 1), 0.125, 0.0).astype(jnp.bfloat16)
    count = 10 * ROWS
    for q in range(width // 256):
        sums = lax.dot_general(
            stacked[:, q * 256 : (q + 1) * 256], pool, (((1,), (0,)), ((), ())),
            preferred_element_type=F32,
        )
        wide[q] = sums[:count] + (sums[count : 2 * count] + sums[2 * count :])

    def coarse_tile(f):
        planes = [
            jnp.concatenate([wide[q, pl.ds(8 * f + zc, 4, stride=2), :] for q in range(half // 128)], axis=1)
            for zc in range(2)
        ]
        return jnp.concatenate(planes, axis=0)

    upper = iota((ROWS, half), 0) < 4
    weight = jnp.where(upper, on[0] + on[1], on[2] + on[3]) * TIME_SQUARE
    ck_out[...] = coarse_tile(6)
    coefs = coarse_coefs(ck_out[...], top_half)
    for c in range(FIELDS):
        cu_out[c] = coarse_tile(c)
        cf_out[c] = coarse_tile(7 + c) * weight
        cw_out[c] = coarse_free(cu_out[c], coarse_tile(3 + c), coefs, cf_out[c])

    for c in range(FIELDS):
        for z in range(PLANES):
            w_out[c, z] = w_out[c, z] - before[c, z]
    pack(
        top_half,
        lambda f, z: now[f, z] if f < 3 else w_out[f - 3, z],
        lambda f: cu_out[f] if f < 3 else cw_out[f - 3],
        lambda z: stiff[z], ck_out[...],
        a_buf, b_buf, y_buf, db_buf, width,
    )


class Got:
    def __init__(self, with_k, width, y=None, a=None, ya=None, b=None, db=None):
        self.y, self.a, self.ya, self.b, self.db = y, a, ya, b, db
        self.width = width
        self.fields = 7 if with_k else 6
        self.base = 3 * width + (width // 2 if with_k else 0)

    def plane(self, buf, f):
        return buf[:, f * self.width : (f + 1) * self.width]

    def rows(self, f, z):
        return spread(take(self.y, fine_row(f * PLANES + z, self.width)))

    def corner(self, buf, f):
        return spread(take(buf, corner_fine(min(f, 3), self.width)))

    def coarse_rows(self, f, upper):
        lines = [take(self.y, coarse_row(2 * f + zc, self.width, self.base)) for zc in range(2)]
        return jnp.where(upper, spread(lines[0]), spread(lines[1]))

    def coarse_corner(self, f, upper):
        pieces = corner_coarse(min(f, 3), self.width)
        return jnp.where(upper, spread(take(self.db, pieces)), spread(take(self.ya, pieces)))

    def coarse_planes(self, c, upper):
        half = self.width // 2
        at = self.fields * self.width + c * half
        low, high = self.b[:, at : at + half], self.a[:, at : at + half]
        return (
            jnp.where(upper, low, roll(high, 4, 0)),
            jnp.where(upper, roll(low, 4, 0), high),
        )

    def coarse_stiff_planes(self, upper):
        quarter = self.width // 4
        at = self.fields * self.width + 2 * quarter * FIELDS
        low, high = self.b[:, at : at + quarter], self.a[:, at : at + quarter]
        return jnp.where(
            upper,
            jnp.concatenate([low, roll(low, 4, 0)], axis=1),
            jnp.concatenate([roll(high, 4, 0), high], axis=1),
        )


LAST = PLANES - 1


def near_faces(got, stiff, halo, top_half):
    edge = iota(stiff.shape[1:], 0) == jnp.where(top_half, ROWS - 1, 0)
    for z in range(PLANES):
        halo[z] = jnp.where(edge, FINE_FACE * (stiff[z] + got.rows(6, z)), 0.0)
    k, kd = got.plane(got.a, 6), got.corner(got.ya, 6)
    halo[4] = FINE_FACE * (stiff[LAST] + k)
    halo[5] = jnp.where(edge, FINE_FACE * (k + kd), 0.0)
    halo[6] = FINE_FACE * (got.rows(6, LAST) + kd)


def far_faces(got, stiff, halo, top_half):
    edge = iota(stiff.shape[1:], 0) == jnp.where(top_half, ROWS - 1, 0)
    k, kd = got.plane(got.b, 6), got.corner(got.db, 6)
    halo[0] = FINE_FACE * (stiff[0] + k)
    halo[1] = jnp.where(edge, FINE_FACE * (k + kd), 0.0)
    halo[2] = FINE_FACE * (got.rows(6, 0) + kd)


def coarse_faces(got, ck, halo, top_half, has_far):
    row = iota(ck.shape, 0)
    upper = row < 4
    edge = lax.rem(row, 4) == jnp.where(top_half, 3, 0)
    k = ck[...]
    kz, ky, kd = got.coarse_stiff_planes(upper), got.coarse_rows(6, upper), got.coarse_corner(6, upper)
    halo[0] = COARSE_FACE * (k + kz)
    halo[1] = jnp.where(edge, COARSE_FACE * (k + ky), 0.0)
    halo[2] = jnp.where(edge, COARSE_FACE * (kz + kd), 0.0)
    halo[3] = COARSE_FACE * (ky + kd)
    halo[4] = jnp.where(upper, jnp.where(has_far, 1.0, 0.0), 1.0)


def early(got, coef, halo, force, now, free, mid, mid_y, mid_a, part):
    for c in range(FIELDS):
        for z in range(PLANES):
            u = now[c, z]
            u_y = got.rows(c, z)
            flux = halo[z] * (u_y - u)
            new = free[c, z] + flux
            new_y = got.rows(3 + c, z) - flux
            if z == LAST:
                other, corner = got.plane(got.a, c), got.corner(got.ya, c)
                flux = halo[4] * (other - u)
                new = new + flux
                mid_a[c] = got.plane(got.a, 3 + c) - flux + halo[5] * (corner - other)
                new_y = new_y + halo[6] * (corner - u_y)
            mid[c, z] = new
            mid_y[c, z] = new_y
        for z in (2, 3):
            u = mid[c, z]
            new = fine_free(lambda n: mid[c, n], now[c, z], z, coef, force[c, z])
            new = new + halo[z] * (mid_y[c, z] - u)
            if z == LAST:
                new = new + halo[4] * (mid_a[c] - u)
            part[c, z - 2] = new


def late(got, coef, near, far, force, now, mid, mid_y, first, emit, has_far):
    for c in range(FIELDS):
        u = now[c, 0]
        other, corner = got.plane(got.b, c), got.corner(got.db, c)
        flux = far[0] * (other - u)
        first[c] = mid[c, 0] + flux
        beyond = got.plane(got.b, 3 + c) - flux + far[1] * (corner - other)
        beyond = jnp.where(has_far, beyond, 0.0)
        new_y = mid_y[c, 0] + far[2] * (corner - got.rows(c, 0))

        def field(n):
            return first[c] if n == 0 else mid[c, n]

        u = first[c]
        new = fine_free(field, now[c, 0], 0, coef, force[c, 0])
        emit(c, 0, new + near[0] * (new_y - u) + far[0] * (beyond - u))
        new = fine_free(field, now[c, 1], 1, coef, force[c, 1])
        emit(c, 1, new + near[1] * (mid_y[c, 1] - mid[c, 1]))


def coarse_steps(got, halo, cu_now, cu_free, ck, cf, top_half, emit):
    upper = iota(cf.shape[1:], 0) < 4
    face_z, face_y, face_zd, face_yd, inside = [halo[n] for n in range(5)]
    coefs = coarse_coefs(ck[...], top_half)
    for c in range(FIELDS):
        u = cu_now[c]
        u_z, w_z = got.coarse_planes(c, upper)
        u_y = got.coarse_rows(c, upper)
        u_d = got.coarse_corner(c, upper)
        flux_z = face_z * (u_z - u)
        flux_y = face_y * (u_y - u)
        new = cu_free[c] + flux_z + flux_y
        new_z = inside * (w_z - flux_z + face_zd * (u_d - u_z))
        new_y = got.coarse_rows(3 + c, upper) - flux_y + face_yd * (u_d - u_y)
        after = coarse_free(new, u, coefs, cf[c])
        emit(c, new, after + face_z * (new_z - new) + face_y * (new_y - new), coefs)


def early_two_kernel(
    y, a, ya, coef, force, stiff, now, free,
    halo, mid, mid_y, part, w_part,
    mid_a,
):
    got = Got(True, stiff.shape[2], y=y, a=a, ya=ya)
    near_faces(got, stiff, halo, place()[0])
    early(got, coef, halo, force, now, free, mid, mid_y, mid_a, part)
    for c in range(FIELDS):
        w_part[c] = fine_free(lambda n: part[c, n - 2], mid[c, LAST], LAST, coef, force[c, LAST])


def late_two_kernel(
    y, b, db, a, ya, coef, force, stiff, now, near, mid, mid_y, part, w_part, cu_now, cu_free, ck, cf,
    y_buf, b_buf, db_buf, a_buf, far, coarse_halo, u_out, w_out, cu_out, cw_out,
    first,
):
    top_half, has_far, _ = place()
    got = Got(True, stiff.shape[2], y=y, a=a, ya=ya, b=b, db=db)
    far_faces(got, stiff, far, top_half)
    coarse_faces(got, ck, coarse_halo, top_half, has_far)

    def emit(c, z, value):
        u_out[c, z] = value

    def emit_coarse(c, before, value, coefs):
        cu_out[c] = value
        cw_out[c] = coarse_free(value, before, coefs, cf[c])

    late(got, coef, near, far, force, now, mid, mid_y, first, emit, has_far)
    coarse_steps(got, coarse_halo, cu_now, cu_free, ck, cf, top_half, emit_coarse)
    for c in range(FIELDS):
        for z in (2, 3):
            u_out[c, z] = part[c, z - 2]
        w_out[c, LAST] = w_part[c]
        for z in range(LAST):
            before = first[c] if z == 0 else mid[c, z]
            w_out[c, z] = fine_free(lambda n: u_out[c, n], before, z, coef, force[c, z])
    pack(
        top_half,
        lambda f, z: u_out[f, z] if f < 3 else w_out[f - 3, z],
        lambda f: cu_out[f] if f < 3 else cw_out[f - 3],
        None, None, a_buf, b_buf, y_buf, db_buf, stiff.shape[2],
    )


def early_last_kernel(
    y, a, ya, coef, force, halo, now, free,
    mid, mid_y, part,
    mid_a,
):
    got = Got(False, coef.shape[3], y=y, a=a, ya=ya)
    early(got, coef, halo, force, now, free, mid, mid_y, mid_a, part)


def late_last_kernel(
    y, b, db, a, ya, coef, force, now, near, far, mid, mid_y, part, cu_now, cu_free, ck, cf, coarse_halo,
    u_hbm, cu_hbm,
    first, last, coarse_last, sems,
):
    top_half, has_far, plane = place()
    got = Got(False, coef.shape[3], y=y, a=a, ya=ya, b=b, db=db)
    copies = []

    def send(src, dst):
        copies.append(pltpu.make_async_copy(src, dst, sems.at[len(copies)]))
        copies[-1].start()

    for z in (2, 3):
        send(part.at[:, z - 2], u_hbm.at[:, plane(z)])

    def emit(c, z, value):
        last[c, z] = value
        send(last.at[c, z], u_hbm.at[c, plane(z)])

    def emit_coarse(c, before, value, coefs):
        for zc in range(2):
            coarse_last[c, zc] = value[4 * zc : 4 * zc + 4]

    coarse_steps(got, coarse_halo, cu_now, cu_free, ck, cf, top_half, emit_coarse)
    for zc in range(2):
        send(coarse_last.at[:, zc], cu_hbm.at[:, plane(zc, 2)])
    late(got, coef, near, far, force, now, mid, mid_y, first, emit, has_far)
    for copy in copies:
        copy.wait()


def struct(*shape):
    return jax.ShapeDtypeStruct(shape, F32)


def call(kernel, name, outs, scratch, operands, in_space=pltpu.VMEM, out_space=pltpu.VMEM, flops=None):
    estimate = None
    if flops is not None:
        estimate = pl.CostEstimate(flops=flops, bytes_accessed=1024, transcendentals=0)
    return pl.pallas_call(
        kernel,
        name=name,
        out_shape=outs,
        in_specs=[pl.BlockSpec(memory_space=in_space)] * len(operands),
        out_specs=[pl.BlockSpec(memory_space=out_space)] * len(outs),
        scratch_shapes=scratch,
        cost_estimate=estimate,
        compiler_params=pltpu.CompilerParams(vmem_limit_bytes=32 * 1024 * 1024),
    )(*operands)


def corner_kernel(width, with_k, y_ref, out_ref):
    base = 3 * width + (width // 2 if with_k else 0)
    for g in range(4 if with_k else 3):
        f = 6 if g == 3 else g
        put(out_ref, corner_fine(g, width), take(y_ref, fine_row(f * PLANES + LAST, width)))
        put(out_ref, corner_coarse(g, width), take(y_ref, coarse_row(2 * f + 1, width, base)))
    if not with_k:
        out_ref[6:8, :] = jnp.zeros((2, out_ref.shape[1]), F32)


def exchange(bufs, width, with_k):
    count = lax.axis_size("ax")
    pair_a = [(i, i ^ 1) for i in range(count)]
    pair_b = [(i, i + 1 if i % 2 else i - 1) for i in range(1, count - 1)]
    across = [(2 * i + s, 2 * j + 1 - s) for i, j in pair_b for s in (0, 1)]
    y, b, db, a = bufs
    y = lax.ppermute(y, "xs", [(0, 1), (1, 0)])
    b = lax.ppermute(b, "ax", pair_b)
    db = lax.ppermute(db, ("ax", "xs"), across)
    a = lax.ppermute(a, "ax", pair_a)
    kernel = functools.partial(corner_kernel, width, with_k)
    (line,) = call(kernel, "corner_lines", [struct(ROWS, width // 2 + width // 4)], [], (y,), flops=CORNER_FLOPS)
    ya = lax.ppermute(line, "ax", pair_a)
    return y, b, db, a, ya


CORNER_FLOPS = 2_000_000_000
EARLY_FLOPS = 1


def local(displacement, previous, stiffness, tissue_mask, compartment, drive):
    width = displacement.shape[3]
    half = width // 2
    quarter = width // 4
    field = struct(FIELDS, PLANES, ROWS, width)
    coarse = struct(FIELDS, ROWS, half)
    part = struct(FIELDS, 2, ROWS, width)
    tile = struct(FIELDS, ROWS, width)

    def buffers(fields, with_k):
        plane = fields * width + 3 * half + (quarter if with_k else 0)
        rows = 3 * width + (3 * half if with_k else half + quarter)
        return [struct(ROWS, rows), struct(ROWS, plane + PAD_B), struct(ROWS, half + quarter + PAD), struct(ROWS, plane)]

    scratch_tile = pltpu.VMEM(tile.shape, F32)
    y, b, db, a, now, stiff, coef, force, w, cu, cw, ck, cf = call(
        begin_kernel,
        "restrict_and_first_step",
        buffers(7, True)
        + [field, struct(*stiffness.shape), struct(6, PLANES, ROWS, width), field, field]
        + [coarse, coarse, struct(ROWS, half), coarse],
        [
            pltpu.SMEM(tissue_mask.shape, jnp.int32),
            pltpu.SMEM(drive.shape, F32),
            pltpu.VMEM(compartment.shape, jnp.int32),
            pltpu.VMEM(field.shape, F32),
            scratch_tile,
            pltpu.VMEM((half // 128, 10 * ROWS, 128), F32),
            pltpu.SemaphoreType.DMA((3 + 3 * PLANES,)),
        ],
        [
            pltpu.with_memory_space_constraint(x, pltpu.HBM)
            for x in (tissue_mask, drive, compartment, stiffness, displacement, previous)
        ],
        in_space=pltpu.HBM,
    )
    y, b, db, a, ya = exchange((y, b, db, a), width, True)
    near, mid, mid_y, done, w_done = call(
        early_two_kernel,
        "early_two_steps",
        [struct(7, ROWS, width), field, field, part, tile],
        [scratch_tile],
        (y, a, ya, coef, force, stiff, now, w),
        flops=EARLY_FLOPS,
    )
    y, b, db, a, far, coarse_halo, u, w, cu, cw = call(
        late_two_kernel,
        "late_two_steps",
        buffers(6, False) + [struct(3, ROWS, width), struct(5, ROWS, half), field, field, coarse, coarse],
        [scratch_tile],
        (y, b, db, a, ya, coef, force, stiff, now, near, mid, mid_y, done, w_done, cu, cw, ck, cf),
    )
    y, b, db, a, ya = exchange((y, b, db, a), width, False)
    mid, mid_y, done = call(
        early_last_kernel,
        "early_last_steps",
        [field, field, part],
        [scratch_tile],
        (y, a, ya, coef, force, near, u, w),
        flops=EARLY_FLOPS,
    )
    return call(
        late_last_kernel,
        "late_last_steps",
        [field, struct(FIELDS, 2, 4, half)],
        [
            scratch_tile,
            pltpu.VMEM(part.shape, F32),
            pltpu.VMEM((FIELDS, 2, 4, half), F32),
            pltpu.SemaphoreType.DMA((10,)),
        ],
        (y, b, db, a, ya, coef, force, u, near, far, mid, mid_y, done, cu, cw, ck, cf, coarse_halo),
        out_space=pltpu.HBM,
    )


def solution(mesh):
    placed = (
        P(None, "ax", "xs", None),
        P(None, "ax", "xs", None),
        P("ax", "xs", None),
        P("ax"),
        P("xs", None),
        P(),
    )

    def run(*args):
        return tuple(local(*args))

    return jax.shard_map(
        run,
        mesh=mesh,
        in_specs=placed,
        out_specs=(P(None, "ax", "xs", None), P(None, "ax", "xs", None)),
        check_vma=False,
    )
```
